32 devices in a mesh: batch: 1, blk: 4 (over x, core), box: 8 (over z, y).
Axes of the slice: x: 2, y: 2, z: 4, core: 2. Of those that a mesh axis runs over, the one named last changes fastest.
Arguments:
- surface_points: float32 [3, 4096], P(None, ('blk', 'box')), may hold values from -4 to 4
- angle_ids: int32 [128], P('batch'), may hold values from 0 to 16383
- near_mask: int32 [32, 8], P(('blk', 'box')), may hold values 0 or 1
- skeleton: int32 [32, 32], P(('blk', 'box')), may hold values from 0 to 127, as said below
- box_inverse_parts: float32 [32, 2, 128, 128], P(('blk', 'box')), may hold values from -0.375 to 0.375
- near_coupling: float32 [32, 8, 2, 32, 128], P(('blk', 'box')), may hold values from -0.25 to 0.25
- top_inverse: float32 [4, 2, 256, 256], P('blk', None, 'box'), may hold values from -0.25 to 0.25
Outputs:
- scattered: float32 [2, 128, 4096], P(None, ('batch', 'box'), 'blk')
The draws below stay inside these ranges and needn't reach their ends.
Inputs may be any that keep to these rules, and one draw needn't show every extreme that they name: `skeleton`: each row holds 32 distinct row numbers of a box.
All inputs are finite; a program needn't handle non-finite values. No bound on the sum of `near_mask` on one device may be relied on, other than what follows from the above.
Results may differ from the reference program's by a relative error of at most 0.0003.
Values sent between devices are 32-bit elements; how exact they have to be, the bound alone decides.
No kernel may reach another device: no remote copies, remote signals or barrier semaphores. Data moves between devices by JAX's collectives and lax.ppermute only.
A program may use at most 64 MiB of HBM per device.

```python
import jax
import jax.numpy as jnp
from jax import lax

B = 128
SKELETON_COUNT = 32
SWEEP = 16384
ANGLE_COUNT = 128
Q = 8
BOX_TOTAL = 32
NPTS = 4096
SK = 256
N_BLK = 4


def draw_skeleton(key, part):
    scores = jax.random.randint(jax.random.fold_in(key, 7), (BOX_TOTAL, B), 0, 1 << 20) * B + jnp.arange(B, dtype=jnp.int32)[None, :]
    order = jnp.argsort(scores, axis=1, stable=True)
    return order[:, :SKELETON_COUNT].astype(jnp.int32)


def set_ends(drawn, key, low, largest):
    extent = drawn.shape
    place = [jax.random.randint(jax.random.fold_in(key, axis), (), 0, extent[axis]) for axis in range(len(extent))]
    drawn = drawn.at[tuple(place)].set(low)
    longest = extent.index(max(extent))
    place[longest] = (place[longest] + 1) % extent[longest]
    return drawn.at[tuple(place)].set(largest)


def level_of(key, dims, shards, low, top_value):
    level = 1.0
    for axis_at, shards_of in shards:
        heights = jax.random.uniform(jax.random.fold_in(jax.random.fold_in(key, 6), axis_at), (shards_of,), jnp.float32, low / len(shards), top_value / len(shards))
        level = level * jnp.repeat(jnp.exp(heights), dims[axis_at] // shards_of).reshape((-1,) + (1,) * (len(dims) - 1 - axis_at))
    return level


def bell_draw(own_key, extent, scale, bound, shards=(), kind=jnp.bfloat16):
    array = jax.random.normal(own_key, extent, jnp.float32) * scale
    if len(shards) > 0:
        array = level_of(own_key, extent, shards, -0.22, 0.18) * array
    return jnp.clip(array, min=-bound, max=bound).astype(kind)


def setup_inputs(seed: int = 0, part: int = 0) -> dict:
    keys = jax.random.split(jax.random.key(seed), 8)
    own_keys = jax.random.split(jax.random.fold_in(keys[7], part), 8)
    surface_points = jnp.clip(jax.random.uniform(keys[0], (3, NPTS), jnp.float32, -4.0, 4.0) * level_of(keys[0], (3, NPTS), ((1, 32),), -0.4, 0.0), -4.0, 4.0)
    angle_ids = set_ends(jax.random.randint(own_keys[1], (ANGLE_COUNT,), 0, SWEEP), jax.random.fold_in(own_keys[1], 1), 0, SWEEP - 1).astype(jnp.int32)
    near_mask = set_ends((jax.random.randint(keys[2], (BOX_TOTAL, 8), 0, 4) < 3).astype(jnp.int32), jax.random.fold_in(keys[2], 1), 0, 1)
    skeleton = draw_skeleton(jax.random.fold_in(keys[7], 71), part)
    box_inverse_parts = bell_draw(keys[4], (BOX_TOTAL, 2, B, B), (2 * B) ** -0.5, 0.375, ((0, 32),), jnp.float32)
    near_coupling = bell_draw(keys[5], (BOX_TOTAL, 8, 2, SKELETON_COUNT, B), (16 * SKELETON_COUNT) ** -0.5, 0.25, ((0, 32),), jnp.float32)
    top_inverse = bell_draw(keys[6], (N_BLK, 2, SK, SK), (2 * SK) ** -0.5, 0.25, ((0, 4), (2, 8)), jnp.float32)
    return {"surface_points": surface_points, "angle_ids": angle_ids, "near_mask": near_mask, "skeleton": skeleton, "box_inverse_parts": box_inverse_parts, "near_coupling": near_coupling, "top_inverse": top_inverse}


wavenumber = 24.0
offsets = ((-1, -1), (-1, 0), (-1, 1), (0, -1), (0, 1), (1, -1), (1, 0), (1, 1))


def incident(points, angles):
    theta = angles.astype(jnp.float32) * (2.0 * jnp.pi / SWEEP)
    phase = wavenumber * (points[0][:, None] * jnp.cos(theta)[None, :] + points[1][:, None] * (0.6 * jnp.sin(theta))[None, :] + points[2][:, None] * (0.8 * jnp.sin(theta))[None, :])
    return jnp.stack([jnp.cos(phase), jnp.sin(phase)])


def complex_multiply(form, mat_re, mat_im, vec_re, vec_im):
    first = jnp.einsum(form, mat_re, vec_re, precision=lax.Precision.HIGHEST) - jnp.einsum(form, mat_im, vec_im, precision=lax.Precision.HIGHEST)
    second = jnp.einsum(form, mat_re, vec_im, precision=lax.Precision.HIGHEST) + jnp.einsum(form, mat_im, vec_re, precision=lax.Precision.HIGHEST)
    return first, second


def reference(surface_points, angle_ids, near_mask, skeleton, box_inverse_parts, near_coupling, top_inverse):
    field = incident(surface_points, angle_ids).reshape(2, BOX_TOTAL, B, ANGLE_COUNT)
    zre, zim = complex_multiply("brc,bca->bra", box_inverse_parts[:, 0], box_inverse_parts[:, 1], field[0], field[1])
    picker = jnp.broadcast_to(skeleton[:, :, None], (BOX_TOTAL, SKELETON_COUNT, ANGLE_COUNT))
    sre = jnp.take_along_axis(zre, picker, axis=1).reshape(N_BLK, Q, SKELETON_COUNT, ANGLE_COUNT)
    sim = jnp.take_along_axis(zim, picker, axis=1).reshape(N_BLK, Q, SKELETON_COUNT, ANGLE_COUNT)
    weights = near_coupling * near_mask.astype(jnp.float32)[:, :, None, None, None]
    weights = weights.reshape(N_BLK, Q, 8, 2, SKELETON_COUNT, B)
    cre = jnp.zeros((N_BLK, Q, B, ANGLE_COUNT), jnp.float32)
    cim = jnp.zeros((N_BLK, Q, B, ANGLE_COUNT), jnp.float32)
    for number, (step_s, step_q) in enumerate(offsets):
        near_re = jnp.roll(sre, (-step_s, -step_q), axis=(0, 1))
        near_im = jnp.roll(sim, (-step_s, -step_q), axis=(0, 1))
        term_re, term_im = complex_multiply("sqkr,sqka->sqra", weights[:, :, number, 0], weights[:, :, number, 1], near_re, near_im)
        cre = cre + term_re
        cim = cim + term_im
    weight_real = zre - cre.reshape(BOX_TOTAL, B, ANGLE_COUNT)
    wim = zim - cim.reshape(BOX_TOTAL, B, ANGLE_COUNT)
    tre = jnp.take_along_axis(weight_real, picker, axis=1).reshape(N_BLK, SK, ANGLE_COUNT)
    tim = jnp.take_along_axis(wim, picker, axis=1).reshape(N_BLK, SK, ANGLE_COUNT)
    output_real, yim = complex_multiply("src,sca->sra", top_inverse[:, 0], top_inverse[:, 1], tre, tim)
    one_hot_picker = (skeleton[:, :, None] == jnp.arange(B)[None, None, :]).astype(jnp.float32)
    vector_real = weight_real + jnp.einsum("wtj,wtc->wjc", one_hot_picker, output_real.reshape(BOX_TOTAL, SKELETON_COUNT, ANGLE_COUNT), precision=lax.Precision.HIGHEST)
    vector_imaginary = wim + jnp.einsum("wtj,wtc->wjc", one_hot_picker, yim.reshape(BOX_TOTAL, SKELETON_COUNT, ANGLE_COUNT), precision=lax.Precision.HIGHEST)
    solution_real, solution_imaginary = complex_multiply("vfd,vfg->vdg", box_inverse_parts[:, 0], box_inverse_parts[:, 1], vector_real, vector_imaginary)
    result = jnp.stack([solution_real.reshape(NPTS, ANGLE_COUNT), solution_imaginary.reshape(NPTS, ANGLE_COUNT)])
    return jnp.transpose(result, (0, 2, 1))
```

```python
import functools

import jax
import jax.numpy as jnp
import numpy as np
from jax import lax
from jax.experimental import pallas as pl
from jax.experimental.pallas import tpu as pltpu
from jax.sharding import PartitionSpec as P

SWEEP = 16384
WAVENUMBER = 24.0
F32 = jnp.float32
BF16 = jnp.bfloat16
VMEM = pl.BlockSpec(memory_space=pltpu.VMEM)
NN = (((1,), (0,)), ((), ()))
NT = (((1,), (1,)), ((), ()))
TN = (((0,), (0,)), ((), ()))

HALF_PI_1 = float(np.float32(201.0 / 128.0))
HALF_PI_2 = float(np.float32(np.round((np.pi / 2 - HALF_PI_1) * 2.0**22) / 2.0**22))
HALF_PI_3 = float(np.float32(np.pi / 2 - HALF_PI_1 - HALF_PI_2))


def cat(parts, axis):
    return jnp.concatenate(parts, axis=axis)


def dot(a, b, form=NN):
    return lax.dot_general(a, b, form, preferred_element_type=F32)


def split(x):
    high = x.astype(BF16)
    return high, (x - high.astype(F32)).astype(BF16)


def dot3(a, b, form=NN):
    return dot(a[0], b[0], form) + (dot(a[0], b[1], form) + dot(a[1], b[0], form))


def both(pair, function):
    return function(pair[0]), function(pair[1])


def sin_cos_small(r):
    s = r * r
    sin = r + r * s * (-1.6666654611e-1 + s * (8.3321608736e-3 - s * 1.9515295891e-4))
    cos = 1.0 - 0.5 * s + s * s * (4.166664568298827e-2 + s * (-1.388731625493765e-3 + s * 2.443315711809948e-5))
    return sin, cos


def by_quadrant(quadrant, sin, cos):
    odd = (quadrant & 1) == 1
    out_sin = jnp.where(odd, cos, sin)
    out_cos = jnp.where(odd, sin, cos)
    out_sin = jnp.where((quadrant & 2) == 2, -out_sin, out_sin)
    out_cos = jnp.where(((quadrant + 1) & 2) == 2, -out_cos, out_cos)
    return out_sin, out_cos


def one_hot(skeleton, width):
    rows = lax.broadcasted_iota(jnp.int32, (width, skeleton.shape[1]), 0)
    return jnp.where(rows == skeleton, 1.0, 0.0).astype(BF16)


def rows_form(re, im):
    return cat([cat([re, -im], 1), cat([im, re], 1)], 0)


def columns_form(re, im):
    return cat([cat([re, im], 1), cat([-im, re], 1)], 0)


def field_kernel(points, angles, skeleton, inverse, top, u_out, static_out, high_out, low_out):
    count = angles.shape[1]
    width = points.shape[1]
    rank = skeleton.shape[1]
    ids = angles[...]
    quadrant = (ids + SWEEP // 8) >> (SWEEP.bit_length() - 3)
    rest = ids - quadrant * (SWEEP // 4)
    sin, cos = by_quadrant(quadrant, *sin_cos_small(rest.astype(F32) * (2.0 * np.pi / SWEEP)))
    pick = lax.broadcasted_iota(jnp.int32, (8, count), 0) == 0
    columns = jnp.where(pick, cos, sin).T
    cos_column = columns[:, 0:1]
    sin_column = columns[:, 1:2]
    x = points[0:1, :] * WAVENUMBER
    yz = points[1:2, :] * (0.6 * WAVENUMBER) + points[2:3, :] * (0.8 * WAVENUMBER)
    phase = x * cos_column + yz * sin_column
    turns = jnp.round(phase * (2.0 / np.pi))
    r = ((phase - turns * HALF_PI_1) - turns * HALF_PI_2) - turns * HALF_PI_3
    field_sin, field_cos = by_quadrant(turns.astype(jnp.int32), *sin_cos_small(r))
    field = split(cat([field_cos, field_sin], 1))
    high_out[...] = field[0]
    low_out[...] = field[1]
    parts = split(cat([inverse[0, 0], inverse[0, 1]], 1))
    picker = one_hot(skeleton[...], width)
    rows = dot(picker, cat(parts, 1), TN)
    rows_high = rows[:, : 2 * width]
    rows_low = rows[:, 2 * width :]
    whole = rows_high + rows_low
    form = both((rows_high, rows_low), lambda v: rows_form(v[:, :width], v[:, width:]).astype(BF16))
    u_out[...] = dot3(form, field, NT)
    depth = top.shape[3]
    for part in range(2):
        at = slice(part * rank, (part + 1) * rank)
        static_out[at, :depth] = top[0, part]
        static_out[at, depth:] = whole[:, part * width : (part + 1) * width]


def coupling_kernel(high, low, skeleton, mask, inverse, coupling, base_out, high_out, low_out):
    width = inverse.shape[2]
    sides = coupling.shape[1]
    rank = coupling.shape[3]
    depth = sides * rank
    field = (high[...], low[...])
    re = split(inverse[0, 0])
    im = split(inverse[0, 1])
    row_matrix = (rows_form(re[0], im[0]), rows_form(re[1], im[1]))
    column_matrix = (columns_form(re[0], im[0]), columns_form(re[1], im[1]))
    picker = one_hot(skeleton[...], width)
    zero = jnp.zeros_like(picker)
    picker2 = cat([cat([picker, zero], 1), cat([zero, picker], 1)], 0)
    z = split(dot3(field, row_matrix, NT))
    u = dot(z[0], picker2) + dot(z[1], picker2)
    near = []
    for side in range(sides):
        weight = mask[0, side].astype(F32)
        near.append(cat([coupling[0, side, 0] * weight, coupling[0, side, 1] * weight], 1))
    near = split(cat(near, 0))
    base_out[:, : 2 * width] = dot3(z, column_matrix)
    base_out[:, 2 * width :] = u
    applied = split(dot3(near, column_matrix))
    for k, out in enumerate((high_out, low_out)):
        chosen = dot(near[k], picker2).astype(BF16)
        for matrix, at, part in ((applied[k], 0, width), (chosen, 2 * width, rank)):
            out[:depth, at : at + 2 * part] = matrix
            out[depth:, at : at + part] = -matrix[:, part:]
            out[depth:, at + part : at + 2 * part] = matrix[:, :part]


def message_kernel(up, down, left, right, base, high, low, out):
    boxes = out.shape[0]
    count = base.shape[0]
    width = out.shape[2]
    rank = up.shape[0] // 2
    share = count // boxes
    half = share // 2
    order = (left[0], up[...], right[0], left[1], right[1], left[2], down[...], right[2])
    stacked = cat([v[:rank] for v in order] + [v[rank:] for v in order], 0)
    near = split(stacked.T)
    w = base[...] - dot3(near, (high[...], low[...]))
    for box in range(boxes):
        at = box * share
        out[box, :share] = w[at : at + share, :width]
        out[box, share : 2 * share] = w[at : at + share, width : 2 * width]
        t = w[at : at + share, 2 * width :]
        out[box, 2 * share : 2 * share + half] = cat([t[:half], t[half:]], 1)


def top_kernel(message, static, out):
    boxes = message.shape[0]
    width = message.shape[2]
    share = out.shape[1]
    half = share // 2
    rank = static.shape[1] // 2
    depth = boxes * rank
    t_re = []
    t_im = []
    for box in range(boxes):
        packed = message[box, 2 * share : 2 * share + half]
        t = cat([packed[:, : 2 * rank], packed[:, 2 * rank :]], 0)
        t_re.append(t[:, :rank])
        t_im.append(t[:, rank:])
    t = split(cat(t_re + t_im, 1))
    top = []
    for box in range(boxes):
        top.append(rows_form(static[box, :rank, :depth], static[box, rank:, :depth]))
    y = dot3(t, split(cat(top, 0)), NT)
    for box in range(boxes):
        local = split(columns_form(static[box, :rank, depth:], static[box, rank:, depth:]))
        part = split(y[:, box * 2 * rank : (box + 1) * 2 * rank])
        x = dot3(part, local)
        at = slice(box * width, (box + 1) * width)
        out[0, :, at] = message[box, :share] + x[:, :width]
        out[1, :, at] = message[box, share : 2 * share] + x[:, width:]


def call(kernel, outs, *arrays, smem=()):
    specs = [pl.BlockSpec(memory_space=pltpu.SMEM) if i in smem else VMEM for i in range(len(arrays))]
    return pl.pallas_call(
        kernel,
        out_shape=[jax.ShapeDtypeStruct(shape, dtype) for shape, dtype in outs],
        in_specs=specs,
        out_specs=[VMEM] * len(outs),
        compiler_params=pltpu.CompilerParams(vmem_limit_bytes=40 * 1024 * 1024),
    )(*arrays)


def shifted(value, axis, step):
    count = lax.axis_size(axis)
    return lax.ppermute(value, axis, [(i, (i + step) % count) for i in range(count)])


def on_device(surface_points, angle_ids, near_mask, skeleton, box_inverse_parts, near_coupling, top_inverse):
    boxes = lax.axis_size("box")
    width = box_inverse_parts.shape[2]
    count = angle_ids.shape[0]
    rank = skeleton.shape[1]
    sides = near_mask.shape[1]
    depth = top_inverse.shape[3]
    share = count // boxes
    u, static, high, low = call(
        field_kernel,
        [
            ((2 * rank, count), F32),
            ((2 * rank, depth + width), F32),
            ((count, 2 * width), BF16),
            ((count, 2 * width), BF16),
        ],
        surface_points, angle_ids.reshape(1, count), skeleton, box_inverse_parts, top_inverse,
    )
    up = shifted(u, "blk", 1)
    down = shifted(u, "blk", -1)
    column = jnp.stack([up, u, down])
    left = shifted(column, "box", 1)
    right = shifted(column, "box", -1)
    static = lax.all_gather(static, "box")
    base, matrix_high, matrix_low = call(
        coupling_kernel,
        [
            ((count, 2 * width + 2 * rank), F32),
            ((2 * sides * rank, 2 * width + 2 * rank), BF16),
            ((2 * sides * rank, 2 * width + 2 * rank), BF16),
        ],
        high, low, skeleton, near_mask, box_inverse_parts, near_coupling, smem=(3,),
    )
    rows = 2 * share + -(-share // 16) * 8
    (message,) = call(
        message_kernel, [((boxes, rows, width), F32)],
        up, down, left, right, base, matrix_high, matrix_low,
    )
    message = lax.all_to_all(message, "box", split_axis=0, concat_axis=0, tiled=True)
    (out,) = call(top_kernel, [((2, share, boxes * width), F32)], message, static)
    return out


def solution(mesh):
    return jax.shard_map(
        on_device,
        mesh=mesh,
        in_specs=(
            P(None, ("blk", "box")),
            P("batch"),
            P(("blk", "box"), None),
            P(("blk", "box"), None),
            P(("blk", "box"), None, None, None),
            P(("blk", "box"), None, None, None, None),
            P("blk", None, "box", None),
        ),
        out_specs=P(None, ("batch", "box"), "blk"),
        check_vma=False,
    )
```

```python
import functools

import jax
import jax.numpy as jnp
import numpy as np
from jax import lax
from jax.experimental import pallas as pl
from jax.experimental.pallas import tpu as pltpu
from jax.sharding import PartitionSpec as P

SWEEP = 16384
WAVENUMBER = 24.0
F32 = jnp.float32
BF16 = jnp.bfloat16
VMEM = pl.BlockSpec(memory_space=pltpu.VMEM)
NN = (((1,), (0,)), ((), ()))
NT = (((1,), (1,)), ((), ()))
TN = (((0,), (0,)), ((), ()))

HALF_PI_1 = float(np.float32(201.0 / 128.0))
HALF_PI_2 = float(np.float32(np.round((np.pi / 2 - HALF_PI_1) * 2.0**22) / 2.0**22))
HALF_PI_3 = float(np.float32(np.pi / 2 - HALF_PI_1 - HALF_PI_2))


def cat(parts, axis):
    return jnp.concatenate(parts, axis=axis)


def dot(a, b, form=NN):
    return lax.dot_general(a, b, form, preferred_element_type=F32)


def split(x):
    high = x.astype(BF16)
    return high, (x - high.astype(F32)).astype(BF16)


def dot3(a, b, form=NN):
    return dot(a[0], b[0], form) + (dot(a[0], b[1], form) + dot(a[1], b[0], form))


def both(pair, function):
    return function(pair[0]), function(pair[1])


def sin_cos_small(r):
    s = r * r
    sin = r + r * s * (-1.6666654611e-1 + s * (8.3321608736e-3 - s * 1.9515295891e-4))
    cos = 1.0 - 0.5 * s + s * s * (4.166664568298827e-2 + s * (-1.388731625493765e-3 + s * 2.443315711809948e-5))
    return sin, cos


def by_quadrant(quadrant, sin, cos):
    odd = (quadrant & 1) == 1
    out_sin = jnp.where(odd, cos, sin)
    out_cos = jnp.where(odd, sin, cos)
    out_sin = jnp.where((quadrant & 2) == 2, -out_sin, out_sin)
    out_cos = jnp.where(((quadrant + 1) & 2) == 2, -out_cos, out_cos)
    return out_sin, out_cos


def one_hot(skeleton, width):
    rows = lax.broadcasted_iota(jnp.int32, (width, skeleton.shape[1]), 0)
    return jnp.where(rows == skeleton, 1.0, 0.0).astype(BF16)


def rows_form(re, im):
    return cat([cat([re, -im], 1), cat([im, re], 1)], 0)


def columns_form(re, im):
    return cat([cat([re, im], 1), cat([-im, re], 1)], 0)


def field_kernel(points_in, angles_in, skeleton_in, inverse_in, top_in, u_out, static_out, high_out, low_out,
                 points, angles, skeleton, inverse, top, sems):
    copies = [
        pltpu.make_async_copy(source, target, sems.at[k])
        for k, (source, target) in enumerate((
            (angles_in, angles), (points_in, points), (skeleton_in, skeleton), (inverse_in, inverse), (top_in, top),
        ))
    ]
    for copy in copies:
        copy.start()
    count = angles.shape[1]
    width = points.shape[1]
    rank = skeleton.shape[1]
    copies[0].wait()
    ids = angles[...]
    quadrant = (ids + SWEEP // 8) >> (SWEEP.bit_length() - 3)
    rest = ids - quadrant * (SWEEP // 4)
    sin, cos = by_quadrant(quadrant, *sin_cos_small(rest.astype(F32) * (2.0 * np.pi / SWEEP)))
    pick = lax.broadcasted_iota(jnp.int32, (8, count), 0) == 0
    columns = jnp.where(pick, cos, sin).T
    cos_column = columns[:, 0:1]
    sin_column = columns[:, 1:2]
    copies[1].wait()
    x = points[0:1, :] * WAVENUMBER
    yz = points[1:2, :] * (0.6 * WAVENUMBER) + points[2:3, :] * (0.8 * WAVENUMBER)
    phase = x * cos_column + yz * sin_column
    turns = jnp.round(phase * (2.0 / np.pi))
    r = ((phase - turns * HALF_PI_1) - turns * HALF_PI_2) - turns * HALF_PI_3
    field_sin, field_cos = by_quadrant(turns.astype(jnp.int32), *sin_cos_small(r))
    field = split(cat([field_cos, field_sin], 1))
    high_out[...] = field[0]
    low_out[...] = field[1]
    copies[2].wait()
    picker = one_hot(skeleton[...], width)
    copies[3].wait()
    parts = split(cat([inverse[0, 0], inverse[0, 1]], 1))
    rows = dot(picker, cat(parts, 1), TN)
    rows_high = rows[:, : 2 * width]
    rows_low = rows[:, 2 * width :]
    whole = rows_high + rows_low
    form = both((rows_high, rows_low), lambda v: rows_form(v[:, :width], v[:, width:]).astype(BF16))
    u_out[...] = dot3(form, field, NT)
    depth = top.shape[3]
    copies[4].wait()
    for part in range(2):
        at = slice(part * rank, (part + 1) * rank)
        static_out[at, :depth] = top[0, part]
        static_out[at, depth:] = whole[:, part * width : (part + 1) * width]


def coupling_kernel(high, low, skeleton, mask, inverse, coupling, base_out, high_out, low_out):
    width = inverse.shape[2]
    sides = coupling.shape[1]
    rank = coupling.shape[3]
    depth = sides * rank
    field = (high[...], low[...])
    re = split(inverse[0, 0])
    im = split(inverse[0, 1])
    row_matrix = (rows_form(re[0], im[0]), rows_form(re[1], im[1]))
    column_matrix = (columns_form(re[0], im[0]), columns_form(re[1], im[1]))
    picker = one_hot(skeleton[...], width)
    zero = jnp.zeros_like(picker)
    picker2 = cat([cat([picker, zero], 1), cat([zero, picker], 1)], 0)
    z = split(dot3(field, row_matrix, NT))
    u = dot(z[0], picker2) + dot(z[1], picker2)
    near = []
    for side in range(sides):
        weight = mask[0, side].astype(F32)
        near.append(cat([coupling[0, side, 0] * weight, coupling[0, side, 1] * weight], 1))
    near = split(cat(near, 0))
    base_out[:, : 2 * width] = dot3(z, column_matrix)
    base_out[:, 2 * width :] = u
    applied = split(dot3(near, column_matrix))
    for k, out in enumerate((high_out, low_out)):
        chosen = dot(near[k], picker2).astype(BF16)
        for matrix, at, part in ((applied[k], 0, width), (chosen, 2 * width, rank)):
            out[:depth, at : at + 2 * part] = matrix
            out[depth:, at : at + part] = -matrix[:, part:]
            out[depth:, at + part : at + 2 * part] = matrix[:, :part]


def message_kernel(up, middle, down, base, high, low, out):
    boxes = out.shape[0]
    count = base.shape[0]
    width = out.shape[2]
    rank = up.shape[1] // 2
    share = count // boxes
    half = share // 2
    order = (up[0], up[1], up[2], middle[0], middle[2], down[0], down[1], down[2])
    stacked = cat([v[:rank] for v in order] + [v[rank:] for v in order], 0)
    near = split(stacked.T)
    w = base[...] - dot3(near, (high[...], low[...]))
    for box in range(boxes):
        at = box * share
        out[box, :share] = w[at : at + share, :width]
        out[box, share : 2 * share] = w[at : at + share, width : 2 * width]
        t = w[at : at + share, 2 * width :]
        out[box, 2 * share : 2 * share + half] = cat([t[:half], t[half:]], 1)


def top_kernel(message, kept, came, out):
    boxes = message.shape[0]
    width = message.shape[2]
    share = out.shape[1]
    half = share // 2
    rank = kept.shape[1] // 2
    depth = boxes * rank
    me = lax.axis_index("box")
    offsets = [0]
    while len(offsets) < boxes:
        offsets += [k ^ (boxes // 2 // len(offsets)) for k in offsets]
    t_re = []
    t_im = []
    for box in range(boxes):
        packed = message[box, 2 * share : 2 * share + half]
        t = cat([packed[:, : 2 * rank], packed[:, 2 * rank :]], 0)
        t_re.append(t[:, :rank])
        t_im.append(t[:, rank:])
    t = split(cat(t_re + t_im, 1))
    static = [kept[k] for k in range(boxes // 2)] + [came[k] for k in range(boxes // 2)]
    top = []
    for v in static:
        top.append(rows_form(v[:rank, :depth], v[rank:, :depth]))
    y = dot3(t, split(cat(top, 0)), NT)
    for k, v in enumerate(static):
        box = me ^ offsets[k]
        local = split(columns_form(v[:rank, depth:], v[rank:, depth:]))
        part = split(y[:, k * 2 * rank : (k + 1) * 2 * rank])
        x = dot3(part, local)
        at = pl.ds(pl.multiple_of(box * width, width), width)
        out[0, :, at] = message[box, :share] + x[:, :width]
        out[1, :, at] = message[box, share : 2 * share] + x[:, width:]


def call(kernel, outs, *arrays, smem=(), hbm=(), scratch=()):
    spaces = {i: pl.BlockSpec(memory_space=pltpu.SMEM) for i in smem}
    spaces.update({i: pl.BlockSpec(memory_space=pl.ANY) for i in hbm})
    return pl.pallas_call(
        kernel,
        out_shape=[jax.ShapeDtypeStruct(shape, dtype) for shape, dtype in outs],
        in_specs=[spaces.get(i, VMEM) for i in range(len(arrays))],
        out_specs=[VMEM] * len(outs),
        scratch_shapes=scratch,
        compiler_params=pltpu.CompilerParams(vmem_limit_bytes=40 * 1024 * 1024),
    )(*arrays)


def shifted(value, axis, step):
    count = lax.axis_size(axis)
    return lax.ppermute(value, axis, [(i, (i + step) % count) for i in range(count)])


def on_device(surface_points, angle_ids, near_mask, skeleton, box_inverse_parts, near_coupling, top_inverse):
    boxes = lax.axis_size("box")
    width = box_inverse_parts.shape[2]
    count = angle_ids.shape[0]
    rank = skeleton.shape[1]
    sides = near_mask.shape[1]
    depth = top_inverse.shape[3]
    share = count // boxes
    arrays = (surface_points, angle_ids.reshape(1, count), skeleton, box_inverse_parts, top_inverse)
    u, static, high, low = call(
        field_kernel,
        [
            ((2 * rank, count), F32),
            ((2 * rank, depth + width), F32),
            ((count, 2 * width), BF16),
            ((count, 2 * width), BF16),
        ],
        *arrays,
        hbm=range(len(arrays)),
        scratch=[pltpu.VMEM(v.shape, v.dtype) for v in arrays] + [pltpu.SemaphoreType.DMA((len(arrays),))],
    )
    left = shifted(u, "box", 1)
    right = shifted(u, "box", -1)
    row = jnp.stack([left, u, right])
    up = shifted(row, "blk", 1)
    down = shifted(row, "blk", -1)
    kept = static[None]
    step = boxes // 2
    while step > 0:
        came = lax.ppermute(kept, "box", [(i, i ^ step) for i in range(boxes)])
        if step > 1:
            kept = jnp.concatenate([kept, came])
        step //= 2
    base, matrix_high, matrix_low = call(
        coupling_kernel,
        [
            ((count, 2 * width + 2 * rank), F32),
            ((2 * sides * rank, 2 * width + 2 * rank), BF16),
            ((2 * sides * rank, 2 * width + 2 * rank), BF16),
        ],
        high, low, skeleton, near_mask, box_inverse_parts, near_coupling, smem=(3,),
    )
    rows = 2 * share + -(-share // 16) * 8
    (message,) = call(
        message_kernel, [((boxes, rows, width), F32)],
        up, row, down, base, matrix_high, matrix_low,
    )
    message = lax.all_to_all(message, "box", split_axis=0, concat_axis=0, tiled=True)
    (out,) = call(top_kernel, [((2, share, boxes * width), F32)], message, kept, came)
    return out


def solution(mesh):
    return jax.shard_map(
        on_device,
        mesh=mesh,
        in_specs=(
            P(None, ("blk", "box")),
            P("batch"),
            P(("blk", "box"), None),
            P(("blk", "box"), None),
            P(("blk", "box"), None, None, None),
            P(("blk", "box"), None, None, None, None),
            P("blk", None, "box", None),
        ),
        out_specs=P(None, ("batch", "box"), "blk"),
        check_vma=False,
    )
```

```python
import functools

import jax
import jax.numpy as jnp
import numpy as np
from jax import lax
from jax.experimental import pallas as pl
from jax.experimental.pallas import tpu as pltpu
from jax.sharding import PartitionSpec as P

SWEEP = 16384
WAVENUMBER = 24.0
F32 = jnp.float32
BF16 = jnp.bfloat16
VMEM = pl.BlockSpec(memory_space=pltpu.VMEM)
NN = (((1,), (0,)), ((), ()))
NT = (((1,), (1,)), ((), ()))
TN = (((0,), (0,)), ((), ()))

HALF_PI_1 = float(np.float32(201.0 / 128.0))
HALF_PI_2 = float(np.float32(np.round((np.pi / 2 - HALF_PI_1) * 2.0**22) / 2.0**22))
HALF_PI_3 = float(np.float32(np.pi / 2 - HALF_PI_1 - HALF_PI_2))


def cat(parts, axis):
    return jnp.concatenate(parts, axis=axis)


def dot(a, b, form=NN):
    return lax.dot_general(a, b, form, preferred_element_type=F32)


def split(x):
    high = x.astype(BF16)
    return high, (x - high.astype(F32)).astype(BF16)


def dot3(a, b, form=NN):
    return dot(a[0], b[0], form) + (dot(a[0], b[1], form) + dot(a[1], b[0], form))


def both(pair, function):
    return function(pair[0]), function(pair[1])


def sin_cos_small(r):
    s = r * r
    sin = r + r * s * (-1.6666654611e-1 + s * (8.3321608736e-3 - s * 1.9515295891e-4))
    cos = 1.0 - 0.5 * s + s * s * (4.166664568298827e-2 + s * (-1.388731625493765e-3 + s * 2.443315711809948e-5))
    return sin, cos


def by_quadrant(quadrant, sin, cos):
    odd = (quadrant & 1) == 1
    out_sin = jnp.where(odd, cos, sin)
    out_cos = jnp.where(odd, sin, cos)
    out_sin = jnp.where((quadrant & 2) == 2, -out_sin, out_sin)
    out_cos = jnp.where(((quadrant + 1) & 2) == 2, -out_cos, out_cos)
    return out_sin, out_cos


def one_hot(skeleton, width):
    rows = lax.broadcasted_iota(jnp.int32, (width, skeleton.shape[1]), 0)
    return jnp.where(rows == skeleton, 1.0, 0.0).astype(BF16)


def rows_form(re, im):
    return cat([cat([re, -im], 1), cat([im, re], 1)], 0)


def columns_form(re, im):
    return cat([cat([re, im], 1), cat([-im, re], 1)], 0)


def field_kernel(points_in, angles_in, skeleton_in, inverse_in, top_in, u_out, static_out, high_out, low_out,
                 points, angles, skeleton, inverse, top, sems):
    copies = [
        pltpu.make_async_copy(source, target, sems.at[k])
        for k, (source, target) in enumerate((
            (angles_in, angles), (points_in, points), (skeleton_in, skeleton), (inverse_in, inverse), (top_in, top),
        ))
    ]
    for copy in copies:
        copy.start()
    count = angles.shape[1]
    width = points.shape[1]
    rank = skeleton.shape[1]
    copies[0].wait()
    ids = angles[...]
    quadrant = (ids + SWEEP // 8) >> (SWEEP.bit_length() - 3)
    rest = ids - quadrant * (SWEEP // 4)
    sin, cos = by_quadrant(quadrant, *sin_cos_small(rest.astype(F32) * (2.0 * np.pi / SWEEP)))
    pick = lax.broadcasted_iota(jnp.int32, (8, count), 0) == 0
    columns = jnp.where(pick, cos, sin).T
    cos_column = columns[:, 0:1]
    sin_column = columns[:, 1:2]
    copies[1].wait()
    x = points[0:1, :] * WAVENUMBER
    yz = points[1:2, :] * (0.6 * WAVENUMBER) + points[2:3, :] * (0.8 * WAVENUMBER)
    phase = x * cos_column + yz * sin_column
    turns = jnp.round(phase * (2.0 / np.pi))
    r = ((phase - turns * HALF_PI_1) - turns * HALF_PI_2) - turns * HALF_PI_3
    field_sin, field_cos = by_quadrant(turns.astype(jnp.int32), *sin_cos_small(r))
    field = split(cat([field_cos, field_sin], 1))
    high_out[...] = field[0]
    low_out[...] = field[1]
    copies[2].wait()
    picker = one_hot(skeleton[...], width)
    copies[3].wait()
    parts = split(cat([inverse[0, 0], inverse[0, 1]], 1))
    rows = dot(picker, cat(parts, 1), TN)
    rows_high = rows[:, : 2 * width]
    rows_low = rows[:, 2 * width :]
    whole = rows_high + rows_low
    form = both((rows_high, rows_low), lambda v: rows_form(v[:, :width], v[:, width:]).astype(BF16))
    u_out[...] = dot3(form, field, NT)
    depth = top.shape[3]
    copies[4].wait()
    for part in range(2):
        at = slice(part * rank, (part + 1) * rank)
        static_out[at, :depth] = top[0, part]
        static_out[at, depth:] = whole[:, part * width : (part + 1) * width]


def coupling_kernel(high, low, skeleton, mask, inverse, coupling, base_out, high_out, low_out):
    width = inverse.shape[2]
    sides = coupling.shape[1]
    rank = coupling.shape[3]
    depth = sides * rank
    field = (high[...], low[...])
    re = split(inverse[0, 0])
    im = split(inverse[0, 1])
    row_matrix = (rows_form(re[0], im[0]), rows_form(re[1], im[1]))
    column_matrix = (columns_form(re[0], im[0]), columns_form(re[1], im[1]))
    picker = one_hot(skeleton[...], width)
    zero = jnp.zeros_like(picker)
    picker2 = cat([cat([picker, zero], 1), cat([zero, picker], 1)], 0)
    z = split(dot3(field, row_matrix, NT))
    u = dot(z[0], picker2) + dot(z[1], picker2)
    near = []
    for side in range(sides):
        weight = mask[0, side].astype(F32)
        near.append(cat([coupling[0, side, 0] * weight, coupling[0, side, 1] * weight], 1))
    near = split(cat(near, 0))
    base_out[:, : 2 * width] = dot3(z, column_matrix)
    base_out[:, 2 * width :] = u
    applied = split(dot3(near, column_matrix))
    for k, out in enumerate((high_out, low_out)):
        chosen = dot(near[k], picker2).astype(BF16)
        for matrix, at, part in ((applied[k], 0, width), (chosen, 2 * width, rank)):
            out[:depth, at : at + 2 * part] = matrix
            out[depth:, at : at + part] = -matrix[:, part:]
            out[depth:, at + part : at + 2 * part] = matrix[:, :part]


def join_kernel(left, u, right, mine, came, row_out, pair_out):
    row_out[0] = left[...]
    row_out[1] = u[...]
    row_out[2] = right[...]
    pair_out[0] = mine[...]
    pair_out[1] = came[...]


def message_kernel(up, middle, down, base, high, low, out):
    boxes = out.shape[0]
    count = base.shape[0]
    width = out.shape[2]
    rank = up.shape[1] // 2
    share = count // boxes
    half = share // 2
    order = (up[0], up[1], up[2], middle[0], middle[2], down[0], down[1], down[2])
    stacked = cat([v[:rank] for v in order] + [v[rank:] for v in order], 0)
    near = split(stacked.T)
    w = base[...] - dot3(near, (high[...], low[...]))
    for box in range(boxes):
        at = box * share
        out[box, :share] = w[at : at + share, :width]
        out[box, share : 2 * share] = w[at : at + share, width : 2 * width]
        t = w[at : at + share, 2 * width :]
        out[box, 2 * share : 2 * share + half] = cat([t[:half], t[half:]], 1)


def top_kernel(offsets, message, *refs):
    static_in, out = refs[:-1], refs[-1]
    boxes = message.shape[0]
    width = message.shape[2]
    share = out.shape[1]
    half = share // 2
    rank = static_in[0].shape[1] // 2
    depth = boxes * rank
    me = lax.axis_index("box")
    t_re = []
    t_im = []
    for box in range(boxes):
        packed = message[box, 2 * share : 2 * share + half]
        t = cat([packed[:, : 2 * rank], packed[:, 2 * rank :]], 0)
        t_re.append(t[:, :rank])
        t_im.append(t[:, rank:])
    t = split(cat(t_re + t_im, 1))
    static = [v[k] for v in static_in for k in range(v.shape[0])]
    top = []
    for v in static:
        top.append(rows_form(v[:rank, :depth], v[rank:, :depth]))
    y = dot3(t, split(cat(top, 0)), NT)
    for k, v in enumerate(static):
        box = k if offsets is None else me ^ offsets[k]
        local = split(columns_form(v[:rank, depth:], v[rank:, depth:]))
        part = split(y[:, k * 2 * rank : (k + 1) * 2 * rank])
        x = dot3(part, local)
        at = pl.ds(pl.multiple_of(box * width, width), width)
        out[0, :, at] = message[box, :share] + x[:, :width]
        out[1, :, at] = message[box, share : 2 * share] + x[:, width:]


def call(kernel, outs, *arrays, smem=(), hbm=(), scratch=()):
    spaces = {i: pl.BlockSpec(memory_space=pltpu.SMEM) for i in smem}
    spaces.update({i: pl.BlockSpec(memory_space=pltpu.HBM) for i in hbm})
    return pl.pallas_call(
        kernel,
        out_shape=[jax.ShapeDtypeStruct(shape, dtype) for shape, dtype in outs],
        in_specs=[spaces.get(i, VMEM) for i in range(len(arrays))],
        out_specs=[VMEM] * len(outs),
        scratch_shapes=scratch,
        compiler_params=pltpu.CompilerParams(vmem_limit_bytes=40 * 1024 * 1024),
    )(*arrays)


def shifted(value, axis, step):
    count = lax.axis_size(axis)
    return lax.ppermute(value, axis, [(i, (i + step) % count) for i in range(count)])


def swapped(value, axis, bit):
    return lax.ppermute(value, axis, [(i, i ^ bit) for i in range(lax.axis_size(axis))])


def on_device(surface_points, angle_ids, near_mask, skeleton, box_inverse_parts, near_coupling, top_inverse):
    boxes = lax.axis_size("box")
    width = box_inverse_parts.shape[2]
    count = angle_ids.shape[0]
    rank = skeleton.shape[1]
    sides = near_mask.shape[1]
    depth = top_inverse.shape[3]
    share = count // boxes
    arrays = (surface_points, angle_ids.reshape(1, count), skeleton, box_inverse_parts, top_inverse)
    arrays = [pltpu.with_memory_space_constraint(v, pltpu.HBM) for v in arrays]
    u, static, high, low = call(
        field_kernel,
        [
            ((2 * rank, count), F32),
            ((2 * rank, depth + width), F32),
            ((count, 2 * width), BF16),
            ((count, 2 * width), BF16),
        ],
        *arrays,
        hbm=range(len(arrays)),
        scratch=[pltpu.VMEM(v.shape, v.dtype) for v in arrays] + [pltpu.SemaphoreType.DMA((len(arrays),))],
    )
    left = shifted(u, "box", 1)
    right = shifted(u, "box", -1)
    if boxes == 8:
        came = swapped(static, "box", 4)
        row, pair = call(
            join_kernel, [((3,) + u.shape, F32), ((2,) + static.shape, F32)], left, u, right, static, came
        )
        over_two = swapped(pair, "box", 2)
        over_one = swapped(pair, "box", 1)
        over_three = swapped(over_one[:1], "box", 2)
        over_seven = swapped(over_two[1:], "box", 1)
        static = (pair, over_two, over_one, over_three, over_seven)
        offsets = (0, 4, 2, 6, 1, 5, 3, 7)
    else:
        row = jnp.stack([left, u, right])
        static = (lax.all_gather(static, "box"),)
        offsets = None
    up = shifted(row, "blk", 1)
    down = shifted(row, "blk", -1)
    base, matrix_high, matrix_low = call(
        coupling_kernel,
        [
            ((count, 2 * width + 2 * rank), F32),
            ((2 * sides * rank, 2 * width + 2 * rank), BF16),
            ((2 * sides * rank, 2 * width + 2 * rank), BF16),
        ],
        high, low, skeleton, near_mask, box_inverse_parts, near_coupling, smem=(3,),
    )
    rows = 2 * share + -(-share // 16) * 8
    (message,) = call(
        message_kernel, [((boxes, rows, width), F32)],
        up, row, down, base, matrix_high, matrix_low,
    )
    message = lax.all_to_all(message, "box", split_axis=0, concat_axis=0, tiled=True)
    (out,) = call(
        functools.partial(top_kernel, offsets), [((2, share, boxes * width), F32)], message, *static
    )
    return out


def solution(mesh):
    return jax.shard_map(
        on_device,
        mesh=mesh,
        in_specs=(
            P(None, ("blk", "box")),
            P("batch"),
            P(("blk", "box"), None),
            P(("blk", "box"), None),
            P(("blk", "box"), None, None, None),
            P(("blk", "box"), None, None, None, None),
            P("blk", None, "box", None),
        ),
        out_specs=P(None, ("batch", "box"), "blk"),
        check_vma=False,
    )
```

```python
import functools

import jax
import jax.numpy as jnp
import numpy as np
from jax import lax
from jax.experimental import pallas as pl
from jax.experimental.pallas import tpu as pltpu
from jax.sharding import PartitionSpec as P

SWEEP = 16384
WAVENUMBER = 24.0
F32 = jnp.float32
BF16 = jnp.bfloat16
VMEM = pl.BlockSpec(memory_space=pltpu.VMEM)
NN = (((1,), (0,)), ((), ()))
NT = (((1,), (1,)), ((), ()))
TN = (((0,), (0,)), ((), ()))

HALF_PI_1 = float(np.float32(201.0 / 128.0))
HALF_PI_2 = float(np.float32(np.round((np.pi / 2 - HALF_PI_1) * 2.0**22) / 2.0**22))
HALF_PI_3 = float(np.float32(np.pi / 2 - HALF_PI_1 - HALF_PI_2))


def cat(parts, axis):
    return jnp.concatenate(parts, axis=axis)


def dot(a, b, form=NN):
    return lax.dot_general(a, b, form, preferred_element_type=F32)


def split(x):
    high = x.astype(BF16)
    return high, (x - high.astype(F32)).astype(BF16)


def dot3(a, b, form=NN):
    return dot(a[0], b[0], form) + (dot(a[0], b[1], form) + dot(a[1], b[0], form))


def both(pair, function):
    return function(pair[0]), function(pair[1])


def sin_cos_small(r):
    s = r * r
    sin = r + r * s * (-1.6666654611e-1 + s * (8.3321608736e-3 - s * 1.9515295891e-4))
    cos = 1.0 - 0.5 * s + s * s * (4.166664568298827e-2 + s * (-1.388731625493765e-3 + s * 2.443315711809948e-5))
    return sin, cos


def by_quadrant(quadrant, sin, cos):
    odd = (quadrant & 1) == 1
    out_sin = jnp.where(odd, cos, sin)
    out_cos = jnp.where(odd, sin, cos)
    out_sin = jnp.where((quadrant & 2) == 2, -out_sin, out_sin)
    out_cos = jnp.where(((quadrant + 1) & 2) == 2, -out_cos, out_cos)
    return out_sin, out_cos


def one_hot(skeleton, width):
    rows = lax.broadcasted_iota(jnp.int32, (width, skeleton.shape[1]), 0)
    return jnp.where(rows == skeleton, 1.0, 0.0).astype(BF16)


def rows_form(re, im):
    return cat([cat([re, -im], 1), cat([im, re], 1)], 0)


def columns_form(re, im):
    return cat([cat([re, im], 1), cat([-im, re], 1)], 0)


def field_kernel(points_in, angles_in, skeleton_in, inverse_in, top_in, u_out, static_out, high_out, low_out,
                 points, angles, skeleton, inverse, top, sems):
    copies = [
        pltpu.make_async_copy(source, target, sems.at[k])
        for k, (source, target) in enumerate((
            (angles_in, angles), (points_in, points), (skeleton_in, skeleton), (inverse_in, inverse), (top_in, top),
        ))
    ]
    for copy in copies:
        copy.start()
    count = angles.shape[1]
    width = points.shape[1]
    rank = skeleton.shape[1]
    copies[0].wait()
    ids = angles[...]
    quadrant = (ids + SWEEP // 8) >> (SWEEP.bit_length() - 3)
    rest = ids - quadrant * (SWEEP // 4)
    sin, cos = by_quadrant(quadrant, *sin_cos_small(rest.astype(F32) * (2.0 * np.pi / SWEEP)))
    pick = lax.broadcasted_iota(jnp.int32, (8, count), 0) == 0
    columns = jnp.where(pick, cos, sin).T
    cos_column = columns[:, 0:1]
    sin_column = columns[:, 1:2]
    copies[1].wait()
    x = points[0:1, :] * WAVENUMBER
    yz = points[1:2, :] * (0.6 * WAVENUMBER) + points[2:3, :] * (0.8 * WAVENUMBER)
    phase = x * cos_column + yz * sin_column
    turns = jnp.round(phase * (2.0 / np.pi))
    r = ((phase - turns * HALF_PI_1) - turns * HALF_PI_2) - turns * HALF_PI_3
    field_sin, field_cos = by_quadrant(turns.astype(jnp.int32), *sin_cos_small(r))
    field = split(cat([field_cos, field_sin], 1))
    high_out[...] = field[0]
    low_out[...] = field[1]
    copies[2].wait()
    picker = one_hot(skeleton[...], width)
    copies[3].wait()
    parts = split(cat([inverse[0, 0], inverse[0, 1]], 1))
    rows = dot(picker, cat(parts, 1), TN)
    rows_high = rows[:, : 2 * width]
    rows_low = rows[:, 2 * width :]
    whole = rows_high + rows_low
    form = both((rows_high, rows_low), lambda v: rows_form(v[:, :width], v[:, width:]).astype(BF16))
    u_out[...] = dot3(form, field, NT)
    depth = top.shape[3]
    copies[4].wait()
    for part in range(2):
        at = slice(part * rank, (part + 1) * rank)
        static_out[at, :depth] = top[0, part]
        static_out[at, depth:] = whole[:, part * width : (part + 1) * width]


def coupling_kernel(high, low, skeleton_in, mask_in, inverse_in, coupling_in, base_out, high_out, low_out,
                    skeleton, mask, inverse, coupling, sems):
    copies = [
        pltpu.make_async_copy(source, target, sems.at[k])
        for k, (source, target) in enumerate((
            (skeleton_in, skeleton), (mask_in, mask), (inverse_in, inverse), (coupling_in, coupling),
        ))
    ]
    for copy in copies:
        copy.start()
    for copy in copies:
        copy.wait()
    width = inverse.shape[2]
    sides = coupling.shape[1]
    rank = coupling.shape[3]
    depth = sides * rank
    field = (high[...], low[...])
    re = split(inverse[0, 0])
    im = split(inverse[0, 1])
    row_matrix = (rows_form(re[0], im[0]), rows_form(re[1], im[1]))
    column_matrix = (columns_form(re[0], im[0]), columns_form(re[1], im[1]))
    picker = one_hot(skeleton[...], width)
    zero = jnp.zeros_like(picker)
    picker2 = cat([cat([picker, zero], 1), cat([zero, picker], 1)], 0)
    z = split(dot3(field, row_matrix, NT))
    u = dot(z[0], picker2) + dot(z[1], picker2)
    near = []
    for side in range(sides):
        weight = mask[:, side : side + 1].astype(F32)
        near.append(cat([coupling[0, side, 0] * weight, coupling[0, side, 1] * weight], 1))
    near = split(cat(near, 0))
    base_out[:, : 2 * width] = dot3(z, column_matrix)
    base_out[:, 2 * width :] = u
    applied = split(dot3(near, column_matrix))
    for k, out in enumerate((high_out, low_out)):
        chosen = dot(near[k], picker2).astype(BF16)
        for matrix, at, part in ((applied[k], 0, width), (chosen, 2 * width, rank)):
            out[:depth, at : at + 2 * part] = matrix
            out[depth:, at : at + part] = -matrix[:, part:]
            out[depth:, at + part : at + 2 * part] = matrix[:, :part]


def join_kernel(base, left, u, right, two, four, row_out, pair_out):
    row_out[0] = left[...]
    row_out[1] = u[...]
    row_out[2] = right[...]
    pair_out[0] = two[...]
    pair_out[1] = four[...]


def message_kernel(up, middle, down, base, high, low, out):
    boxes = out.shape[0]
    count = base.shape[0]
    width = out.shape[2]
    rank = up.shape[1] // 2
    share = count // boxes
    half = share // 2
    order = (up[0], up[1], up[2], middle[0], middle[2], down[0], down[1], down[2])
    stacked = cat([v[:rank] for v in order] + [v[rank:] for v in order], 0)
    near = split(stacked.T)
    w = base[...] - dot3(near, (high[...], low[...]))
    for box in range(boxes):
        at = box * share
        out[box, :share] = w[at : at + share, :width]
        out[box, share : 2 * share] = w[at : at + share, width : 2 * width]
        t = w[at : at + share, 2 * width :]
        out[box, 2 * share : 2 * share + half] = cat([t[:half], t[half:]], 1)


def top_kernel(offsets, message, *refs):
    static_in, out = refs[:-1], refs[-1]
    boxes = message.shape[0]
    width = message.shape[2]
    share = out.shape[1]
    half = share // 2
    rank = static_in[0].shape[-2] // 2
    depth = boxes * rank
    me = lax.axis_index("box")
    t_re = []
    t_im = []
    for box in range(boxes):
        packed = message[box, 2 * share : 2 * share + half]
        t = cat([packed[:, : 2 * rank], packed[:, 2 * rank :]], 0)
        t_re.append(t[:, :rank])
        t_im.append(t[:, rank:])
    t = split(cat(t_re + t_im, 1))
    static = [block for v in static_in for block in ([v[k] for k in range(v.shape[0])] if len(v.shape) == 3 else [v[...]])]
    top = []
    for v in static:
        top.append(rows_form(v[:rank, :depth], v[rank:, :depth]))
    y = dot3(t, split(cat(top, 0)), NT)
    for k, v in enumerate(static):
        box = k if offsets is None else me ^ offsets[k]
        local = split(columns_form(v[:rank, depth:], v[rank:, depth:]))
        part = split(y[:, k * 2 * rank : (k + 1) * 2 * rank])
        x = dot3(part, local)
        at = pl.ds(pl.multiple_of(box * width, width), width)
        out[0, :, at] = message[box, :share] + x[:, :width]
        out[1, :, at] = message[box, share : 2 * share] + x[:, width:]


def call(kernel, outs, *arrays, hbm=(), copied=()):
    spaces = {i: pl.BlockSpec(memory_space=pl.ANY) for i in hbm}
    spaces.update({i: pl.BlockSpec(memory_space=pltpu.HBM) for i in copied})
    scratch = [pltpu.VMEM(arrays[i].shape, arrays[i].dtype) for i in copied]
    if scratch:
        scratch.append(pltpu.SemaphoreType.DMA((len(scratch),)))
    arrays = [pltpu.with_memory_space_constraint(v, pltpu.HBM) if i in copied else v for i, v in enumerate(arrays)]
    return pl.pallas_call(
        kernel,
        out_shape=[jax.ShapeDtypeStruct(shape, dtype) for shape, dtype in outs],
        in_specs=[spaces.get(i, VMEM) for i in range(len(arrays))],
        out_specs=[VMEM] * len(outs),
        scratch_shapes=scratch,
        compiler_params=pltpu.CompilerParams(vmem_limit_bytes=40 * 1024 * 1024),
    )(*arrays)


def shifted(value, axis, step):
    count = lax.axis_size(axis)
    return lax.ppermute(value, axis, [(i, (i + step) % count) for i in range(count)])


def swapped(value, axis, bit):
    return lax.ppermute(value, axis, [(i, i ^ bit) for i in range(lax.axis_size(axis))])


def on_device(surface_points, angle_ids, near_mask, skeleton, box_inverse_parts, near_coupling, top_inverse):
    boxes = lax.axis_size("box")
    width = box_inverse_parts.shape[2]
    count = angle_ids.shape[0]
    rank = skeleton.shape[1]
    sides = near_mask.shape[1]
    depth = top_inverse.shape[3]
    share = count // boxes
    arrays = (surface_points, angle_ids.reshape(1, count), skeleton, box_inverse_parts, top_inverse)
    u, static, high, low = call(
        field_kernel,
        [
            ((2 * rank, count), F32),
            ((2 * rank, depth + width), F32),
            ((count, 2 * width), BF16),
            ((count, 2 * width), BF16),
        ],
        *arrays,
        copied=range(len(arrays)),
    )
    base, matrix_high, matrix_low = call(
        coupling_kernel,
        [
            ((count, 2 * width + 2 * rank), F32),
            ((2 * sides * rank, 2 * width + 2 * rank), BF16),
            ((2 * sides * rank, 2 * width + 2 * rank), BF16),
        ],
        high, low, skeleton, near_mask, box_inverse_parts, near_coupling, copied=range(2, 6),
    )
    left = shifted(u, "box", 1)
    right = shifted(u, "box", -1)
    if boxes == 8:
        four = swapped(static, "box", 4)
        two = swapped(static, "box", 2)
        one = swapped(static, "box", 1)
        row, pair = call(
            join_kernel, [((3,) + u.shape, F32), ((2,) + static.shape, F32)],
            base, left, u, right, two, four, hbm=(0,),
        )
        static = (static, four, two, one, swapped(pair, "box", 1), swapped(four, "box", 2), swapped(four, "box", 3))
        offsets = (0, 4, 2, 1, 3, 5, 6, 7)
    else:
        row = jnp.stack([left, u, right])
        static = (lax.all_gather(static, "box"),)
        offsets = None
    up = shifted(row, "blk", 1)
    down = shifted(row, "blk", -1)
    rows = 2 * share + -(-share // 16) * 8
    (message,) = call(
        message_kernel, [((boxes, rows, width), F32)],
        up, row, down, base, matrix_high, matrix_low,
    )
    message = lax.all_to_all(message, "box", split_axis=0, concat_axis=0, tiled=True)
    (out,) = call(
        functools.partial(top_kernel, offsets), [((2, share, boxes * width), F32)], message, *static
    )
    return out


def solution(mesh):
    return jax.shard_map(
        on_device,
        mesh=mesh,
        in_specs=(
            P(None, ("blk", "box")),
            P("batch"),
            P(("blk", "box"), None),
            P(("blk", "box"), None),
            P(("blk", "box"), None, None, None),
            P(("blk", "box"), None, None, None, None),
            P("blk", None, "box", None),
        ),
        out_specs=P(None, ("batch", "box"), "blk"),
        check_vma=False,
    )
```

```python
import functools

import jax
import jax.numpy as jnp
import numpy as np
from jax import lax
from jax.experimental import pallas as pl
from jax.experimental.pallas import tpu as pltpu
from jax.sharding import PartitionSpec as P

SWEEP = 16384
WAVENUMBER = 24.0
F32 = jnp.float32
BF16 = jnp.bfloat16
VMEM = pl.BlockSpec(memory_space=pltpu.VMEM)
NN = (((1,), (0,)), ((), ()))
NT = (((1,), (1,)), ((), ()))
TN = (((0,), (0,)), ((), ()))

HALF_PI_1 = float(np.float32(201.0 / 128.0))
HALF_PI_2 = float(np.float32(np.round((np.pi / 2 - HALF_PI_1) * 2.0**22) / 2.0**22))
HALF_PI_3 = float(np.float32(np.pi / 2 - HALF_PI_1 - HALF_PI_2))


def cat(parts, axis):
    return jnp.concatenate(parts, axis=axis)


def dot(a, b, form=NN):
    return lax.dot_general(a, b, form, preferred_element_type=F32)


def split(x):
    high = x.astype(BF16)
    return high, (x - high.astype(F32)).astype(BF16)


def dot3(a, b, form=NN):
    return dot(a[0], b[0], form) + (dot(a[0], b[1], form) + dot(a[1], b[0], form))


def both(pair, function):
    return function(pair[0]), function(pair[1])


def sin_cos_small(r):
    s = r * r
    sin = r + r * s * (-1.6666654611e-1 + s * (8.3321608736e-3 - s * 1.9515295891e-4))
    cos = 1.0 - 0.5 * s + s * s * (4.166664568298827e-2 + s * (-1.388731625493765e-3 + s * 2.443315711809948e-5))
    return sin, cos


def by_quadrant(quadrant, sin, cos):
    odd = (quadrant & 1) == 1
    out_sin = jnp.where(odd, cos, sin)
    out_cos = jnp.where(odd, sin, cos)
    out_sin = jnp.where((quadrant & 2) == 2, -out_sin, out_sin)
    out_cos = jnp.where(((quadrant + 1) & 2) == 2, -out_cos, out_cos)
    return out_sin, out_cos


def one_hot(skeleton, width):
    rows = lax.broadcasted_iota(jnp.int32, (width, skeleton.shape[1]), 0)
    return jnp.where(rows == skeleton, 1.0, 0.0).astype(BF16)


def rows_form(re, im):
    return cat([cat([re, -im], 1), cat([im, re], 1)], 0)


def columns_form(re, im):
    return cat([cat([re, im], 1), cat([-im, re], 1)], 0)


def field_kernel(points_in, angles_in, skeleton_in, inverse_in, top_in, u_out, static_out, high_out, low_out,
                 points, angles, skeleton, inverse, top, sems):
    copies = [
        pltpu.make_async_copy(source, target, sems.at[k])
        for k, (source, target) in enumerate((
            (angles_in, angles), (points_in, points), (skeleton_in, skeleton), (inverse_in, inverse), (top_in, top),
        ))
    ]
    for copy in copies:
        copy.start()
    count = angles.shape[1]
    width = points.shape[1]
    rank = skeleton.shape[1]
    copies[0].wait()
    ids = angles[...]
    quadrant = (ids + SWEEP // 8) >> (SWEEP.bit_length() - 3)
    rest = ids - quadrant * (SWEEP // 4)
    sin, cos = by_quadrant(quadrant, *sin_cos_small(rest.astype(F32) * (2.0 * np.pi / SWEEP)))
    pick = lax.broadcasted_iota(jnp.int32, (8, count), 0) == 0
    columns = jnp.where(pick, cos, sin).T
    cos_column = columns[:, 0:1]
    sin_column = columns[:, 1:2]
    copies[1].wait()
    x = points[0:1, :] * WAVENUMBER
    yz = points[1:2, :] * (0.6 * WAVENUMBER) + points[2:3, :] * (0.8 * WAVENUMBER)
    phase = x * cos_column + yz * sin_column
    turns = jnp.round(phase * (2.0 / np.pi))
    r = ((phase - turns * HALF_PI_1) - turns * HALF_PI_2) - turns * HALF_PI_3
    field_sin, field_cos = by_quadrant(turns.astype(jnp.int32), *sin_cos_small(r))
    field = split(cat([field_cos, field_sin], 1))
    high_out[...] = field[0]
    low_out[...] = field[1]
    copies[2].wait()
    picker = one_hot(skeleton[...], width)
    copies[3].wait()
    parts = split(cat([inverse[0, 0], inverse[0, 1]], 1))
    rows = dot(picker, cat(parts, 1), TN)
    rows_high = rows[:, : 2 * width]
    rows_low = rows[:, 2 * width :]
    whole = rows_high + rows_low
    form = both((rows_high, rows_low), lambda v: rows_form(v[:, :width], v[:, width:]).astype(BF16))
    u_out[...] = dot3(form, field, NT)
    depth = top.shape[3]
    copies[4].wait()
    for part in range(2):
        at = slice(part * rank, (part + 1) * rank)
        static_out[at, :depth] = top[0, part]
        static_out[at, depth:] = whole[:, part * width : (part + 1) * width]


def coupling_kernel(high, low, skeleton_in, mask_in, inverse_in, coupling_in, base_out, high_out, low_out,
                    skeleton, mask, inverse, coupling, sems):
    copies = [
        pltpu.make_async_copy(source, target, sems.at[k])
        for k, (source, target) in enumerate((
            (skeleton_in, skeleton), (mask_in, mask), (inverse_in, inverse), (coupling_in, coupling),
        ))
    ]
    for copy in copies:
        copy.start()
    for copy in copies:
        copy.wait()
    width = inverse.shape[2]
    sides = coupling.shape[1]
    rank = coupling.shape[3]
    depth = sides * rank
    field = (high[...], low[...])
    re = split(inverse[0, 0])
    im = split(inverse[0, 1])
    row_matrix = (rows_form(re[0], im[0]), rows_form(re[1], im[1]))
    column_matrix = (columns_form(re[0], im[0]), columns_form(re[1], im[1]))
    picker = one_hot(skeleton[...], width)
    zero = jnp.zeros_like(picker)
    picker2 = cat([cat([picker, zero], 1), cat([zero, picker], 1)], 0)
    z = split(dot3(field, row_matrix, NT))
    u = dot(z[0], picker2) + dot(z[1], picker2)
    near = []
    for side in range(sides):
        weight = mask[:, side : side + 1].astype(F32)
        near.append(cat([coupling[0, side, 0] * weight, coupling[0, side, 1] * weight], 1))
    near = split(cat(near, 0))
    base_out[:, : 2 * width] = dot3(z, column_matrix)
    base_out[:, 2 * width :] = u
    applied = split(dot3(near, column_matrix))
    for k, out in enumerate((high_out, low_out)):
        chosen = dot(near[k], picker2).astype(BF16)
        for matrix, at, part in ((applied[k], 0, width), (chosen, 2 * width, rank)):
            out[:depth, at : at + 2 * part] = matrix
            out[depth:, at : at + part] = -matrix[:, part:]
            out[depth:, at + part : at + 2 * part] = matrix[:, :part]


def join_kernel(base, even, odd, u, mine, came, row_out, pair_out):
    first = lax.axis_index("box") % 2 == 0
    row_out[0] = jnp.where(first, odd[...], even[...])
    row_out[1] = u[...]
    row_out[2] = jnp.where(first, even[...], odd[...])
    pair_out[0] = mine[...]
    pair_out[1] = came[...]


def message_kernel(even, middle, odd, base, high, low, out):
    first = lax.axis_index("blk") % 2 == 0
    up = jnp.where(first, odd[...], even[...])
    down = jnp.where(first, even[...], odd[...])
    boxes = out.shape[0]
    count = base.shape[0]
    width = out.shape[2]
    rank = up.shape[1] // 2
    share = count // boxes
    half = share // 2
    order = (up[0], up[1], up[2], middle[0], middle[2], down[0], down[1], down[2])
    stacked = cat([v[:rank] for v in order] + [v[rank:] for v in order], 0)
    near = split(stacked.T)
    w = base[...] - dot3(near, (high[...], low[...]))
    for box in range(boxes):
        at = box * share
        out[box, :share] = w[at : at + share, :width]
        out[box, share : 2 * share] = w[at : at + share, width : 2 * width]
        t = w[at : at + share, 2 * width :]
        out[box, 2 * share : 2 * share + half] = cat([t[:half], t[half:]], 1)


def blocks_of(refs):
    return [block for v in refs for block in ([v[k] for k in range(v.shape[0])] if len(v.shape) == 3 else [v[...]])]


def prepare_kernel(*refs):
    top_high, top_low, local_high, local_low = refs[-4:]
    rows = local_high.shape[1]
    rank = rows // 2
    depth = top_high.shape[1] // 2
    for k, block in enumerate(blocks_of(refs[:-4])):
        at = slice(k * rows, (k + 1) * rows)
        for part, top_out, local_out in zip(split(block), (top_high, top_low), (local_high, local_low)):
            top_out[at] = rows_form(part[:rank, :depth], part[rank:, :depth])
            local_out[k] = columns_form(part[:rank, depth:], part[rank:, depth:])


def top_kernel(offsets, message, top_high, top_low, local_high, local_low, *refs):
    out = refs[-1]
    boxes = message.shape[0]
    width = message.shape[2]
    share = out.shape[1]
    half = share // 2
    ready, rows = local_high.shape[:2]
    rank = rows // 2
    depth = boxes * rank
    me = lax.axis_index("box")
    top = [(top_high[...], top_low[...])]
    local = [(local_high[k], local_low[k]) for k in range(ready)]
    late = [split(block) for block in blocks_of(refs[:-1])]
    if late:
        top.append([
            cat([rows_form(v[k][:rank, :depth], v[k][rank:, :depth]) for v in late], 0) for k in range(2)
        ])
        local += [both(v, lambda part: columns_form(part[:rank, depth:], part[rank:, depth:])) for v in late]
    t_re = []
    t_im = []
    for box in range(boxes):
        packed = message[box, 2 * share : 2 * share + half]
        t = cat([packed[:, : 2 * rank], packed[:, 2 * rank :]], 0)
        t_re.append(t[:, :rank])
        t_im.append(t[:, rank:])
    t = split(cat(t_re + t_im, 1))
    t_both = cat(t, 0)
    y = []
    for high, low in top:
        first = dot(t_both, high, NT)
        y.append(first[:share] + (first[share:] + dot(t[0], low, NT)))
    y = split(cat(y, 1))
    for k in range(boxes):
        box = k if offsets is None else me ^ offsets[k]
        part = [v[:, k * rows : (k + 1) * rows] for v in y]
        x = dot3(part, local[k])
        at = pl.ds(pl.multiple_of(box * width, width), width)
        out[0, :, at] = message[box, :share] + x[:, :width]
        out[1, :, at] = message[box, share : 2 * share] + x[:, width:]


def call(kernel, outs, *arrays, hbm=(), copied=()):
    spaces = {i: pl.BlockSpec(memory_space=pl.ANY) for i in hbm}
    spaces.update({i: pl.BlockSpec(memory_space=pltpu.HBM) for i in copied})
    scratch = [pltpu.VMEM(arrays[i].shape, arrays[i].dtype) for i in copied]
    if scratch:
        scratch.append(pltpu.SemaphoreType.DMA((len(scratch),)))
    arrays = [pltpu.with_memory_space_constraint(v, pltpu.HBM) if i in copied else v for i, v in enumerate(arrays)]
    return pl.pallas_call(
        kernel,
        out_shape=[jax.ShapeDtypeStruct(shape, dtype) for shape, dtype in outs],
        in_specs=[spaces.get(i, VMEM) for i in range(len(arrays))],
        out_specs=[VMEM] * len(outs),
        scratch_shapes=scratch,
        compiler_params=pltpu.CompilerParams(vmem_limit_bytes=40 * 1024 * 1024),
    )(*arrays)


def swapped(value, axis, bit):
    return lax.ppermute(value, axis, [(i, i ^ bit) for i in range(lax.axis_size(axis))])


def beside(value, axis):
    count = lax.axis_size(axis)
    even = lax.ppermute(value, axis, [(i, i ^ 1) for i in range(count)])
    odd = lax.ppermute(value, axis, [(i, (i + 1) % count if i % 2 else (i - 1) % count) for i in range(count)])
    return even, odd


def on_device(surface_points, angle_ids, near_mask, skeleton, box_inverse_parts, near_coupling, top_inverse):
    boxes = lax.axis_size("box")
    width = box_inverse_parts.shape[2]
    count = angle_ids.shape[0]
    rank = skeleton.shape[1]
    sides = near_mask.shape[1]
    depth = top_inverse.shape[3]
    share = count // boxes
    u, static, high, low = call(
        field_kernel,
        [
            ((2 * rank, count), F32),
            ((2 * rank, depth + width), F32),
            ((count, 2 * width), BF16),
            ((count, 2 * width), BF16),
        ],
        surface_points, angle_ids.reshape(1, count), skeleton, box_inverse_parts, top_inverse,
        copied=range(5),
    )
    base, matrix_high, matrix_low = call(
        coupling_kernel,
        [
            ((count, 2 * width + 2 * rank), F32),
            ((2 * sides * rank, 2 * width + 2 * rank), BF16),
            ((2 * sides * rank, 2 * width + 2 * rank), BF16),
        ],
        high, low, skeleton, near_mask, box_inverse_parts, near_coupling,
        copied=range(2, 6),
    )
    even, odd = beside(u, "box")
    four = swapped(static, "box", boxes // 2)
    row, pair = call(
        join_kernel, [((3,) + u.shape, F32), ((2,) + static.shape, F32)], base, even, odd, u, static, four, hbm=(0,)
    )
    if boxes == 8:
        two = swapped(pair, "box", 2)
        one = swapped(pair, "box", 1)
        early = [pair, two, one]
        late = [swapped(one[:1], "box", 2), swapped(two[1:], "box", 1)]
        offsets = (0, 4, 2, 6, 1, 5, 3, 7)
    else:
        early = [lax.all_gather(static, "box")]
        late = []
        offsets = None
    even, odd = beside(row, "blk")
    length = 2 * share + -(-share // 16) * 8
    (message,) = call(
        message_kernel, [((boxes, length, width), F32)],
        even, row, odd, base, matrix_high, matrix_low,
    )
    message = lax.all_to_all(message, "box", split_axis=0, concat_axis=0, tiled=True)
    ready = boxes - len(late)
    top = ((ready * 2 * rank, 2 * depth), BF16)
    local = ((ready, 2 * rank, 2 * width), BF16)
    prepared = call(prepare_kernel, [top, top, local, local], *early)
    (out,) = call(
        functools.partial(top_kernel, offsets), [((2, share, boxes * width), F32)], message, *prepared, *late
    )
    return out


def solution(mesh):
    return jax.shard_map(
        on_device,
        mesh=mesh,
        in_specs=(
            P(None, ("blk", "box")),
            P("batch"),
            P(("blk", "box"), None),
            P(("blk", "box"), None),
            P(("blk", "box"), None, None, None),
            P(("blk", "box"), None, None, None, None),
            P("blk", None, "box", None),
        ),
        out_specs=P(None, ("batch", "box"), "blk"),
        check_vma=False,
    )
```

```python
import functools

import jax
import jax.numpy as jnp
import numpy as np
from jax import lax
from jax.experimental import pallas as pl
from jax.experimental.pallas import tpu as pltpu
from jax.sharding import PartitionSpec as P

SWEEP = 16384
WAVENUMBER = 24.0
F32 = jnp.float32
BF16 = jnp.bfloat16
VMEM = pl.BlockSpec(memory_space=pltpu.VMEM)
NN = (((1,), (0,)), ((), ()))
NT = (((1,), (1,)), ((), ()))
TN = (((0,), (0,)), ((), ()))

HALF_PI_1 = float(np.float32(201.0 / 128.0))
HALF_PI_2 = float(np.float32(np.round((np.pi / 2 - HALF_PI_1) * 2.0**22) / 2.0**22))
HALF_PI_3 = float(np.float32(np.pi / 2 - HALF_PI_1 - HALF_PI_2))


def cat(parts, axis):
    return jnp.concatenate(parts, axis=axis)


def dot(a, b, form=NN):
    return lax.dot_general(a, b, form, preferred_element_type=F32)


def split(x):
    high = x.astype(BF16)
    return high, (x - high.astype(F32)).astype(BF16)


def dot3(a, b, form=NN):
    return dot(a[0], b[0], form) + (dot(a[0], b[1], form) + dot(a[1], b[0], form))


def both(pair, function):
    return function(pair[0]), function(pair[1])


def sin_cos_small(r):
    s = r * r
    sin = r + r * s * (-1.6666654611e-1 + s * (8.3321608736e-3 - s * 1.9515295891e-4))
    cos = 1.0 - 0.5 * s + s * s * (4.166664568298827e-2 + s * (-1.388731625493765e-3 + s * 2.443315711809948e-5))
    return sin, cos


def by_quadrant(quadrant, sin, cos):
    odd = (quadrant & 1) == 1
    out_sin = jnp.where(odd, cos, sin)
    out_cos = jnp.where(odd, sin, cos)
    out_sin = jnp.where((quadrant & 2) == 2, -out_sin, out_sin)
    out_cos = jnp.where(((quadrant + 1) & 2) == 2, -out_cos, out_cos)
    return out_sin, out_cos


def one_hot(skeleton, width):
    rows = lax.broadcasted_iota(jnp.int32, (width, skeleton.shape[1]), 0)
    return jnp.where(rows == skeleton, 1.0, 0.0).astype(BF16)


def rows_form(re, im):
    return cat([cat([re, -im], 1), cat([im, re], 1)], 0)


def columns_form(re, im):
    return cat([cat([re, im], 1), cat([-im, re], 1)], 0)


def field_kernel(points_in, angles_in, skeleton_in, inverse_in, top_in, u_out, static_out, high_out, low_out,
                 points, angles, skeleton, inverse, top, sems):
    copies = [
        pltpu.make_async_copy(source, target, sems.at[k])
        for k, (source, target) in enumerate((
            (angles_in, angles), (points_in, points), (skeleton_in, skeleton), (inverse_in, inverse), (top_in, top),
        ))
    ]
    for copy in copies:
        copy.start()
    count = angles.shape[1]
    width = points.shape[1]
    rank = skeleton.shape[1]
    copies[0].wait()
    ids = angles[...]
    quadrant = (ids + SWEEP // 8) >> (SWEEP.bit_length() - 3)
    rest = ids - quadrant * (SWEEP // 4)
    sin, cos = by_quadrant(quadrant, *sin_cos_small(rest.astype(F32) * (2.0 * np.pi / SWEEP)))
    pick = lax.broadcasted_iota(jnp.int32, (8, count), 0) == 0
    columns = jnp.where(pick, cos, sin).T
    cos_column = columns[:, 0:1]
    sin_column = columns[:, 1:2]
    copies[1].wait()
    x = points[0:1, :] * WAVENUMBER
    yz = points[1:2, :] * (0.6 * WAVENUMBER) + points[2:3, :] * (0.8 * WAVENUMBER)
    phase = x * cos_column + yz * sin_column
    turns = jnp.round(phase * (2.0 / np.pi))
    r = ((phase - turns * HALF_PI_1) - turns * HALF_PI_2) - turns * HALF_PI_3
    field_sin, field_cos = by_quadrant(turns.astype(jnp.int32), *sin_cos_small(r))
    field = split(cat([field_cos, field_sin], 1))
    high_out[...] = field[0]
    low_out[...] = field[1]
    copies[2].wait()
    picker = one_hot(skeleton[...], width)
    copies[3].wait()
    parts = split(cat([inverse[0, 0], inverse[0, 1]], 1))
    rows = dot(picker, cat(parts, 1), TN)
    rows_high = rows[:, : 2 * width]
    rows_low = rows[:, 2 * width :]
    whole = rows_high + rows_low
    form = both((rows_high, rows_low), lambda v: rows_form(v[:, :width], v[:, width:]).astype(BF16))
    u_out[...] = dot3(form, field, NT)
    depth = top.shape[3]
    copies[4].wait()
    for part in range(2):
        at = slice(part * rank, (part + 1) * rank)
        static_out[at, :depth] = top[0, part]
        static_out[at, depth:] = whole[:, part * width : (part + 1) * width]


def coupling_kernel(high, low, skeleton_in, mask_in, inverse_in, coupling_in, base_out, high_out, low_out,
                    skeleton, mask, inverse, coupling, sems):
    copies = [
        pltpu.make_async_copy(source, target, sems.at[k])
        for k, (source, target) in enumerate((
            (skeleton_in, skeleton), (mask_in, mask), (inverse_in, inverse), (coupling_in, coupling),
        ))
    ]
    for copy in copies:
        copy.start()
    for copy in copies:
        copy.wait()
    width = inverse.shape[2]
    sides = coupling.shape[1]
    rank = coupling.shape[3]
    depth = sides * rank
    field = (high[...], low[...])
    re = split(inverse[0, 0])
    im = split(inverse[0, 1])
    row_matrix = (rows_form(re[0], im[0]), rows_form(re[1], im[1]))
    column_matrix = (columns_form(re[0], im[0]), columns_form(re[1], im[1]))
    picker = one_hot(skeleton[...], width)
    zero = jnp.zeros_like(picker)
    picker2 = cat([cat([picker, zero], 1), cat([zero, picker], 1)], 0)
    z = split(dot3(field, row_matrix, NT))
    u = dot(z[0], picker2) + dot(z[1], picker2)
    near = []
    for side in range(sides):
        weight = mask[:, side : side + 1].astype(F32)
        near.append(cat([coupling[0, side, 0] * weight, coupling[0, side, 1] * weight], 1))
    near = split(cat(near, 0))
    base_out[:, : 2 * width] = dot3(z, column_matrix)
    base_out[:, 2 * width :] = u
    applied = split(dot3(near, column_matrix))
    for k, out in enumerate((high_out, low_out)):
        chosen = dot(near[k], picker2).astype(BF16)
        for matrix, at, part in ((applied[k], 0, width), (chosen, 2 * width, rank)):
            out[:depth, at : at + 2 * part] = matrix
            out[depth:, at : at + part] = -matrix[:, part:]
            out[depth:, at + part : at + 2 * part] = matrix[:, :part]


def join_kernel(base, even, odd, u, mine, came, row_out, pair_out):
    first = lax.axis_index("box") % 2 == 0
    row_out[0] = jnp.where(first, odd[...], even[...])
    row_out[1] = u[...]
    row_out[2] = jnp.where(first, even[...], odd[...])
    pair_out[0] = mine[...]
    pair_out[1] = came[...]


def stack_kernel(even, odd, first, second, out):
    count = first.shape[0]
    out[:count] = first[...]
    out[count:] = second[...]


def message_kernel(even, middle, odd, base, high, low, out):
    first = lax.axis_index("blk") % 2 == 0
    up = jnp.where(first, odd[...], even[...])
    down = jnp.where(first, even[...], odd[...])
    boxes = out.shape[0]
    count = base.shape[0]
    width = out.shape[2]
    rank = up.shape[1] // 2
    share = count // boxes
    half = share // 2
    order = (up[0], up[1], up[2], middle[0], middle[2], down[0], down[1], down[2])
    stacked = cat([v[:rank] for v in order] + [v[rank:] for v in order], 0)
    near = split(stacked.T)
    w = base[...] - dot3(near, (high[...], low[...]))
    for box in range(boxes):
        at = box * share
        out[box, :share] = w[at : at + share, :width]
        out[box, share : 2 * share] = w[at : at + share, width : 2 * width]
        t = w[at : at + share, 2 * width :]
        out[box, 2 * share : 2 * share + half] = cat([t[:half], t[half:]], 1)


def blocks_of(refs):
    return [block for v in refs for block in ([v[k] for k in range(v.shape[0])] if len(v.shape) == 3 else [v[...]])]


def prepare_kernel(*refs):
    top_high, top_low, local_high, local_low = refs[-4:]
    rows = local_high.shape[1]
    rank = rows // 2
    depth = top_high.shape[1] // 2
    for k, block in enumerate(blocks_of(refs[:-4])):
        at = slice(k * rows, (k + 1) * rows)
        for part, top_out, local_out in zip(split(block), (top_high, top_low), (local_high, local_low)):
            top_out[at] = rows_form(part[:rank, :depth], part[rank:, :depth])
            local_out[k] = columns_form(part[:rank, depth:], part[rank:, depth:])


def top_kernel(offsets, message, top_high, top_low, local_high, local_low, *refs):
    out_hbm, out, sems = refs[-3:]
    boxes = message.shape[0]
    width = message.shape[2]
    share = out.shape[1]
    half = share // 2
    ready, rows = local_high.shape[:2]
    rank = rows // 2
    depth = boxes * rank
    me = lax.axis_index("box")
    top = [(top_high[...], top_low[...])]
    local = [(local_high[k], local_low[k]) for k in range(ready)]
    late = [split(block) for block in blocks_of(refs[:-3])]
    if late:
        top.append([
            cat([rows_form(v[k][:rank, :depth], v[k][rank:, :depth]) for v in late], 0) for k in range(2)
        ])
        local += [both(v, lambda part: columns_form(part[:rank, depth:], part[rank:, depth:])) for v in late]
    t_re = []
    t_im = []
    for box in range(boxes):
        packed = message[box, 2 * share : 2 * share + half]
        t = cat([packed[:, : 2 * rank], packed[:, 2 * rank :]], 0)
        t_re.append(t[:, :rank])
        t_im.append(t[:, rank:])
    t = split(cat(t_re + t_im, 1))
    t_both = cat(t, 0)
    y = []
    for high, low in top:
        first = dot(t_both, high, NT)
        y.append(first[:share] + (first[share:] + dot(t[0], low, NT)))
    y = split(cat(y, 1))
    copies = []
    for k in range(boxes):
        box = k if offsets is None else me ^ offsets[k]
        part = [v[:, k * rows : (k + 1) * rows] for v in y]
        x = dot3(part, local[k])
        at = pl.ds(pl.multiple_of(box * width, width), width)
        out[0, :, at] = message[box, :share] + x[:, :width]
        out[1, :, at] = message[box, share : 2 * share] + x[:, width:]
        copies.append(pltpu.make_async_copy(out.at[:, :, at], out_hbm.at[:, :, at], sems.at[k]))
        copies[k].start()
    for copy in copies:
        copy.wait()


def call(kernel, outs, *arrays, hbm=(), copied=()):
    spaces = {i: pl.BlockSpec(memory_space=pl.ANY) for i in hbm}
    spaces.update({i: pl.BlockSpec(memory_space=pltpu.HBM) for i in copied})
    scratch = [pltpu.VMEM(arrays[i].shape, arrays[i].dtype) for i in copied]
    if scratch:
        scratch.append(pltpu.SemaphoreType.DMA((len(scratch),)))
    arrays = [pltpu.with_memory_space_constraint(v, pltpu.HBM) if i in copied else v for i, v in enumerate(arrays)]
    return pl.pallas_call(
        kernel,
        out_shape=[jax.ShapeDtypeStruct(shape, dtype) for shape, dtype in outs],
        in_specs=[spaces.get(i, VMEM) for i in range(len(arrays))],
        out_specs=[VMEM] * len(outs),
        scratch_shapes=scratch,
        compiler_params=pltpu.CompilerParams(vmem_limit_bytes=40 * 1024 * 1024),
    )(*arrays)


def swapped(value, axis, bit):
    return lax.ppermute(value, axis, [(i, i ^ bit) for i in range(lax.axis_size(axis))])


def beside(value, axis):
    count = lax.axis_size(axis)
    even = lax.ppermute(value, axis, [(i, i ^ 1) for i in range(count)])
    odd = lax.ppermute(value, axis, [(i, (i + 1) % count if i % 2 else (i - 1) % count) for i in range(count)])
    return even, odd


def on_device(surface_points, angle_ids, near_mask, skeleton, box_inverse_parts, near_coupling, top_inverse):
    boxes = lax.axis_size("box")
    width = box_inverse_parts.shape[2]
    count = angle_ids.shape[0]
    rank = skeleton.shape[1]
    sides = near_mask.shape[1]
    depth = top_inverse.shape[3]
    share = count // boxes
    u, static, high, low = call(
        field_kernel,
        [
            ((2 * rank, count), F32),
            ((2 * rank, depth + width), F32),
            ((count, 2 * width), BF16),
            ((count, 2 * width), BF16),
        ],
        surface_points, angle_ids.reshape(1, count), skeleton, box_inverse_parts, top_inverse,
        copied=range(5),
    )
    base, matrix_high, matrix_low = call(
        coupling_kernel,
        [
            ((count, 2 * width + 2 * rank), F32),
            ((2 * sides * rank, 2 * width + 2 * rank), BF16),
            ((2 * sides * rank, 2 * width + 2 * rank), BF16),
        ],
        high, low, skeleton, near_mask, box_inverse_parts, near_coupling,
        copied=range(2, 6),
    )
    even, odd = beside(u, "box")
    step = boxes // 2
    came = swapped(static, "box", step)
    row, blocks = call(
        join_kernel, [((3,) + u.shape, F32), ((2,) + static.shape, F32)], base, even, odd, u, static, came, hbm=(0,)
    )
    even, odd = beside(row, "blk")
    if boxes & (boxes - 1) == 0:
        offsets = [0, step]
        while step > 1:
            step //= 2
            came = swapped(blocks, "box", step)
            if step > 1:
                shape = (2 * len(offsets),) + static.shape
                (blocks,) = call(stack_kernel, [(shape, F32)], even, odd, blocks, came, hbm=(0, 1))
            offsets += [k ^ step for k in offsets]
        early, late = [blocks, came], []
    else:
        early, late = [lax.all_gather(static, "box")], []
        offsets = None
    length = 2 * share + -(-share // 16) * 8
    (message,) = call(
        message_kernel, [((boxes, length, width), F32)],
        even, row, odd, base, matrix_high, matrix_low,
    )
    message = lax.all_to_all(message, "box", split_axis=0, concat_axis=0, tiled=True)
    ready = boxes - len(late)
    top = ((ready * 2 * rank, 2 * depth), BF16)
    local = ((ready, 2 * rank, 2 * width), BF16)
    prepared = call(prepare_kernel, [top, top, local, local], *early)
    arrays = (message, *prepared, *late)
    shape = (2, share, boxes * width)
    return pl.pallas_call(
        functools.partial(top_kernel, offsets),
        out_shape=jax.ShapeDtypeStruct(shape, F32),
        in_specs=[VMEM] * len(arrays),
        out_specs=pl.BlockSpec(memory_space=pltpu.HBM),
        scratch_shapes=[pltpu.VMEM(shape, F32), pltpu.SemaphoreType.DMA((boxes,))],
        compiler_params=pltpu.CompilerParams(vmem_limit_bytes=40 * 1024 * 1024),
    )(*arrays)


def solution(mesh):
    return jax.shard_map(
        on_device,
        mesh=mesh,
        in_specs=(
            P(None, ("blk", "box")),
            P("batch"),
            P(("blk", "box"), None),
            P(("blk", "box"), None),
            P(("blk", "box"), None, None, None),
            P(("blk", "box"), None, None, None, None),
            P("blk", None, "box", None),
        ),
        out_specs=P(None, ("batch", "box"), "blk"),
        check_vma=False,
    )
```

```python
import functools

import jax
import jax.numpy as jnp
import numpy as np
from jax import lax
from jax.experimental import pallas as pl
from jax.experimental.pallas import tpu as pltpu
from jax.sharding import PartitionSpec as P

SWEEP = 16384
WAVENUMBER = 24.0
F32 = jnp.float32
BF16 = jnp.bfloat16
VMEM = pl.BlockSpec(memory_space=pltpu.VMEM)
NN = (((1,), (0,)), ((), ()))
NT = (((1,), (1,)), ((), ()))
TN = (((0,), (0,)), ((), ()))

HALF_PI_1 = float(np.float32(201.0 / 128.0))
HALF_PI_2 = float(np.float32(np.round((np.pi / 2 - HALF_PI_1) * 2.0**22) / 2.0**22))
HALF_PI_3 = float(np.float32(np.pi / 2 - HALF_PI_1 - HALF_PI_2))


def cat(parts, axis):
    return jnp.concatenate(parts, axis=axis)


def dot(a, b, form=NN):
    return lax.dot_general(a, b, form, preferred_element_type=F32)


def split(x):
    high = x.astype(BF16)
    return high, (x - high.astype(F32)).astype(BF16)


def dot3(a, b, form=NN):
    return dot(a[0], b[0], form) + (dot(a[0], b[1], form) + dot(a[1], b[0], form))


def both(pair, function):
    return function(pair[0]), function(pair[1])


def sin_cos_small(r):
    s = r * r
    sin = r + r * s * (-1.6666654611e-1 + s * (8.3321608736e-3 - s * 1.9515295891e-4))
    cos = 1.0 - 0.5 * s + s * s * (4.166664568298827e-2 + s * (-1.388731625493765e-3 + s * 2.443315711809948e-5))
    return sin, cos


def by_quadrant(quadrant, sin, cos):
    odd = (quadrant & 1) == 1
    out_sin = jnp.where(odd, cos, sin)
    out_cos = jnp.where(odd, sin, cos)
    out_sin = jnp.where((quadrant & 2) == 2, -out_sin, out_sin)
    out_cos = jnp.where(((quadrant + 1) & 2) == 2, -out_cos, out_cos)
    return out_sin, out_cos


def one_hot(skeleton, width):
    rows = lax.broadcasted_iota(jnp.int32, (width, skeleton.shape[1]), 0)
    return jnp.where(rows == skeleton, 1.0, 0.0).astype(BF16)


def rows_form(re, im):
    return cat([cat([re, -im], 1), cat([im, re], 1)], 0)


def columns_form(re, im):
    return cat([cat([re, im], 1), cat([-im, re], 1)], 0)


def field_kernel(points_in, angles_in, skeleton_in, inverse_in, top_in, u_out, static_out, high_out, low_out,
                 points, angles, skeleton, inverse, top, sems):
    copies = [
        pltpu.make_async_copy(source, target, sems.at[k])
        for k, (source, target) in enumerate((
            (angles_in, angles), (points_in, points), (skeleton_in, skeleton), (inverse_in, inverse), (top_in, top),
        ))
    ]
    for copy in copies:
        copy.start()
    count = angles.shape[1]
    width = points.shape[1]
    rank = skeleton.shape[1]
    copies[0].wait()
    ids = angles[...]
    quadrant = (ids + SWEEP // 8) >> (SWEEP.bit_length() - 3)
    rest = ids - quadrant * (SWEEP // 4)
    sin, cos = by_quadrant(quadrant, *sin_cos_small(rest.astype(F32) * (2.0 * np.pi / SWEEP)))
    pick = lax.broadcasted_iota(jnp.int32, (8, count), 0) == 0
    columns = jnp.where(pick, cos, sin).T
    cos_column = columns[:, 0:1]
    sin_column = columns[:, 1:2]
    copies[1].wait()
    x = points[0:1, :] * WAVENUMBER
    yz = points[1:2, :] * (0.6 * WAVENUMBER) + points[2:3, :] * (0.8 * WAVENUMBER)
    phase = x * cos_column + yz * sin_column
    turns = jnp.round(phase * (2.0 / np.pi))
    r = ((phase - turns * HALF_PI_1) - turns * HALF_PI_2) - turns * HALF_PI_3
    field_sin, field_cos = by_quadrant(turns.astype(jnp.int32), *sin_cos_small(r))
    field = split(cat([field_cos, field_sin], 1))
    high_out[...] = field[0]
    low_out[...] = field[1]
    copies[2].wait()
    picker = one_hot(skeleton[...], width)
    copies[3].wait()
    parts = split(cat([inverse[0, 0], inverse[0, 1]], 1))
    rows = dot(picker, cat(parts, 1), TN)
    rows_high = rows[:, : 2 * width]
    rows_low = rows[:, 2 * width :]
    whole = rows_high + rows_low
    form = both((rows_high, rows_low), lambda v: rows_form(v[:, :width], v[:, width:]).astype(BF16))
    u_out[...] = dot3(form, field, NT)
    depth = top.shape[3]
    copies[4].wait()
    for part in range(2):
        at = slice(part * rank, (part + 1) * rank)
        static_out[at, :depth] = top[0, part]
        static_out[at, depth:] = whole[:, part * width : (part + 1) * width]


def coupling_kernel(high, low, skeleton_in, mask_in, inverse_in, coupling_in, base_out, high_out, low_out,
                    skeleton, mask, inverse, coupling, sems):
    copies = [
        pltpu.make_async_copy(source, target, sems.at[k])
        for k, (source, target) in enumerate((
            (skeleton_in, skeleton), (mask_in, mask), (inverse_in, inverse), (coupling_in, coupling),
        ))
    ]
    for copy in copies:
        copy.start()
    for copy in copies:
        copy.wait()
    width = inverse.shape[2]
    sides = coupling.shape[1]
    rank = coupling.shape[3]
    depth = sides * rank
    field = (high[...], low[...])
    re = split(inverse[0, 0])
    im = split(inverse[0, 1])
    row_matrix = (rows_form(re[0], im[0]), rows_form(re[1], im[1]))
    column_matrix = (columns_form(re[0], im[0]), columns_form(re[1], im[1]))
    picker = one_hot(skeleton[...], width)
    zero = jnp.zeros_like(picker)
    picker2 = cat([cat([picker, zero], 1), cat([zero, picker], 1)], 0)
    z = split(dot3(field, row_matrix, NT))
    u = dot(z[0], picker2) + dot(z[1], picker2)
    near = []
    for side in range(sides):
        weight = mask[:, side : side + 1].astype(F32)
        near.append(cat([coupling[0, side, 0] * weight, coupling[0, side, 1] * weight], 1))
    near = split(cat(near, 0))
    base_out[:, : 2 * width] = dot3(z, column_matrix)
    base_out[:, 2 * width :] = u
    applied = split(dot3(near, column_matrix))
    for k, out in enumerate((high_out, low_out)):
        chosen = dot(near[k], picker2).astype(BF16)
        for matrix, at, part in ((applied[k], 0, width), (chosen, 2 * width, rank)):
            out[:depth, at : at + 2 * part] = matrix
            out[depth:, at : at + part] = -matrix[:, part:]
            out[depth:, at + part : at + 2 * part] = matrix[:, :part]


def join_kernel(base, even, odd, u, mine, came, row_out, pair_out):
    first = lax.axis_index("box") % 2 == 0
    row_out[0] = jnp.where(first, odd[...], even[...])
    row_out[1] = u[...]
    row_out[2] = jnp.where(first, even[...], odd[...])
    pair_out[0] = mine[...]
    pair_out[1] = came[...]


def message_kernel(even, middle, odd, base, high, low, keep_out, send_out):
    first = lax.axis_index("blk") % 2 == 0
    up = jnp.where(first, odd[...], even[...])
    down = jnp.where(first, even[...], odd[...])
    boxes = 2 * keep_out.shape[0]
    count = base.shape[0]
    width = keep_out.shape[2]
    rank = up.shape[1] // 2
    share = count // boxes
    half = share // 2
    order = (up[0], up[1], up[2], middle[0], middle[2], down[0], down[1], down[2])
    stacked = cat([v[:rank] for v in order] + [v[rank:] for v in order], 0)
    near = split(stacked.T)
    w = base[...] - dot3(near, (high[...], low[...]))
    lower = lax.axis_index("box") % 2 == 0
    for pair in range(boxes // 2):
        at = 2 * pair * share
        mine = w[at : at + share]
        other = w[at + share : at + 2 * share]
        for out, rows in (
            (keep_out, jnp.where(lower, mine, other)),
            (send_out, jnp.where(lower, other, mine)),
        ):
            out[pair, :share] = rows[:, :width]
            out[pair, share : 2 * share] = rows[:, width : 2 * width]
            t = rows[:, 2 * width :]
            out[pair, 2 * share : 2 * share + half] = cat([t[:half], t[half:]], 1)


def forward_kernel(keep, came, *outs):
    place = lax.axis_index("box") // 2
    for k, out in enumerate(outs):
        out[0] = keep[place ^ k]
        out[1] = came[place ^ k]


def blocks_of(refs):
    return [block for v in refs for block in ([v[k] for k in range(v.shape[0])] if len(v.shape) == 3 else [v[...]])]


def stacked_form(block, rank, depth):
    high, low = both(block, lambda part: columns_form(part[:rank, depth:], part[rank:, depth:]))
    return cat([high, high, low], 0)


def prepare_kernel(*refs):
    top_high, top_low, local_out = refs[-3:]
    depth = top_high.shape[1] // 2
    rank = local_out.shape[1] // 6
    for k, block in enumerate(blocks_of(refs[:-3])):
        at = slice(2 * k * rank, 2 * (k + 1) * rank)
        parts = split(block)
        for part, top_out in zip(parts, (top_high, top_low)):
            top_out[at] = rows_form(part[:rank, :depth], part[rank:, :depth])
        local_out[k] = stacked_form(parts, rank, depth)


def top_kernel(offsets, messages, top_high, top_low, prepared, *refs):
    pieces = refs[:messages]
    late = [split(block) for block in blocks_of(refs[messages:-2])]
    out, packed = refs[-2:]
    boxes = 2 * messages
    width = pieces[0].shape[2]
    share = out.shape[1]
    half = share // 2
    ready = prepared.shape[0]
    rank = prepared.shape[1] // 6
    rows = 2 * rank
    depth = boxes * rank
    me = lax.axis_index("box")
    top = [(top_high[...], top_low[...])]
    local = [prepared[k] for k in range(ready)]
    if late:
        top.append([
            cat([rows_form(v[k][:rank, :depth], v[k][rank:, :depth]) for v in late], 0) for k in range(2)
        ])
        local += [stacked_form(v, rank, depth) for v in late]
    for k in range(boxes):
        packed[me ^ k] = pieces[k // 2][k % 2, 2 * share : 2 * share + half]
    t_re = []
    t_im = []
    for box in range(boxes):
        t = cat([packed[box, :, :rows], packed[box, :, rows:]], 0)
        t_re.append(t[:, :rank])
        t_im.append(t[:, rank:])
    t = split(cat(t_re + t_im, 1))
    t_both = cat(t, 0)
    y = []
    for high, low in top:
        first = dot(t_both, high, NT)
        y.append(first[:share] + (first[share:] + dot(t[0], low, NT)))
    y = split(cat(y, 1))
    for k in range(boxes):
        at = slice(k * rows, (k + 1) * rows)
        x = dot(cat([y[0][:, at], y[1][:, at], y[0][:, at]], 1), local[k])
        offset = offsets[k]
        piece = pieces[offset // 2]
        at = pl.ds(pl.multiple_of((me ^ offset) * width, width), width)
        out[0, :, at] = piece[offset % 2, :share] + x[:, :width]
        out[1, :, at] = piece[offset % 2, share : 2 * share] + x[:, width:]


def call(kernel, outs, *arrays, hbm=(), copied=(), extra=()):
    spaces = {i: pl.BlockSpec(memory_space=pl.ANY) for i in hbm}
    spaces.update({i: pl.BlockSpec(memory_space=pltpu.HBM) for i in copied})
    scratch = [pltpu.VMEM(arrays[i].shape, arrays[i].dtype) for i in copied]
    if scratch:
        scratch.append(pltpu.SemaphoreType.DMA((len(scratch),)))
    scratch += extra
    arrays = [pltpu.with_memory_space_constraint(v, pltpu.HBM) if i in copied else v for i, v in enumerate(arrays)]
    return pl.pallas_call(
        kernel,
        out_shape=[jax.ShapeDtypeStruct(shape, dtype) for shape, dtype in outs],
        in_specs=[spaces.get(i, VMEM) for i in range(len(arrays))],
        out_specs=[VMEM] * len(outs),
        scratch_shapes=scratch,
        compiler_params=pltpu.CompilerParams(vmem_limit_bytes=40 * 1024 * 1024),
    )(*arrays)


def swapped(value, axis, bit):
    return lax.ppermute(value, axis, [(i, i ^ bit) for i in range(lax.axis_size(axis))])


def beside(value, axis):
    count = lax.axis_size(axis)
    even = lax.ppermute(value, axis, [(i, i ^ 1) for i in range(count)])
    odd = lax.ppermute(value, axis, [(i, (i + 1) % count if i % 2 else (i - 1) % count) for i in range(count)])
    return even, odd


def on_device(surface_points, angle_ids, near_mask, skeleton, box_inverse_parts, near_coupling, top_inverse):
    boxes = lax.axis_size("box")
    width = box_inverse_parts.shape[2]
    count = angle_ids.shape[0]
    rank = skeleton.shape[1]
    sides = near_mask.shape[1]
    depth = top_inverse.shape[3]
    share = count // boxes
    u, static, high, low = call(
        field_kernel,
        [
            ((2 * rank, count), F32),
            ((2 * rank, depth + width), F32),
            ((count, 2 * width), BF16),
            ((count, 2 * width), BF16),
        ],
        surface_points, angle_ids.reshape(1, count), skeleton, box_inverse_parts, top_inverse,
        copied=range(5),
    )
    base, matrix_high, matrix_low = call(
        coupling_kernel,
        [
            ((count, 2 * width + 2 * rank), F32),
            ((2 * sides * rank, 2 * width + 2 * rank), BF16),
            ((2 * sides * rank, 2 * width + 2 * rank), BF16),
        ],
        high, low, skeleton, near_mask, box_inverse_parts, near_coupling,
        copied=range(2, 6),
    )
    even, odd = beside(u, "box")
    four = swapped(static, "box", boxes // 2)
    row, pair = call(
        join_kernel, [((3,) + u.shape, F32), ((2,) + static.shape, F32)], base, even, odd, u, static, four, hbm=(0,)
    )
    if boxes == 8:
        two = swapped(pair, "box", 2)
        one = swapped(pair, "box", 1)
        early = [pair, two, one]
        late = [swapped(one[:1], "box", 2), swapped(two[1:], "box", 1)]
        offsets = (0, 4, 2, 6, 1, 5, 3, 7)
    else:
        early, late = [pair], []
        offsets = [0, boxes // 2]
        step = boxes // 4
        while step > 0:
            early.append(swapped(jnp.concatenate(early), "box", step))
            offsets += [k ^ step for k in offsets]
            step //= 2
    even, odd = beside(row, "blk")
    length = 2 * share + -(-share // 16) * 8
    message = ((boxes // 2, length, width), F32)
    keep, send = call(
        message_kernel, [message, message],
        even, row, odd, base, matrix_high, matrix_low,
    )
    pieces = call(
        forward_kernel, [((2, length, width), F32)] * (boxes // 2), keep, swapped(send, "box", 1)
    )
    pieces = [pieces[0]] + [swapped(pieces[k], "box", 2 * k) for k in range(1, boxes // 2)]
    ready = boxes - len(late)
    top = ((ready * 2 * rank, 2 * depth), BF16)
    local = ((ready, 6 * rank, 2 * width), BF16)
    prepared = call(prepare_kernel, [top, top, local], *early)
    (out,) = call(
        functools.partial(top_kernel, offsets, len(pieces)), [((2, share, boxes * width), F32)],
        *prepared, *pieces, *late,
        extra=[pltpu.VMEM((boxes, share // 2, width), F32)],
    )
    return out


def solution(mesh):
    return jax.shard_map(
        on_device,
        mesh=mesh,
        in_specs=(
            P(None, ("blk", "box")),
            P("batch"),
            P(("blk", "box"), None),
            P(("blk", "box"), None),
            P(("blk", "box"), None, None, None),
            P(("blk", "box"), None, None, None, None),
            P("blk", None, "box", None),
        ),
        out_specs=P(None, ("batch", "box"), "blk"),
        check_vma=False,
    )
```

```python
import functools

import jax
import jax.numpy as jnp
import numpy as np
from jax import lax
from jax.experimental import pallas as pl
from jax.experimental.pallas import tpu as pltpu
from jax.sharding import PartitionSpec as P

SWEEP = 16384
WAVENUMBER = 24.0
F32 = jnp.float32
BF16 = jnp.bfloat16
COST = pl.CostEstimate(flops=10**10, bytes_accessed=10**7, transcendentals=0)
VMEM = pl.BlockSpec(memory_space=pltpu.VMEM)
NN = (((1,), (0,)), ((), ()))
NT = (((1,), (1,)), ((), ()))
TN = (((0,), (0,)), ((), ()))

HALF_PI_1 = float(np.float32(201.0 / 128.0))
HALF_PI_2 = float(np.float32(np.round((np.pi / 2 - HALF_PI_1) * 2.0**22) / 2.0**22))
HALF_PI_3 = float(np.float32(np.pi / 2 - HALF_PI_1 - HALF_PI_2))


def cat(parts, axis):
    return jnp.concatenate(parts, axis=axis)


def dot(a, b, form=NN):
    return lax.dot_general(a, b, form, preferred_element_type=F32)


def split(x):
    high = x.astype(BF16)
    return high, (x - high.astype(F32)).astype(BF16)


def dot3(a, b, form=NN):
    return dot(a[0], b[0], form) + (dot(a[0], b[1], form) + dot(a[1], b[0], form))


def both(pair, function):
    return function(pair[0]), function(pair[1])


def sin_cos_small(r):
    s = r * r
    sin = r + r * s * (-1.6666654611e-1 + s * (8.3321608736e-3 - s * 1.9515295891e-4))
    cos = 1.0 - 0.5 * s + s * s * (4.166664568298827e-2 + s * (-1.388731625493765e-3 + s * 2.443315711809948e-5))
    return sin, cos


def by_quadrant(quadrant, sin, cos):
    odd = (quadrant & 1) == 1
    out_sin = jnp.where(odd, cos, sin)
    out_cos = jnp.where(odd, sin, cos)
    out_sin = jnp.where((quadrant & 2) == 2, -out_sin, out_sin)
    out_cos = jnp.where(((quadrant + 1) & 2) == 2, -out_cos, out_cos)
    return out_sin, out_cos


def one_hot(skeleton, width):
    rows = lax.broadcasted_iota(jnp.int32, (width, skeleton.shape[1]), 0)
    return jnp.where(rows == skeleton, 1.0, 0.0).astype(BF16)


def rows_form(re, im):
    return cat([cat([re, -im], 1), cat([im, re], 1)], 0)


def columns_form(re, im):
    return cat([cat([re, im], 1), cat([-im, re], 1)], 0)


def field_kernel(points_in, angles_in, skeleton_in, inverse_in, top_in, u_out, static_out, high_out, low_out,
                 points, angles, skeleton, inverse, top, sems):
    copies = [
        pltpu.make_async_copy(source, target, sems.at[k])
        for k, (source, target) in enumerate((
            (angles_in, angles), (points_in, points), (skeleton_in, skeleton), (inverse_in, inverse), (top_in, top),
        ))
    ]
    for copy in copies:
        copy.start()
    count = angles.shape[1]
    width = points.shape[1]
    rank = skeleton.shape[1]
    copies[0].wait()
    ids = angles[...]
    quadrant = (ids + SWEEP // 8) >> (SWEEP.bit_length() - 3)
    rest = ids - quadrant * (SWEEP // 4)
    sin, cos = by_quadrant(quadrant, *sin_cos_small(rest.astype(F32) * (2.0 * np.pi / SWEEP)))
    pick = lax.broadcasted_iota(jnp.int32, (8, count), 0) == 0
    columns = jnp.where(pick, cos, sin).T
    cos_column = columns[:, 0:1]
    sin_column = columns[:, 1:2]
    copies[1].wait()
    x = points[0:1, :] * WAVENUMBER
    yz = points[1:2, :] * (0.6 * WAVENUMBER) + points[2:3, :] * (0.8 * WAVENUMBER)
    phase = x * cos_column + yz * sin_column
    turns = jnp.round(phase * (2.0 / np.pi))
    r = ((phase - turns * HALF_PI_1) - turns * HALF_PI_2) - turns * HALF_PI_3
    field_sin, field_cos = by_quadrant(turns.astype(jnp.int32), *sin_cos_small(r))
    field = split(cat([field_cos, field_sin], 1))
    high_out[...] = field[0]
    low_out[...] = field[1]
    copies[2].wait()
    picker = one_hot(skeleton[...], width)
    copies[3].wait()
    parts = split(cat([inverse[0, 0], inverse[0, 1]], 1))
    rows = dot(picker, cat(parts, 1), TN)
    rows_high = rows[:, : 2 * width]
    rows_low = rows[:, 2 * width :]
    whole = rows_high + rows_low
    form = both((rows_high, rows_low), lambda v: rows_form(v[:, :width], v[:, width:]).astype(BF16))
    u_out[...] = dot3(form, field, NT)
    depth = top.shape[3]
    copies[4].wait()
    for part in range(2):
        at = slice(part * rank, (part + 1) * rank)
        static_out[at, :depth] = top[0, part]
        static_out[at, depth:] = whole[:, part * width : (part + 1) * width]


def coupling_kernel(high, low, skeleton_in, mask_in, inverse_in, coupling_in, base_out, high_out, low_out,
                    skeleton, mask, inverse, coupling, sems):
    copies = [
        pltpu.make_async_copy(source, target, sems.at[k])
        for k, (source, target) in enumerate((
            (skeleton_in, skeleton), (mask_in, mask), (inverse_in, inverse), (coupling_in, coupling),
        ))
    ]
    for copy in copies:
        copy.start()
    for copy in copies:
        copy.wait()
    width = inverse.shape[2]
    sides = coupling.shape[1]
    rank = coupling.shape[3]
    depth = sides * rank
    field = (high[...], low[...])
    re = split(inverse[0, 0])
    im = split(inverse[0, 1])
    row_matrix = (rows_form(re[0], im[0]), rows_form(re[1], im[1]))
    column_matrix = (columns_form(re[0], im[0]), columns_form(re[1], im[1]))
    picker = one_hot(skeleton[...], width)
    zero = jnp.zeros_like(picker)
    picker2 = cat([cat([picker, zero], 1), cat([zero, picker], 1)], 0)
    z = split(dot3(field, row_matrix, NT))
    u = dot(z[0], picker2) + dot(z[1], picker2)
    near = []
    for side in range(sides):
        weight = mask[:, side : side + 1].astype(F32)
        near.append(cat([coupling[0, side, 0] * weight, coupling[0, side, 1] * weight], 1))
    near = split(cat(near, 0))
    base_out[:, : 2 * width] = dot3(z, column_matrix)
    base_out[:, 2 * width :] = u
    applied = split(dot3(near, column_matrix))
    for k, out in enumerate((high_out, low_out)):
        chosen = dot(near[k], picker2).astype(BF16)
        for matrix, at, part in ((applied[k], 0, width), (chosen, 2 * width, rank)):
            out[:depth, at : at + 2 * part] = matrix
            out[depth:, at : at + part] = -matrix[:, part:]
            out[depth:, at + part : at + 2 * part] = matrix[:, :part]


def join_kernel(base, middle_even, middle_odd, even, odd, mine, came, sides_out, pair_out):
    first = lax.axis_index("box") % 2 == 0
    sides_out[0] = jnp.where(first, odd[...], even[...])
    sides_out[1] = jnp.where(first, even[...], odd[...])
    pair_out[0] = mine[...]
    pair_out[1] = came[...]


def message_kernel(even, odd, middle_even, middle_odd, sides, base, high, low, keep_out, send_out):
    first = lax.axis_index("blk") % 2 == 0
    up = jnp.where(first, odd[...], even[...])
    down = jnp.where(first, even[...], odd[...])
    middle_up = jnp.where(first, middle_odd[...], middle_even[...])
    middle_down = jnp.where(first, middle_even[...], middle_odd[...])
    boxes = 2 * keep_out.shape[0]
    count = base.shape[0]
    width = keep_out.shape[2]
    rank = up.shape[1] // 2
    share = count // boxes
    half = share // 2
    order = (up[0], middle_up, up[1], sides[0], sides[1], down[0], middle_down, down[1])
    stacked = cat([v[:rank] for v in order] + [v[rank:] for v in order], 0)
    near = split(stacked.T)
    w = base[...] - dot3(near, (high[...], low[...]))
    lower = lax.axis_index("box") % 2 == 0
    for pair in range(boxes // 2):
        at = 2 * pair * share
        mine = w[at : at + share]
        other = w[at + share : at + 2 * share]
        for out, rows in (
            (keep_out, jnp.where(lower, mine, other)),
            (send_out, jnp.where(lower, other, mine)),
        ):
            out[pair, :share] = rows[:, :width]
            out[pair, share : 2 * share] = rows[:, width : 2 * width]
            t = rows[:, 2 * width :]
            out[pair, 2 * share : 2 * share + half] = cat([t[:half], t[half:]], 1)


def forward_kernel(keep, came, *outs):
    place = lax.axis_index("box") // 2
    for k, out in enumerate(outs):
        out[0] = keep[place ^ k]
        out[1] = came[place ^ k]


def blocks_of(refs):
    return [block for v in refs for block in ([v[k] for k in range(v.shape[0])] if len(v.shape) == 3 else [v[...]])]


def stacked_form(block, rank, depth):
    high, low = both(block, lambda part: columns_form(part[:rank, depth:], part[rank:, depth:]))
    return cat([high, high, low], 0)


def prepare_kernel(*refs):
    top_high, top_low, local_out = refs[-3:]
    depth = top_high.shape[1] // 2
    rank = local_out.shape[1] // 6
    for k, block in enumerate(blocks_of(refs[:-3])):
        at = slice(2 * k * rank, 2 * (k + 1) * rank)
        parts = split(block)
        for part, top_out in zip(parts, (top_high, top_low)):
            top_out[at] = rows_form(part[:rank, :depth], part[rank:, :depth])
        local_out[k] = stacked_form(parts, rank, depth)


def top_kernel(offsets, messages, top_high, top_low, prepared, *refs):
    pieces = refs[:messages]
    late = [split(block) for block in blocks_of(refs[messages:-2])]
    out, packed = refs[-2:]
    boxes = 2 * messages
    width = pieces[0].shape[2]
    share = out.shape[1]
    half = share // 2
    ready = prepared.shape[0]
    rank = prepared.shape[1] // 6
    rows = 2 * rank
    depth = boxes * rank
    me = lax.axis_index("box")
    top = [(top_high[...], top_low[...])]
    local = [prepared[k] for k in range(ready)]
    if late:
        top.append([
            cat([rows_form(v[k][:rank, :depth], v[k][rank:, :depth]) for v in late], 0) for k in range(2)
        ])
        local += [stacked_form(v, rank, depth) for v in late]
    for k in range(boxes):
        packed[me ^ k] = pieces[k // 2][k % 2, 2 * share : 2 * share + half]
    t_re = []
    t_im = []
    for box in range(boxes):
        t = cat([packed[box, :, :rows], packed[box, :, rows:]], 0)
        t_re.append(t[:, :rank])
        t_im.append(t[:, rank:])
    t = split(cat(t_re + t_im, 1))
    t_both = cat(t, 0)
    y = []
    for high, low in top:
        first = dot(t_both, high, NT)
        y.append(first[:share] + (first[share:] + dot(t[0], low, NT)))
    y = split(cat(y, 1))
    for k in range(boxes):
        at = slice(k * rows, (k + 1) * rows)
        x = dot(cat([y[0][:, at], y[1][:, at], y[0][:, at]], 1), local[k])
        offset = offsets[k]
        piece = pieces[offset // 2]
        at = pl.ds(pl.multiple_of((me ^ offset) * width, width), width)
        out[0, :, at] = piece[offset % 2, :share] + x[:, :width]
        out[1, :, at] = piece[offset % 2, share : 2 * share] + x[:, width:]


def call(kernel, outs, *arrays, hbm=(), copied=(), extra=(), cost=None):
    spaces = {i: pl.BlockSpec(memory_space=pl.ANY) for i in hbm}
    spaces.update({i: pl.BlockSpec(memory_space=pltpu.HBM) for i in copied})
    scratch = [pltpu.VMEM(arrays[i].shape, arrays[i].dtype) for i in copied]
    if scratch:
        scratch.append(pltpu.SemaphoreType.DMA((len(scratch),)))
    scratch += extra
    arrays = [pltpu.with_memory_space_constraint(v, pltpu.HBM) if i in copied else v for i, v in enumerate(arrays)]
    return pl.pallas_call(
        kernel,
        out_shape=[jax.ShapeDtypeStruct(shape, dtype) for shape, dtype in outs],
        in_specs=[spaces.get(i, VMEM) for i in range(len(arrays))],
        out_specs=[VMEM] * len(outs),
        scratch_shapes=scratch,
        cost_estimate=cost,
        compiler_params=pltpu.CompilerParams(vmem_limit_bytes=40 * 1024 * 1024),
    )(*arrays)


def swapped(value, axis, bit):
    return lax.ppermute(value, axis, [(i, i ^ bit) for i in range(lax.axis_size(axis))])


def beside(value, axis):
    count = lax.axis_size(axis)
    even = lax.ppermute(value, axis, [(i, i ^ 1) for i in range(count)])
    odd = lax.ppermute(value, axis, [(i, (i + 1) % count if i % 2 else (i - 1) % count) for i in range(count)])
    return even, odd


def on_device(surface_points, angle_ids, near_mask, skeleton, box_inverse_parts, near_coupling, top_inverse):
    boxes = lax.axis_size("box")
    width = box_inverse_parts.shape[2]
    count = angle_ids.shape[0]
    rank = skeleton.shape[1]
    sides = near_mask.shape[1]
    depth = top_inverse.shape[3]
    share = count // boxes
    u, static, high, low = call(
        field_kernel,
        [
            ((2 * rank, count), F32),
            ((2 * rank, depth + width), F32),
            ((count, 2 * width), BF16),
            ((count, 2 * width), BF16),
        ],
        surface_points, angle_ids.reshape(1, count), skeleton, box_inverse_parts, top_inverse,
        copied=range(5),
    )
    base, matrix_high, matrix_low = call(
        coupling_kernel,
        [
            ((count, 2 * width + 2 * rank), F32),
            ((2 * sides * rank, 2 * width + 2 * rank), BF16),
            ((2 * sides * rank, 2 * width + 2 * rank), BF16),
        ],
        high, low, skeleton, near_mask, box_inverse_parts, near_coupling,
        copied=range(2, 6),
    )
    even, odd = beside(u, "box")
    four = swapped(static, "box", boxes // 2)
    middle = beside(u, "blk")
    across, pair = call(
        join_kernel, [((2,) + u.shape, F32), ((2,) + static.shape, F32)],
        base, *middle, even, odd, static, four, hbm=(0, 1, 2),
    )
    if boxes == 8:
        two = swapped(pair, "box", 2)
        one = swapped(pair, "box", 1)
        early = [pair, two, one]
        late = [swapped(one[:1], "box", 2), swapped(two[1:], "box", 1)]
        offsets = (0, 4, 2, 6, 1, 5, 3, 7)
    else:
        early, late = [pair], []
        offsets = [0, boxes // 2]
        step = boxes // 4
        while step > 0:
            early.append(swapped(jnp.concatenate(early), "box", step))
            offsets += [k ^ step for k in offsets]
            step //= 2
    even, odd = beside(across, "blk")
    length = 2 * share + -(-share // 16) * 8
    message = ((boxes // 2, length, width), F32)
    keep, send = call(
        message_kernel, [message, message],
        even, odd, *middle, across, base, matrix_high, matrix_low,
        cost=COST,
    )
    pieces = call(
        forward_kernel, [((2, length, width), F32)] * (boxes // 2), keep, swapped(send, "box", 1)
    )
    pieces = [pieces[0]] + [swapped(pieces[k], "box", 2 * k) for k in range(1, boxes // 2)]
    ready = boxes - len(late)
    top = ((ready * 2 * rank, 2 * depth), BF16)
    local = ((ready, 6 * rank, 2 * width), BF16)
    prepared = call(prepare_kernel, [top, top, local], *early)
    (out,) = call(
        functools.partial(top_kernel, offsets, len(pieces)), [((2, share, boxes * width), F32)],
        *prepared, *pieces, *late,
        extra=[pltpu.VMEM((boxes, share // 2, width), F32)],
    )
    return out


def solution(mesh):
    return jax.shard_map(
        on_device,
        mesh=mesh,
        in_specs=(
            P(None, ("blk", "box")),
            P("batch"),
            P(("blk", "box"), None),
            P(("blk", "box"), None),
            P(("blk", "box"), None, None, None),
            P(("blk", "box"), None, None, None, None),
            P("blk", None, "box", None),
        ),
        out_specs=P(None, ("batch", "box"), "blk"),
        check_vma=False,
    )
```

```python
import functools

import jax
import jax.numpy as jnp
import numpy as np
from jax import lax
from jax.experimental import pallas as pl
from jax.experimental.pallas import tpu as pltpu
from jax.sharding import PartitionSpec as P

SWEEP = 16384
WAVENUMBER = 24.0
F32 = jnp.float32
BF16 = jnp.bfloat16
COST = pl.CostEstimate(flops=10**10, bytes_accessed=10**7, transcendentals=0)
VMEM = pl.BlockSpec(memory_space=pltpu.VMEM)
NN = (((1,), (0,)), ((), ()))
NT = (((1,), (1,)), ((), ()))
TN = (((0,), (0,)), ((), ()))

HALF_PI_1 = float(np.float32(201.0 / 128.0))
HALF_PI_2 = float(np.float32(np.round((np.pi / 2 - HALF_PI_1) * 2.0**22) / 2.0**22))
HALF_PI_3 = float(np.float32(np.pi / 2 - HALF_PI_1 - HALF_PI_2))


def cat(parts, axis):
    return jnp.concatenate(parts, axis=axis)


def dot(a, b, form=NN):
    return lax.dot_general(a, b, form, preferred_element_type=F32)


def split(x):
    high = x.astype(BF16)
    return high, (x - high.astype(F32)).astype(BF16)


def dot3(a, b, form=NN):
    return dot(a[0], b[0], form) + (dot(a[0], b[1], form) + dot(a[1], b[0], form))


def both(pair, function):
    return function(pair[0]), function(pair[1])


def sin_cos_small(r):
    s = r * r
    sin = r + r * s * (-1.6666654611e-1 + s * (8.3321608736e-3 - s * 1.9515295891e-4))
    cos = 1.0 - 0.5 * s + s * s * (4.166664568298827e-2 + s * (-1.388731625493765e-3 + s * 2.443315711809948e-5))
    return sin, cos


def by_quadrant(quadrant, sin, cos):
    odd = (quadrant & 1) == 1
    out_sin = jnp.where(odd, cos, sin)
    out_cos = jnp.where(odd, sin, cos)
    out_sin = jnp.where((quadrant & 2) == 2, -out_sin, out_sin)
    out_cos = jnp.where(((quadrant + 1) & 2) == 2, -out_cos, out_cos)
    return out_sin, out_cos


def one_hot(skeleton, width):
    rows = lax.broadcasted_iota(jnp.int32, (width, skeleton.shape[1]), 0)
    return jnp.where(rows == skeleton, 1.0, 0.0).astype(BF16)


def rows_form(re, im):
    return cat([cat([re, -im], 1), cat([im, re], 1)], 0)


def columns_form(re, im):
    return cat([cat([re, im], 1), cat([-im, re], 1)], 0)


def field_kernel(points_in, angles_in, skeleton_in, inverse_in, top_in, u_out, static_out, high_out, low_out,
                 points, angles, skeleton, inverse, top, sems):
    copies = [
        pltpu.make_async_copy(source, target, sems.at[k])
        for k, (source, target) in enumerate((
            (angles_in, angles), (points_in, points), (skeleton_in, skeleton), (inverse_in, inverse), (top_in, top),
        ))
    ]
    for copy in copies:
        copy.start()
    count = angles.shape[1]
    width = points.shape[1]
    rank = skeleton.shape[1]
    copies[0].wait()
    ids = angles[...]
    quadrant = (ids + SWEEP // 8) >> (SWEEP.bit_length() - 3)
    rest = ids - quadrant * (SWEEP // 4)
    sin, cos = by_quadrant(quadrant, *sin_cos_small(rest.astype(F32) * (2.0 * np.pi / SWEEP)))
    pick = lax.broadcasted_iota(jnp.int32, (8, count), 0) == 0
    columns = jnp.where(pick, cos, sin).T
    cos_column = columns[:, 0:1]
    sin_column = columns[:, 1:2]
    copies[1].wait()
    x = points[0:1, :] * WAVENUMBER
    yz = points[1:2, :] * (0.6 * WAVENUMBER) + points[2:3, :] * (0.8 * WAVENUMBER)
    phase = x * cos_column + yz * sin_column
    turns = jnp.round(phase * (2.0 / np.pi))
    r = ((phase - turns * HALF_PI_1) - turns * HALF_PI_2) - turns * HALF_PI_3
    field_sin, field_cos = by_quadrant(turns.astype(jnp.int32), *sin_cos_small(r))
    field = split(cat([field_cos, field_sin], 1))
    high_out[...] = field[0]
    low_out[...] = field[1]
    copies[2].wait()
    picker = one_hot(skeleton[...], width)
    copies[3].wait()
    parts = split(cat([inverse[0, 0], inverse[0, 1]], 1))
    rows = dot(picker, cat(parts, 1), TN)
    rows_high = rows[:, : 2 * width]
    rows_low = rows[:, 2 * width :]
    whole = rows_high + rows_low
    form = both((rows_high, rows_low), lambda v: rows_form(v[:, :width], v[:, width:]).astype(BF16))
    u_out[...] = dot3(form, field, NT)
    depth = top.shape[3]
    copies[4].wait()
    for part in range(2):
        at = slice(part * rank, (part + 1) * rank)
        static_out[at, :depth] = top[0, part]
        static_out[at, depth:] = whole[:, part * width : (part + 1) * width]


def coupling_kernel(high, low, skeleton_in, mask_in, inverse_in, coupling_in, base_out, high_out, low_out,
                    skeleton, mask, inverse, coupling, sems):
    copies = [
        pltpu.make_async_copy(source, target, sems.at[k])
        for k, (source, target) in enumerate((
            (skeleton_in, skeleton), (mask_in, mask), (inverse_in, inverse), (coupling_in, coupling),
        ))
    ]
    for copy in copies:
        copy.start()
    for copy in copies:
        copy.wait()
    width = inverse.shape[2]
    sides = coupling.shape[1]
    rank = coupling.shape[3]
    depth = sides * rank
    field = (high[...], low[...])
    re = split(inverse[0, 0])
    im = split(inverse[0, 1])
    row_matrix = (rows_form(re[0], im[0]), rows_form(re[1], im[1]))
    column_matrix = (columns_form(re[0], im[0]), columns_form(re[1], im[1]))
    picker = one_hot(skeleton[...], width)
    zero = jnp.zeros_like(picker)
    picker2 = cat([cat([picker, zero], 1), cat([zero, picker], 1)], 0)
    z = split(dot3(field, row_matrix, NT))
    u = dot(z[0], picker2) + dot(z[1], picker2)
    near = []
    for side in range(sides):
        weight = mask[:, side : side + 1].astype(F32)
        near.append(cat([coupling[0, side, 0] * weight, coupling[0, side, 1] * weight], 1))
    near = split(cat(near, 0))
    base_out[:, : 2 * width] = dot3(z, column_matrix)
    base_out[:, 2 * width :] = u
    applied = split(dot3(near, column_matrix))
    for k, out in enumerate((high_out, low_out)):
        chosen = dot(near[k], picker2).astype(BF16)
        for matrix, at, part in ((applied[k], 0, width), (chosen, 2 * width, rank)):
            out[:depth, at : at + 2 * part] = matrix
            out[depth:, at : at + part] = -matrix[:, part:]
            out[depth:, at + part : at + 2 * part] = matrix[:, :part]


def hold_kernel(static, out):
    out[...] = static[...]


def pack_kernel(one, two, four, out):
    out[0] = two[...]
    out[1] = four[...]


def join_kernel(base, even, odd, u, row_out):
    first = lax.axis_index("box") % 2 == 0
    row_out[0] = jnp.where(first, odd[...], even[...])
    row_out[1] = u[...]
    row_out[2] = jnp.where(first, even[...], odd[...])


def message_kernel(even, middle, odd, base, high, low, keep_out, send_out):
    first = lax.axis_index("blk") % 2 == 0
    up = jnp.where(first, odd[...], even[...])
    down = jnp.where(first, even[...], odd[...])
    boxes = 2 * keep_out.shape[0]
    count = base.shape[0]
    width = keep_out.shape[2]
    rank = up.shape[1] // 2
    share = count // boxes
    half = share // 2
    order = (up[0], up[1], up[2], middle[0], middle[2], down[0], down[1], down[2])
    stacked = cat([v[:rank] for v in order] + [v[rank:] for v in order], 0)
    near = split(stacked.T)
    w = base[...] - dot3(near, (high[...], low[...]))
    lower = lax.axis_index("box") % 2 == 0
    for pair in range(boxes // 2):
        at = 2 * pair * share
        mine = w[at : at + share]
        other = w[at + share : at + 2 * share]
        for out, rows in (
            (keep_out, jnp.where(lower, mine, other)),
            (send_out, jnp.where(lower, other, mine)),
        ):
            out[pair, :share] = rows[:, :width]
            out[pair, share : 2 * share] = rows[:, width : 2 * width]
            t = rows[:, 2 * width :]
            out[pair, 2 * share : 2 * share + half] = cat([t[:half], t[half:]], 1)


def forward_kernel(count, keep, came, *refs):
    outs = refs[-count:]
    place = lax.axis_index("box") // 2
    for k, out in enumerate(outs):
        out[0] = keep[place ^ k]
        out[1] = came[place ^ k]


def blocks_of(refs):
    return [block for v in refs for block in ([v[k] for k in range(v.shape[0])] if len(v.shape) == 3 else [v[...]])]


def stacked_form(block, rank, depth):
    high, low = both(block, lambda part: columns_form(part[:rank, depth:], part[rank:, depth:]))
    return cat([high, high, low], 0)


def prepare_kernel(*refs):
    top_high, top_low, local_out = refs[-3:]
    depth = top_high.shape[1] // 2
    rank = local_out.shape[1] // 6
    for k, block in enumerate(blocks_of(refs[:-3])):
        at = slice(2 * k * rank, 2 * (k + 1) * rank)
        parts = split(block)
        for part, top_out in zip(parts, (top_high, top_low)):
            top_out[at] = rows_form(part[:rank, :depth], part[rank:, :depth])
        local_out[k] = stacked_form(parts, rank, depth)


def top_kernel(offsets, messages, top_high, top_low, prepared, *refs):
    pieces = refs[:messages]
    late = [split(block) for block in blocks_of(refs[messages:-2])]
    out, packed = refs[-2:]
    boxes = 2 * messages
    width = pieces[0].shape[2]
    share = out.shape[1]
    half = share // 2
    ready = prepared.shape[0]
    rank = prepared.shape[1] // 6
    rows = 2 * rank
    depth = boxes * rank
    me = lax.axis_index("box")
    top = [(top_high[...], top_low[...])]
    local = [prepared[k] for k in range(ready)]
    if late:
        top.append([
            cat([rows_form(v[k][:rank, :depth], v[k][rank:, :depth]) for v in late], 0) for k in range(2)
        ])
        local += [stacked_form(v, rank, depth) for v in late]
    for k in range(boxes):
        packed[me ^ k] = pieces[k // 2][k % 2, 2 * share : 2 * share + half]
    t_re = []
    t_im = []
    for box in range(boxes):
        t = cat([packed[box, :, :rows], packed[box, :, rows:]], 0)
        t_re.append(t[:, :rank])
        t_im.append(t[:, rank:])
    t = split(cat(t_re + t_im, 1))
    t_both = cat(t, 0)
    y = []
    for high, low in top:
        first = dot(t_both, high, NT)
        y.append(first[:share] + (first[share:] + dot(t[0], low, NT)))
    y = split(cat(y, 1))
    for k in range(boxes):
        at = slice(k * rows, (k + 1) * rows)
        x = dot(cat([y[0][:, at], y[1][:, at], y[0][:, at]], 1), local[k])
        offset = offsets[k]
        piece = pieces[offset // 2]
        at = pl.ds(pl.multiple_of((me ^ offset) * width, width), width)
        out[0, :, at] = piece[offset % 2, :share] + x[:, :width]
        out[1, :, at] = piece[offset % 2, share : 2 * share] + x[:, width:]


def call(kernel, outs, *arrays, hbm=(), copied=(), extra=(), cost=None):
    spaces = {i: pl.BlockSpec(memory_space=pl.ANY) for i in hbm}
    spaces.update({i: pl.BlockSpec(memory_space=pltpu.HBM) for i in copied})
    scratch = [pltpu.VMEM(arrays[i].shape, arrays[i].dtype) for i in copied]
    if scratch:
        scratch.append(pltpu.SemaphoreType.DMA((len(scratch),)))
    scratch += extra
    arrays = [pltpu.with_memory_space_constraint(v, pltpu.HBM) if i in copied else v for i, v in enumerate(arrays)]
    return pl.pallas_call(
        kernel,
        out_shape=[jax.ShapeDtypeStruct(shape, dtype) for shape, dtype in outs],
        in_specs=[spaces.get(i, VMEM) for i in range(len(arrays))],
        out_specs=[VMEM] * len(outs),
        scratch_shapes=scratch,
        cost_estimate=cost,
        compiler_params=pltpu.CompilerParams(vmem_limit_bytes=40 * 1024 * 1024),
    )(*arrays)


def swapped(value, axis, bit):
    return lax.ppermute(value, axis, [(i, i ^ bit) for i in range(lax.axis_size(axis))])


def beside(value, axis):
    count = lax.axis_size(axis)
    even = lax.ppermute(value, axis, [(i, i ^ 1) for i in range(count)])
    odd = lax.ppermute(value, axis, [(i, (i + 1) % count if i % 2 else (i - 1) % count) for i in range(count)])
    return even, odd


def on_device(surface_points, angle_ids, near_mask, skeleton, box_inverse_parts, near_coupling, top_inverse):
    boxes = lax.axis_size("box")
    width = box_inverse_parts.shape[2]
    count = angle_ids.shape[0]
    rank = skeleton.shape[1]
    sides = near_mask.shape[1]
    depth = top_inverse.shape[3]
    share = count // boxes
    u, static, high, low = call(
        field_kernel,
        [
            ((2 * rank, count), F32),
            ((2 * rank, depth + width), F32),
            ((count, 2 * width), BF16),
            ((count, 2 * width), BF16),
        ],
        surface_points, angle_ids.reshape(1, count), skeleton, box_inverse_parts, top_inverse,
        copied=range(5),
    )
    base, matrix_high, matrix_low = call(
        coupling_kernel,
        [
            ((count, 2 * width + 2 * rank), F32),
            ((2 * sides * rank, 2 * width + 2 * rank), BF16),
            ((2 * sides * rank, 2 * width + 2 * rank), BF16),
        ],
        high, low, skeleton, near_mask, box_inverse_parts, near_coupling,
        copied=range(2, 6),
    )
    even, odd = beside(u, "box")
    (row,) = call(join_kernel, [((3,) + u.shape, F32)], base, even, odd, u, hbm=(0,))
    (static,) = call(hold_kernel, [(static.shape, F32)], static, cost=COST)
    waited = []
    if boxes == 8:
        four, two, one = [swapped(static, "box", k) for k in (4, 2, 1)]
        (pair,) = call(pack_kernel, [((2,) + static.shape, F32)], one, two, four, hbm=(0,))
        waited = [swapped(four, "box", 2), swapped(four, "box", 3)]
        early, late = [static, four, two, one, *waited], [swapped(pair, "box", 1)]
        offsets = (0, 4, 2, 1, 6, 7, 3, 5)
    else:
        early, late = [static[None]], []
        offsets = [0]
        step = boxes // 2
        while step > 0:
            early.append(swapped(jnp.concatenate(early), "box", step))
            offsets += [k ^ step for k in offsets]
            step //= 2
    even, odd = beside(row, "blk")
    length = 2 * share + -(-share // 16) * 8
    message = ((boxes // 2, length, width), F32)
    keep, send = call(
        message_kernel, [message, message],
        even, row, odd, base, matrix_high, matrix_low,
        cost=COST,
    )
    pieces = call(
        functools.partial(forward_kernel, boxes // 2), [((2, length, width), F32)] * (boxes // 2),
        keep, swapped(send, "box", 1), *waited, hbm=range(2, 2 + len(waited)),
    )
    pieces = [pieces[0]] + [swapped(pieces[k], "box", 2 * k) for k in range(1, boxes // 2)]
    ready = 6 if late else boxes
    top = ((ready * 2 * rank, 2 * depth), BF16)
    local = ((ready, 6 * rank, 2 * width), BF16)
    prepared = call(prepare_kernel, [top, top, local], *early)
    (out,) = call(
        functools.partial(top_kernel, offsets, len(pieces)), [((2, share, boxes * width), F32)],
        *prepared, *pieces, *late,
        extra=[pltpu.VMEM((boxes, share // 2, width), F32)],
    )
    return out


def solution(mesh):
    return jax.shard_map(
        on_device,
        mesh=mesh,
        in_specs=(
            P(None, ("blk", "box")),
            P("batch"),
            P(("blk", "box"), None),
            P(("blk", "box"), None),
            P(("blk", "box"), None, None, None),
            P(("blk", "box"), None, None, None, None),
            P("blk", None, "box", None),
        ),
        out_specs=P(None, ("batch", "box"), "blk"),
        check_vma=False,
    )
```

```python
import functools

import jax
import jax.numpy as jnp
import numpy as np
from jax import lax
from jax.experimental import pallas as pl
from jax.experimental.pallas import tpu as pltpu
from jax.sharding import PartitionSpec as P

SWEEP = 16384
WAVENUMBER = 24.0
F32 = jnp.float32
BF16 = jnp.bfloat16
COST = pl.CostEstimate(flops=10**10, bytes_accessed=10**7, transcendentals=0)
VMEM = pl.BlockSpec(memory_space=pltpu.VMEM)
NN = (((1,), (0,)), ((), ()))
NT = (((1,), (1,)), ((), ()))
TN = (((0,), (0,)), ((), ()))

HALF_PI_1 = float(np.float32(201.0 / 128.0))
HALF_PI_2 = float(np.float32(np.round((np.pi / 2 - HALF_PI_1) * 2.0**22) / 2.0**22))
HALF_PI_3 = float(np.float32(np.pi / 2 - HALF_PI_1 - HALF_PI_2))


def cat(parts, axis):
    return jnp.concatenate(parts, axis=axis)


def dot(a, b, form=NN):
    return lax.dot_general(a, b, form, preferred_element_type=F32)


def split(x):
    high = x.astype(BF16)
    return high, (x - high.astype(F32)).astype(BF16)


def dot3(a, b, form=NN):
    return dot(a[0], b[0], form) + (dot(a[0], b[1], form) + dot(a[1], b[0], form))


def both(pair, function):
    return function(pair[0]), function(pair[1])


def sin_cos_small(r):
    s = r * r
    sin = r + r * s * (-1.6666654611e-1 + s * (8.3321608736e-3 - s * 1.9515295891e-4))
    cos = 1.0 - 0.5 * s + s * s * (4.166664568298827e-2 + s * (-1.388731625493765e-3 + s * 2.443315711809948e-5))
    return sin, cos


def by_quadrant(quadrant, sin, cos):
    odd = (quadrant & 1) == 1
    out_sin = jnp.where(odd, cos, sin)
    out_cos = jnp.where(odd, sin, cos)
    out_sin = jnp.where((quadrant & 2) == 2, -out_sin, out_sin)
    out_cos = jnp.where(((quadrant + 1) & 2) == 2, -out_cos, out_cos)
    return out_sin, out_cos


def one_hot(skeleton, width):
    rows = lax.broadcasted_iota(jnp.int32, (width, skeleton.shape[1]), 0)
    return jnp.where(rows == skeleton, 1.0, 0.0).astype(BF16)


def rows_form(re, im):
    return cat([cat([re, -im], 1), cat([im, re], 1)], 0)


def columns_form(re, im):
    return cat([cat([re, im], 1), cat([-im, re], 1)], 0)


def field_kernel(points_in, angles_in, skeleton_in, inverse_in, top_in, u_out, static_out, high_out, low_out,
                 points, angles, skeleton, inverse, top, sems):
    copies = [
        pltpu.make_async_copy(source, target, sems.at[k])
        for k, (source, target) in enumerate((
            (angles_in, angles), (points_in, points), (skeleton_in, skeleton), (inverse_in, inverse), (top_in, top),
        ))
    ]
    for copy in copies:
        copy.start()
    count = angles.shape[1]
    width = points.shape[1]
    rank = skeleton.shape[1]
    copies[0].wait()
    ids = angles[...]
    quadrant = (ids + SWEEP // 8) >> (SWEEP.bit_length() - 3)
    rest = ids - quadrant * (SWEEP // 4)
    sin, cos = by_quadrant(quadrant, *sin_cos_small(rest.astype(F32) * (2.0 * np.pi / SWEEP)))
    pick = lax.broadcasted_iota(jnp.int32, (8, count), 0) == 0
    columns = jnp.where(pick, cos, sin).T
    cos_column = columns[:, 0:1]
    sin_column = columns[:, 1:2]
    copies[1].wait()
    x = points[0:1, :] * WAVENUMBER
    yz = points[1:2, :] * (0.6 * WAVENUMBER) + points[2:3, :] * (0.8 * WAVENUMBER)
    phase = x * cos_column + yz * sin_column
    turns = jnp.round(phase * (2.0 / np.pi))
    r = ((phase - turns * HALF_PI_1) - turns * HALF_PI_2) - turns * HALF_PI_3
    field_sin, field_cos = by_quadrant(turns.astype(jnp.int32), *sin_cos_small(r))
    field = split(cat([field_cos, field_sin], 1))
    high_out[...] = field[0]
    low_out[...] = field[1]
    copies[2].wait()
    picker = one_hot(skeleton[...], width)
    copies[3].wait()
    parts = split(cat([inverse[0, 0], inverse[0, 1]], 1))
    rows = dot(picker, cat(parts, 1), TN)
    rows_high = rows[:, : 2 * width]
    rows_low = rows[:, 2 * width :]
    whole = rows_high + rows_low
    form = both((rows_high, rows_low), lambda v: rows_form(v[:, :width], v[:, width:]).astype(BF16))
    u_out[...] = dot3(form, field, NT)
    depth = top.shape[3]
    copies[4].wait()
    for part in range(2):
        at = slice(part * rank, (part + 1) * rank)
        static_out[at, :depth] = top[0, part]
        static_out[at, depth:] = whole[:, part * width : (part + 1) * width]


def coupling_kernel(high, low, skeleton_in, mask_in, inverse_in, coupling_in, base_out, high_out, low_out,
                    skeleton, mask, inverse, coupling, sems):
    copies = [
        pltpu.make_async_copy(source, target, sems.at[k])
        for k, (source, target) in enumerate((
            (skeleton_in, skeleton), (mask_in, mask), (inverse_in, inverse), (coupling_in, coupling),
        ))
    ]
    for copy in copies:
        copy.start()
    for copy in copies:
        copy.wait()
    width = inverse.shape[2]
    sides = coupling.shape[1]
    rank = coupling.shape[3]
    depth = sides * rank
    field = (high[...], low[...])
    re = split(inverse[0, 0])
    im = split(inverse[0, 1])
    row_matrix = (rows_form(re[0], im[0]), rows_form(re[1], im[1]))
    column_matrix = (columns_form(re[0], im[0]), columns_form(re[1], im[1]))
    picker = one_hot(skeleton[...], width)
    zero = jnp.zeros_like(picker)
    picker2 = cat([cat([picker, zero], 1), cat([zero, picker], 1)], 0)
    z = split(dot3(field, row_matrix, NT))
    u = dot(z[0], picker2) + dot(z[1], picker2)
    near = []
    for side in range(sides):
        weight = mask[:, side : side + 1].astype(F32)
        near.append(cat([coupling[0, side, 0] * weight, coupling[0, side, 1] * weight], 1))
    near = split(cat(near, 0))
    base_out[:, : 2 * width] = dot3(z, column_matrix)
    base_out[:, 2 * width :] = u
    applied = split(dot3(near, column_matrix))
    for k, out in enumerate((high_out, low_out)):
        chosen = dot(near[k], picker2).astype(BF16)
        for matrix, at, part in ((applied[k], 0, width), (chosen, 2 * width, rank)):
            out[:depth, at : at + 2 * part] = matrix
            out[depth:, at : at + part] = -matrix[:, part:]
            out[depth:, at + part : at + 2 * part] = matrix[:, :part]


def hold_kernel(static, out):
    out[...] = static[...]


def copy_kernel(value, first, second, out):
    out[...] = value[...]


def join_kernel(base, even, odd, u, row_out):
    first = lax.axis_index("box") % 2 == 0
    row_out[0] = jnp.where(first, odd[...], even[...])
    row_out[1] = u[...]
    row_out[2] = jnp.where(first, even[...], odd[...])


def message_kernel(even, middle, odd, base, high, low, keep_out, send_out):
    first = lax.axis_index("blk") % 2 == 0
    up = jnp.where(first, odd[...], even[...])
    down = jnp.where(first, even[...], odd[...])
    boxes = 2 * keep_out.shape[0]
    count = base.shape[0]
    width = keep_out.shape[2]
    rank = up.shape[1] // 2
    share = count // boxes
    half = share // 2
    order = (up[0], up[1], up[2], middle[0], middle[2], down[0], down[1], down[2])
    stacked = cat([v[:rank] for v in order] + [v[rank:] for v in order], 0)
    near = split(stacked.T)
    w = base[...] - dot3(near, (high[...], low[...]))
    lower = lax.axis_index("box") % 2 == 0
    for pair in range(boxes // 2):
        at = 2 * pair * share
        mine = w[at : at + share]
        other = w[at + share : at + 2 * share]
        for out, rows in (
            (keep_out, jnp.where(lower, mine, other)),
            (send_out, jnp.where(lower, other, mine)),
        ):
            out[pair, :share] = rows[:, :width]
            out[pair, share : 2 * share] = rows[:, width : 2 * width]
            t = rows[:, 2 * width :]
            out[pair, 2 * share : 2 * share + half] = cat([t[:half], t[half:]], 1)


def forward_kernel(count, keep, came, *refs):
    outs = refs[-count:]
    place = lax.axis_index("box") // 2
    for k, out in enumerate(outs):
        out[0] = keep[place ^ k]
        out[1] = came[place ^ k]


def blocks_of(refs):
    return [block for v in refs for block in ([v[k] for k in range(v.shape[0])] if len(v.shape) == 3 else [v[...]])]


def stacked_form(block, rank, depth):
    high, low = both(block, lambda part: columns_form(part[:rank, depth:], part[rank:, depth:]))
    return cat([high, high, low], 0)


def prepare_kernel(*refs):
    top_high, top_low, local_out = refs[-3:]
    depth = top_high.shape[1] // 2
    rank = local_out.shape[1] // 6
    for k, block in enumerate(blocks_of(refs[:-3])):
        at = slice(2 * k * rank, 2 * (k + 1) * rank)
        parts = split(block)
        for part, top_out in zip(parts, (top_high, top_low)):
            top_out[at] = rows_form(part[:rank, :depth], part[rank:, :depth])
        local_out[k] = stacked_form(parts, rank, depth)


def top_kernel(offsets, messages, top_high, top_low, prepared, *refs):
    pieces = refs[:messages]
    late = [split(block) for block in blocks_of(refs[messages:-2])]
    out, packed = refs[-2:]
    boxes = 2 * messages
    width = pieces[0].shape[2]
    share = out.shape[1]
    half = share // 2
    ready = prepared.shape[0]
    rank = prepared.shape[1] // 6
    rows = 2 * rank
    depth = boxes * rank
    me = lax.axis_index("box")
    top = [(top_high[...], top_low[...])]
    local = [prepared[k] for k in range(ready)]
    if late:
        top.append([
            cat([rows_form(v[k][:rank, :depth], v[k][rank:, :depth]) for v in late], 0) for k in range(2)
        ])
        local += [stacked_form(v, rank, depth) for v in late]
    for k in range(boxes):
        packed[me ^ k] = pieces[k // 2][k % 2, 2 * share : 2 * share + half]
    t_re = []
    t_im = []
    for box in range(boxes):
        t = cat([packed[box, :, :rows], packed[box, :, rows:]], 0)
        t_re.append(t[:, :rank])
        t_im.append(t[:, rank:])
    t = split(cat(t_re + t_im, 1))
    t_both = cat(t, 0)
    y = []
    for high, low in top:
        first = dot(t_both, high, NT)
        y.append(first[:share] + (first[share:] + dot(t[0], low, NT)))
    y = split(cat(y, 1))
    for k in range(boxes):
        at = slice(k * rows, (k + 1) * rows)
        x = dot(cat([y[0][:, at], y[1][:, at], y[0][:, at]], 1), local[k])
        offset = offsets[k]
        piece = pieces[offset // 2]
        at = pl.ds(pl.multiple_of((me ^ offset) * width, width), width)
        out[0, :, at] = piece[offset % 2, :share] + x[:, :width]
        out[1, :, at] = piece[offset % 2, share : 2 * share] + x[:, width:]


def call(kernel, outs, *arrays, hbm=(), copied=(), extra=(), cost=None):
    spaces = {i: pl.BlockSpec(memory_space=pl.ANY) for i in hbm}
    spaces.update({i: pl.BlockSpec(memory_space=pltpu.HBM) for i in copied})
    scratch = [pltpu.VMEM(arrays[i].shape, arrays[i].dtype) for i in copied]
    if scratch:
        scratch.append(pltpu.SemaphoreType.DMA((len(scratch),)))
    scratch += extra
    arrays = [pltpu.with_memory_space_constraint(v, pltpu.HBM) if i in copied else v for i, v in enumerate(arrays)]
    return pl.pallas_call(
        kernel,
        out_shape=[jax.ShapeDtypeStruct(shape, dtype) for shape, dtype in outs],
        in_specs=[spaces.get(i, VMEM) for i in range(len(arrays))],
        out_specs=[VMEM] * len(outs),
        scratch_shapes=scratch,
        cost_estimate=cost,
        compiler_params=pltpu.CompilerParams(vmem_limit_bytes=40 * 1024 * 1024),
    )(*arrays)


def swapped(value, axis, bit):
    return lax.ppermute(value, axis, [(i, i ^ bit) for i in range(lax.axis_size(axis))])


def beside(value, axis):
    count = lax.axis_size(axis)
    even = lax.ppermute(value, axis, [(i, i ^ 1) for i in range(count)])
    odd = lax.ppermute(value, axis, [(i, (i + 1) % count if i % 2 else (i - 1) % count) for i in range(count)])
    return even, odd


def on_device(surface_points, angle_ids, near_mask, skeleton, box_inverse_parts, near_coupling, top_inverse):
    boxes = lax.axis_size("box")
    width = box_inverse_parts.shape[2]
    count = angle_ids.shape[0]
    rank = skeleton.shape[1]
    sides = near_mask.shape[1]
    depth = top_inverse.shape[3]
    share = count // boxes
    u, static, high, low = call(
        field_kernel,
        [
            ((2 * rank, count), F32),
            ((2 * rank, depth + width), F32),
            ((count, 2 * width), BF16),
            ((count, 2 * width), BF16),
        ],
        surface_points, angle_ids.reshape(1, count), skeleton, box_inverse_parts, top_inverse,
        copied=range(5),
    )
    base, matrix_high, matrix_low = call(
        coupling_kernel,
        [
            ((count, 2 * width + 2 * rank), F32),
            ((2 * sides * rank, 2 * width + 2 * rank), BF16),
            ((2 * sides * rank, 2 * width + 2 * rank), BF16),
        ],
        high, low, skeleton, near_mask, box_inverse_parts, near_coupling,
        copied=range(2, 6),
    )
    even, odd = beside(u, "box")
    (row,) = call(join_kernel, [((3,) + u.shape, F32)], base, even, odd, u, hbm=(0,))
    (static,) = call(hold_kernel, [(static.shape, F32)], static, cost=COST)
    waited = []
    if boxes == 8:
        four, two, one = [swapped(static, "box", k) for k in (4, 2, 1)]
        (four,) = call(copy_kernel, [(static.shape, F32)], four, two, one, hbm=(1, 2))
        five, six, three = swapped(four, "box", 1), swapped(four, "box", 2), swapped(one, "box", 2)
        waited = [five]
        early, late = [static, four, two, one, five, six], [three, swapped(six, "box", 1)]
        offsets = (0, 4, 2, 1, 5, 6, 3, 7)
    else:
        early, late = [static[None]], []
        offsets = [0]
        step = boxes // 2
        while step > 0:
            early.append(swapped(jnp.concatenate(early), "box", step))
            offsets += [k ^ step for k in offsets]
            step //= 2
    even, odd = beside(row, "blk")
    length = 2 * share + -(-share // 16) * 8
    message = ((boxes // 2, length, width), F32)
    keep, send = call(
        message_kernel, [message, message],
        even, row, odd, base, matrix_high, matrix_low,
        cost=COST,
    )
    pieces = call(
        functools.partial(forward_kernel, boxes // 2), [((2, length, width), F32)] * (boxes // 2),
        keep, swapped(send, "box", 1), *waited, hbm=range(2, 2 + len(waited)),
    )
    pieces = [pieces[0]] + [swapped(pieces[k], "box", 2 * k) for k in range(1, boxes // 2)]
    ready = 6 if late else boxes
    top = ((ready * 2 * rank, 2 * depth), BF16)
    local = ((ready, 6 * rank, 2 * width), BF16)
    prepared = call(prepare_kernel, [top, top, local], *early)
    (out,) = call(
        functools.partial(top_kernel, offsets, len(pieces)), [((2, share, boxes * width), F32)],
        *prepared, *pieces, *late,
        extra=[pltpu.VMEM((boxes, share // 2, width), F32)],
    )
    return out


def solution(mesh):
    return jax.shard_map(
        on_device,
        mesh=mesh,
        in_specs=(
            P(None, ("blk", "box")),
            P("batch"),
            P(("blk", "box"), None),
            P(("blk", "box"), None),
            P(("blk", "box"), None, None, None),
            P(("blk", "box"), None, None, None, None),
            P("blk", None, "box", None),
        ),
        out_specs=P(None, ("batch", "box"), "blk"),
        check_vma=False,
    )
```

```python
import functools

import jax
import jax.numpy as jnp
import numpy as np
from jax import lax
from jax.experimental import pallas as pl
from jax.experimental.pallas import tpu as pltpu
from jax.sharding import PartitionSpec as P

SWEEP = 16384
WAVENUMBER = 24.0
F32 = jnp.float32
BF16 = jnp.bfloat16
COST = pl.CostEstimate(flops=10**10, bytes_accessed=10**7, transcendentals=0)
VMEM = pl.BlockSpec(memory_space=pltpu.VMEM)
NN = (((1,), (0,)), ((), ()))
NT = (((1,), (1,)), ((), ()))
TN = (((0,), (0,)), ((), ()))

HALF_PI_1 = float(np.float32(201.0 / 128.0))
HALF_PI_2 = float(np.float32(np.round((np.pi / 2 - HALF_PI_1) * 2.0**22) / 2.0**22))
HALF_PI_3 = float(np.float32(np.pi / 2 - HALF_PI_1 - HALF_PI_2))


def cat(parts, axis):
    return jnp.concatenate(parts, axis=axis)


def dot(a, b, form=NN):
    return lax.dot_general(a, b, form, preferred_element_type=F32)


def split(x):
    high = x.astype(BF16)
    return high, (x - high.astype(F32)).astype(BF16)


def dot3(a, b, form=NN):
    return dot(a[0], b[0], form) + (dot(a[0], b[1], form) + dot(a[1], b[0], form))


def both(pair, function):
    return function(pair[0]), function(pair[1])


def sin_cos_small(r):
    s = r * r
    sin = r + r * s * (-1.6666654611e-1 + s * (8.3321608736e-3 - s * 1.9515295891e-4))
    cos = 1.0 - 0.5 * s + s * s * (4.166664568298827e-2 + s * (-1.388731625493765e-3 + s * 2.443315711809948e-5))
    return sin, cos


def by_quadrant(quadrant, sin, cos):
    odd = (quadrant & 1) == 1
    out_sin = jnp.where(odd, cos, sin)
    out_cos = jnp.where(odd, sin, cos)
    out_sin = jnp.where((quadrant & 2) == 2, -out_sin, out_sin)
    out_cos = jnp.where(((quadrant + 1) & 2) == 2, -out_cos, out_cos)
    return out_sin, out_cos


def one_hot(skeleton, width):
    rows = lax.broadcasted_iota(jnp.int32, (width, skeleton.shape[1]), 0)
    return jnp.where(rows == skeleton, 1.0, 0.0).astype(BF16)


def rows_form(re, im):
    return cat([cat([re, -im], 1), cat([im, re], 1)], 0)


def columns_form(re, im):
    return cat([cat([re, im], 1), cat([-im, re], 1)], 0)


def field_kernel(points_in, angles_in, skeleton_in, inverse_in, top_in, u_out, static_out, high_out, low_out,
                 points, angles, skeleton, inverse, top, sems):
    copies = [
        pltpu.make_async_copy(source, target, sems.at[k])
        for k, (source, target) in enumerate((
            (angles_in, angles), (points_in, points), (skeleton_in, skeleton), (inverse_in, inverse), (top_in, top),
        ))
    ]
    for copy in copies:
        copy.start()
    count = angles.shape[1]
    width = points.shape[1]
    rank = skeleton.shape[1]
    copies[0].wait()
    ids = angles[...]
    quadrant = (ids + SWEEP // 8) >> (SWEEP.bit_length() - 3)
    rest = ids - quadrant * (SWEEP // 4)
    sin, cos = by_quadrant(quadrant, *sin_cos_small(rest.astype(F32) * (2.0 * np.pi / SWEEP)))
    pick = lax.broadcasted_iota(jnp.int32, (8, count), 0) == 0
    columns = jnp.where(pick, cos, sin).T
    cos_column = columns[:, 0:1]
    sin_column = columns[:, 1:2]
    copies[1].wait()
    x = points[0:1, :] * WAVENUMBER
    yz = points[1:2, :] * (0.6 * WAVENUMBER) + points[2:3, :] * (0.8 * WAVENUMBER)
    phase = x * cos_column + yz * sin_column
    turns = jnp.round(phase * (2.0 / np.pi))
    r = ((phase - turns * HALF_PI_1) - turns * HALF_PI_2) - turns * HALF_PI_3
    field_sin, field_cos = by_quadrant(turns.astype(jnp.int32), *sin_cos_small(r))
    field = split(cat([field_cos, field_sin], 1))
    high_out[...] = field[0]
    low_out[...] = field[1]
    copies[2].wait()
    picker = one_hot(skeleton[...], width)
    copies[3].wait()
    parts = split(cat([inverse[0, 0], inverse[0, 1]], 1))
    rows = dot(picker, cat(parts, 1), TN)
    rows_high = rows[:, : 2 * width]
    rows_low = rows[:, 2 * width :]
    whole = rows_high + rows_low
    form = both((rows_high, rows_low), lambda v: rows_form(v[:, :width], v[:, width:]).astype(BF16))
    u_out[...] = dot3(form, field, NT)
    depth = top.shape[3]
    copies[4].wait()
    for part in range(2):
        at = slice(part * rank, (part + 1) * rank)
        static_out[at, :depth] = top[0, part]
        static_out[at, depth:] = whole[:, part * width : (part + 1) * width]


def coupling_kernel(high, low, skeleton_in, mask_in, inverse_in, coupling_in, base_out, high_out, low_out,
                    skeleton, mask, inverse, coupling, sems):
    copies = [
        pltpu.make_async_copy(source, target, sems.at[k])
        for k, (source, target) in enumerate((
            (skeleton_in, skeleton), (mask_in, mask), (inverse_in, inverse), (coupling_in, coupling),
        ))
    ]
    for copy in copies:
        copy.start()
    for copy in copies:
        copy.wait()
    width = inverse.shape[2]
    sides = coupling.shape[1]
    rank = coupling.shape[3]
    depth = sides * rank
    field = (high[...], low[...])
    re = split(inverse[0, 0])
    im = split(inverse[0, 1])
    row_matrix = (rows_form(re[0], im[0]), rows_form(re[1], im[1]))
    column_matrix = (columns_form(re[0], im[0]), columns_form(re[1], im[1]))
    picker = one_hot(skeleton[...], width)
    zero = jnp.zeros_like(picker)
    picker2 = cat([cat([picker, zero], 1), cat([zero, picker], 1)], 0)
    z = split(dot3(field, row_matrix, NT))
    u = dot(z[0], picker2) + dot(z[1], picker2)
    near = []
    for side in range(sides):
        weight = mask[:, side : side + 1].astype(F32)
        near.append(cat([coupling[0, side, 0] * weight, coupling[0, side, 1] * weight], 1))
    near = split(cat(near, 0))
    base_out[:, : 2 * width] = dot3(z, column_matrix)
    base_out[:, 2 * width :] = u
    applied = split(dot3(near, column_matrix))
    for k, out in enumerate((high_out, low_out)):
        chosen = dot(near[k], picker2).astype(BF16)
        for matrix, at, part in ((applied[k], 0, width), (chosen, 2 * width, rank)):
            out[:depth, at : at + 2 * part] = matrix
            out[depth:, at : at + part] = -matrix[:, part:]
            out[depth:, at + part : at + 2 * part] = matrix[:, :part]


def hold_kernel(static, out):
    out[...] = static[...]


def copy_kernel(value, *refs):
    out = refs[-1]
    out[...] = value[...]


def join_kernel(even, odd, u, row_out):
    first = lax.axis_index("box") % 2 == 0
    row_out[0] = jnp.where(first, odd[...], even[...])
    row_out[1] = u[...]
    row_out[2] = jnp.where(first, even[...], odd[...])


def message_kernel(even, middle, odd, base, high, low, keep_out, send_out):
    first = lax.axis_index("blk") % 2 == 0
    up = jnp.where(first, odd[...], even[...])
    down = jnp.where(first, even[...], odd[...])
    boxes = 2 * keep_out.shape[0]
    count = base.shape[0]
    width = keep_out.shape[2]
    rank = up.shape[1] // 2
    share = count // boxes
    half = share // 2
    order = (up[0], up[1], up[2], middle[0], middle[2], down[0], down[1], down[2])
    stacked = cat([v[:rank] for v in order] + [v[rank:] for v in order], 0)
    near = split(stacked.T)
    w = base[...] - dot3(near, (high[...], low[...]))
    lower = lax.axis_index("box") % 2 == 0
    for pair in range(boxes // 2):
        at = 2 * pair * share
        mine = w[at : at + share]
        other = w[at + share : at + 2 * share]
        for out, rows in (
            (keep_out, jnp.where(lower, mine, other)),
            (send_out, jnp.where(lower, other, mine)),
        ):
            out[pair, :share] = rows[:, :width]
            out[pair, share : 2 * share] = rows[:, width : 2 * width]
            t = rows[:, 2 * width :]
            out[pair, 2 * share : 2 * share + half] = cat([t[:half], t[half:]], 1)


def forward_kernel(count, keep, came, *refs):
    outs = refs[-count:]
    place = lax.axis_index("box") // 2
    for k, out in enumerate(outs):
        out[0] = keep[place ^ k]
        out[1] = came[place ^ k]


def blocks_of(refs):
    return [block for v in refs for block in ([v[k] for k in range(v.shape[0])] if len(v.shape) == 3 else [v[...]])]


def stacked_form(block, rank, depth):
    high, low = both(block, lambda part: columns_form(part[:rank, depth:], part[rank:, depth:]))
    return cat([high, high, low], 0)


def prepare_kernel(*refs):
    top_high, top_low, local_out = refs[-3:]
    depth = top_high.shape[1] // 2
    rank = local_out.shape[1] // 6
    for k, block in enumerate(blocks_of(refs[:-3])):
        at = slice(2 * k * rank, 2 * (k + 1) * rank)
        parts = split(block)
        for part, top_out in zip(parts, (top_high, top_low)):
            top_out[at] = rows_form(part[:rank, :depth], part[rank:, :depth])
        local_out[k] = stacked_form(parts, rank, depth)


def top_kernel(offsets, messages, top_high, top_low, prepared, *refs):
    pieces = refs[:messages]
    late = [split(block) for block in blocks_of(refs[messages:-2])]
    out, packed = refs[-2:]
    boxes = 2 * messages
    width = pieces[0].shape[2]
    share = out.shape[1]
    half = share // 2
    ready = prepared.shape[0]
    rank = prepared.shape[1] // 6
    rows = 2 * rank
    depth = boxes * rank
    me = lax.axis_index("box")
    top = [(top_high[...], top_low[...])]
    local = [prepared[k] for k in range(ready)]
    if late:
        top.append([
            cat([rows_form(v[k][:rank, :depth], v[k][rank:, :depth]) for v in late], 0) for k in range(2)
        ])
        local += [stacked_form(v, rank, depth) for v in late]
    for k in range(boxes):
        packed[me ^ k] = pieces[k // 2][k % 2, 2 * share : 2 * share + half]
    t_re = []
    t_im = []
    for box in range(boxes):
        t = cat([packed[box, :, :rows], packed[box, :, rows:]], 0)
        t_re.append(t[:, :rank])
        t_im.append(t[:, rank:])
    t = split(cat(t_re + t_im, 1))
    t_both = cat(t, 0)
    y = []
    for high, low in top:
        first = dot(t_both, high, NT)
        y.append(first[:share] + (first[share:] + dot(t[0], low, NT)))
    y = split(cat(y, 1))
    for k in range(boxes):
        at = slice(k * rows, (k + 1) * rows)
        x = dot(cat([y[0][:, at], y[1][:, at], y[0][:, at]], 1), local[k])
        offset = offsets[k]
        piece = pieces[offset // 2]
        at = pl.ds(pl.multiple_of((me ^ offset) * width, width), width)
        out[0, :, at] = piece[offset % 2, :share] + x[:, :width]
        out[1, :, at] = piece[offset % 2, share : 2 * share] + x[:, width:]


def call(kernel, outs, *arrays, hbm=(), copied=(), extra=(), cost=None):
    spaces = {i: pl.BlockSpec(memory_space=pl.ANY) for i in hbm}
    spaces.update({i: pl.BlockSpec(memory_space=pltpu.HBM) for i in copied})
    scratch = [pltpu.VMEM(arrays[i].shape, arrays[i].dtype) for i in copied]
    if scratch:
        scratch.append(pltpu.SemaphoreType.DMA((len(scratch),)))
    scratch += extra
    arrays = [pltpu.with_memory_space_constraint(v, pltpu.HBM) if i in copied else v for i, v in enumerate(arrays)]
    return pl.pallas_call(
        kernel,
        out_shape=[jax.ShapeDtypeStruct(shape, dtype) for shape, dtype in outs],
        in_specs=[spaces.get(i, VMEM) for i in range(len(arrays))],
        out_specs=[VMEM] * len(outs),
        scratch_shapes=scratch,
        cost_estimate=cost,
        compiler_params=pltpu.CompilerParams(vmem_limit_bytes=40 * 1024 * 1024),
    )(*arrays)


def swapped(value, axis, bit):
    return lax.ppermute(value, axis, [(i, i ^ bit) for i in range(lax.axis_size(axis))])


def beside(value, axis):
    count = lax.axis_size(axis)
    even = lax.ppermute(value, axis, [(i, i ^ 1) for i in range(count)])
    odd = lax.ppermute(value, axis, [(i, (i + 1) % count if i % 2 else (i - 1) % count) for i in range(count)])
    return even, odd


def on_device(surface_points, angle_ids, near_mask, skeleton, box_inverse_parts, near_coupling, top_inverse):
    boxes = lax.axis_size("box")
    width = box_inverse_parts.shape[2]
    count = angle_ids.shape[0]
    rank = skeleton.shape[1]
    sides = near_mask.shape[1]
    depth = top_inverse.shape[3]
    share = count // boxes
    u, static, high, low = call(
        field_kernel,
        [
            ((2 * rank, count), F32),
            ((2 * rank, depth + width), F32),
            ((count, 2 * width), BF16),
            ((count, 2 * width), BF16),
        ],
        surface_points, angle_ids.reshape(1, count), skeleton, box_inverse_parts, top_inverse,
        copied=range(5),
    )
    base, matrix_high, matrix_low = call(
        coupling_kernel,
        [
            ((count, 2 * width + 2 * rank), F32),
            ((2 * sides * rank, 2 * width + 2 * rank), BF16),
            ((2 * sides * rank, 2 * width + 2 * rank), BF16),
        ],
        high, low, skeleton, near_mask, box_inverse_parts, near_coupling,
        copied=range(2, 6), cost=COST,
    )
    even, odd = beside(u, "box")
    (row,) = call(join_kernel, [((3,) + u.shape, F32)], even, odd, u)
    (static,) = call(hold_kernel, [(static.shape, F32)], static, cost=COST)
    if boxes == 8:
        four, two, one = [swapped(static, "box", k) for k in (4, 2, 1)]
        (four,) = call(copy_kernel, [(static.shape, F32)], four, two, one, base, hbm=(1, 2, 3))
        five, six, three = swapped(four, "box", 1), swapped(four, "box", 2), swapped(one, "box", 2)
        early, late, waited = [static, four, two, one, five, six], [three], [five]
        offsets = (0, 4, 2, 1, 5, 6, 3, 7)
    else:
        early, late, waited = [static[None]], [], []
        offsets = [0]
        step = boxes // 2
        while step > 0:
            early.append(swapped(jnp.concatenate(early), "box", step))
            offsets += [k ^ step for k in offsets]
            step //= 2
    even, odd = beside(row, "blk")
    length = 2 * share + -(-share // 16) * 8
    message = ((boxes // 2, length, width), F32)
    keep, send = call(
        message_kernel, [message, message],
        even, row, odd, base, matrix_high, matrix_low,
        cost=COST,
    )
    pieces = call(
        functools.partial(forward_kernel, boxes // 2), [((2, length, width), F32)] * (boxes // 2),
        keep, swapped(send, "box", 1), *waited, hbm=range(2, 2 + len(waited)),
    )
    if late:
        (six,) = call(copy_kernel, [(six.shape, F32)], six, pieces[0], hbm=(1,))
        late.append(swapped(six, "box", 1))
    pieces = [pieces[0]] + [swapped(pieces[k], "box", 2 * k) for k in range(1, boxes // 2)]
    ready = 6 if late else boxes
    top = ((ready * 2 * rank, 2 * depth), BF16)
    local = ((ready, 6 * rank, 2 * width), BF16)
    prepared = call(prepare_kernel, [top, top, local], *early)
    (out,) = call(
        functools.partial(top_kernel, offsets, len(pieces)), [((2, share, boxes * width), F32)],
        *prepared, *pieces, *late,
        extra=[pltpu.VMEM((boxes, share // 2, width), F32)],
    )
    return out


def solution(mesh):
    return jax.shard_map(
        on_device,
        mesh=mesh,
        in_specs=(
            P(None, ("blk", "box")),
            P("batch"),
            P(("blk", "box"), None),
            P(("blk", "box"), None),
            P(("blk", "box"), None, None, None),
            P(("blk", "box"), None, None, None, None),
            P("blk", None, "box", None),
        ),
        out_specs=P(None, ("batch", "box"), "blk"),
        check_vma=False,
    )
```

```python
import functools

import jax
import jax.numpy as jnp
import numpy as np
from jax import lax
from jax.experimental import pallas as pl
from jax.experimental.pallas import tpu as pltpu
from jax.sharding import PartitionSpec as P

SWEEP = 16384
WAVENUMBER = 24.0
F32 = jnp.float32
BF16 = jnp.bfloat16
COST = pl.CostEstimate(flops=10**10, bytes_accessed=10**7, transcendentals=0)
VMEM = pl.BlockSpec(memory_space=pltpu.VMEM)
NN = (((1,), (0,)), ((), ()))
NT = (((1,), (1,)), ((), ()))
TN = (((0,), (0,)), ((), ()))

HALF_PI_1 = float(np.float32(201.0 / 128.0))
HALF_PI_2 = float(np.float32(np.round((np.pi / 2 - HALF_PI_1) * 2.0**22) / 2.0**22))
HALF_PI_3 = float(np.float32(np.pi / 2 - HALF_PI_1 - HALF_PI_2))


def cat(parts, axis):
    return jnp.concatenate(parts, axis=axis)


def dot(a, b, form=NN):
    return lax.dot_general(a, b, form, preferred_element_type=F32)


def split(x):
    high = x.astype(BF16)
    return high, (x - high.astype(F32)).astype(BF16)


def dot3(a, b, form=NN):
    return dot(a[0], b[0], form) + (dot(a[0], b[1], form) + dot(a[1], b[0], form))


def both(pair, function):
    return function(pair[0]), function(pair[1])


def sin_cos_small(r):
    s = r * r
    sin = r + r * s * (-1.6666654611e-1 + s * (8.3321608736e-3 - s * 1.9515295891e-4))
    cos = 1.0 - 0.5 * s + s * s * (4.166664568298827e-2 + s * (-1.388731625493765e-3 + s * 2.443315711809948e-5))
    return sin, cos


def by_quadrant(quadrant, sin, cos):
    odd = (quadrant & 1) == 1
    out_sin = jnp.where(odd, cos, sin)
    out_cos = jnp.where(odd, sin, cos)
    out_sin = jnp.where((quadrant & 2) == 2, -out_sin, out_sin)
    out_cos = jnp.where(((quadrant + 1) & 2) == 2, -out_cos, out_cos)
    return out_sin, out_cos


def one_hot(skeleton, width):
    rows = lax.broadcasted_iota(jnp.int32, (width, skeleton.shape[1]), 0)
    return jnp.where(rows == skeleton, 1.0, 0.0).astype(BF16)


def rows_form(re, im):
    return cat([cat([re, -im], 1), cat([im, re], 1)], 0)


def columns_form(re, im):
    return cat([cat([re, im], 1), cat([-im, re], 1)], 0)


def field_kernel(points_in, angles_in, skeleton_in, inverse_in, top_in, mask_in, u_out, static_out, high_out, low_out,
                 picker_out, mask_out, points, angles, skeleton, inverse, top, mask, sems):
    copies = [
        pltpu.make_async_copy(source, target, sems.at[k])
        for k, (source, target) in enumerate((
            (angles_in, angles), (points_in, points), (skeleton_in, skeleton), (inverse_in, inverse), (top_in, top),
            (mask_in, mask),
        ))
    ]
    for copy in copies:
        copy.start()
    count = angles.shape[1]
    width = points.shape[1]
    rank = skeleton.shape[1]
    copies[0].wait()
    ids = angles[...]
    quadrant = (ids + SWEEP // 8) >> (SWEEP.bit_length() - 3)
    rest = ids - quadrant * (SWEEP // 4)
    sin, cos = by_quadrant(quadrant, *sin_cos_small(rest.astype(F32) * (2.0 * np.pi / SWEEP)))
    pick = lax.broadcasted_iota(jnp.int32, (8, count), 0) == 0
    columns = jnp.where(pick, cos, sin).T
    cos_column = columns[:, 0:1]
    sin_column = columns[:, 1:2]
    copies[1].wait()
    x = points[0:1, :] * WAVENUMBER
    yz = points[1:2, :] * (0.6 * WAVENUMBER) + points[2:3, :] * (0.8 * WAVENUMBER)
    phase = x * cos_column + yz * sin_column
    turns = jnp.round(phase * (2.0 / np.pi))
    r = ((phase - turns * HALF_PI_1) - turns * HALF_PI_2) - turns * HALF_PI_3
    field_sin, field_cos = by_quadrant(turns.astype(jnp.int32), *sin_cos_small(r))
    field = split(cat([field_cos, field_sin], 1))
    high_out[...] = field[0]
    low_out[...] = field[1]
    copies[2].wait()
    picker = one_hot(skeleton[...], width)
    picker_out[...] = picker
    copies[5].wait()
    mask_out[...] = mask[...].astype(F32)
    copies[3].wait()
    parts = split(cat([inverse[0, 0], inverse[0, 1]], 1))
    rows = dot(picker, cat(parts, 1), TN)
    rows_high = rows[:, : 2 * width]
    rows_low = rows[:, 2 * width :]
    whole = rows_high + rows_low
    form = both((rows_high, rows_low), lambda v: rows_form(v[:, :width], v[:, width:]).astype(BF16))
    u_out[...] = dot3(form, field, NT)
    depth = top.shape[3]
    copies[4].wait()
    for part in range(2):
        at = slice(part * rank, (part + 1) * rank)
        static_out[at, :depth] = top[0, part]
        static_out[at, depth:] = whole[:, part * width : (part + 1) * width]


def coupling_kernel(high, low, picker_in, mask, inverse, coupling, base_out, high_out, low_out):
    width = inverse.shape[2]
    sides = coupling.shape[1]
    rank = coupling.shape[3]
    depth = sides * rank
    field = (high[...], low[...])
    re = split(inverse[0, 0])
    im = split(inverse[0, 1])
    row_matrix = (rows_form(re[0], im[0]), rows_form(re[1], im[1]))
    column_matrix = (columns_form(re[0], im[0]), columns_form(re[1], im[1]))
    picker = picker_in[...]
    zero = jnp.zeros_like(picker)
    picker2 = cat([cat([picker, zero], 1), cat([zero, picker], 1)], 0)
    z = split(dot3(field, row_matrix, NT))
    u = dot(z[0], picker2) + dot(z[1], picker2)
    near = []
    for side in range(sides):
        weight = mask[:, side : side + 1]
        near.append(cat([coupling[0, side, 0] * weight, coupling[0, side, 1] * weight], 1))
    near = split(cat(near, 0))
    base_out[:, : 2 * width] = dot3(z, column_matrix)
    base_out[:, 2 * width :] = u
    applied = split(dot3(near, column_matrix))
    for k, out in enumerate((high_out, low_out)):
        chosen = dot(near[k], picker2).astype(BF16)
        for matrix, at, part in ((applied[k], 0, width), (chosen, 2 * width, rank)):
            out[:depth, at : at + 2 * part] = matrix
            out[depth:, at : at + part] = -matrix[:, part:]
            out[depth:, at + part : at + 2 * part] = matrix[:, :part]


def hold_kernel(static, out):
    out[...] = static[...]


def copy_kernel(value, *refs):
    out = refs[-1]
    out[...] = value[...]


def join_kernel(even, odd, u, row_out):
    first = lax.axis_index("box") % 2 == 0
    row_out[0] = jnp.where(first, odd[...], even[...])
    row_out[1] = u[...]
    row_out[2] = jnp.where(first, even[...], odd[...])


def message_kernel(even, middle, odd, base, high, low, keep_out, send_out):
    first = lax.axis_index("blk") % 2 == 0
    up = jnp.where(first, odd[...], even[...])
    down = jnp.where(first, even[...], odd[...])
    boxes = 2 * keep_out.shape[0]
    count = base.shape[0]
    width = keep_out.shape[2]
    rank = up.shape[1] // 2
    share = count // boxes
    half = share // 2
    order = (up[0], up[1], up[2], middle[0], middle[2], down[0], down[1], down[2])
    stacked = cat([v[:rank] for v in order] + [v[rank:] for v in order], 0)
    near = split(stacked.T)
    w = base[...] - dot3(near, (high[...], low[...]))
    lower = lax.axis_index("box") % 2 == 0
    for pair in range(boxes // 2):
        at = 2 * pair * share
        mine = w[at : at + share]
        other = w[at + share : at + 2 * share]
        for out, rows in (
            (keep_out, jnp.where(lower, mine, other)),
            (send_out, jnp.where(lower, other, mine)),
        ):
            out[pair, :share] = rows[:, :width]
            out[pair, share : 2 * share] = rows[:, width : 2 * width]
            t = rows[:, 2 * width :]
            out[pair, 2 * share : 2 * share + half] = cat([t[:half], t[half:]], 1)


def forward_kernel(count, keep, came, *refs):
    outs = refs[-count:]
    place = lax.axis_index("box") // 2
    for k, out in enumerate(outs):
        out[0] = keep[place ^ k]
        out[1] = came[place ^ k]


def blocks_of(refs):
    return [block for v in refs for block in ([v[k] for k in range(v.shape[0])] if len(v.shape) == 3 else [v[...]])]


def stacked_form(block, rank, depth):
    high, low = both(block, lambda part: columns_form(part[:rank, depth:], part[rank:, depth:]))
    return cat([high, high, low], 0)


def prepare_kernel(*refs):
    top_high, top_low, local_out = refs[-3:]
    depth = top_high.shape[0] // 2
    rank = local_out.shape[1] // 6
    for k, block in enumerate(blocks_of(refs[:-3])):
        at = slice(2 * k * rank, 2 * (k + 1) * rank)
        re = block[:rank, :depth]
        im = block[rank:, :depth]
        high, low = split(cat([cat([re, im], 0).T, cat([-im, re], 0).T], 0))
        top_high[:, at] = high
        top_low[:, at] = low
        local_out[k] = stacked_form(split(block), rank, depth)


def top_kernel(offsets, top_high, top_low, local, *refs):
    pieces = refs[:-2][::-1]
    out, packed = refs[-2:]
    boxes = 2 * len(pieces)
    width = pieces[0].shape[2]
    share = out.shape[1]
    half = share // 2
    rank = local.shape[1] // 6
    rows = 2 * rank
    me = lax.axis_index("box")
    for k in range(boxes):
        packed[me ^ k] = pieces[k // 2][k % 2, 2 * share : 2 * share + half]
    t_re = []
    t_im = []
    for box in range(boxes):
        t = cat([packed[box, :, :rows], packed[box, :, rows:]], 0)
        t_re.append(t[:, :rank])
        t_im.append(t[:, rank:])
    t = split(cat(t_re + t_im, 1))
    first = dot(cat(t, 0), top_high[...])
    y = split(first[:share] + (first[share:] + dot(t[0], top_low[...])))
    for k in range(boxes):
        at = slice(k * rows, (k + 1) * rows)
        x = dot(cat([y[0][:, at], y[1][:, at], y[0][:, at]], 1), local[k])
        offset = offsets[k]
        piece = pieces[offset // 2]
        at = pl.ds(pl.multiple_of((me ^ offset) * width, width), width)
        out[0, :, at] = piece[offset % 2, :share] + x[:, :width]
        out[1, :, at] = piece[offset % 2, share : 2 * share] + x[:, width:]


def call(kernel, outs, *arrays, hbm=(), copied=(), extra=(), cost=None):
    spaces = {i: pl.BlockSpec(memory_space=pl.ANY) for i in hbm}
    spaces.update({i: pl.BlockSpec(memory_space=pltpu.HBM) for i in copied})
    scratch = [pltpu.VMEM(arrays[i].shape, arrays[i].dtype) for i in copied]
    if scratch:
        scratch.append(pltpu.SemaphoreType.DMA((len(scratch),)))
    scratch += extra
    arrays = [pltpu.with_memory_space_constraint(v, pltpu.HBM) if i in copied else v for i, v in enumerate(arrays)]
    return pl.pallas_call(
        kernel,
        out_shape=[jax.ShapeDtypeStruct(shape, dtype) for shape, dtype in outs],
        in_specs=[spaces.get(i, VMEM) for i in range(len(arrays))],
        out_specs=[VMEM] * len(outs),
        scratch_shapes=scratch,
        cost_estimate=cost,
        compiler_params=pltpu.CompilerParams(vmem_limit_bytes=40 * 1024 * 1024),
    )(*arrays)


def swapped(value, axis, bit):
    return lax.ppermute(value, axis, [(i, i ^ bit) for i in range(lax.axis_size(axis))])


def beside(value, axis):
    count = lax.axis_size(axis)
    even = lax.ppermute(value, axis, [(i, i ^ 1) for i in range(count)])
    odd = lax.ppermute(value, axis, [(i, (i + 1) % count if i % 2 else (i - 1) % count) for i in range(count)])
    return even, odd


def on_device(surface_points, angle_ids, near_mask, skeleton, box_inverse_parts, near_coupling, top_inverse):
    boxes = lax.axis_size("box")
    width = box_inverse_parts.shape[2]
    count = angle_ids.shape[0]
    rank = skeleton.shape[1]
    sides = near_mask.shape[1]
    depth = top_inverse.shape[3]
    share = count // boxes
    u, static, high, low, picker, mask = call(
        field_kernel,
        [
            ((2 * rank, count), F32),
            ((2 * rank, depth + width), F32),
            ((count, 2 * width), BF16),
            ((count, 2 * width), BF16),
            ((width, rank), BF16),
            (near_mask.shape, F32),
        ],
        surface_points, angle_ids.reshape(1, count), skeleton, box_inverse_parts, top_inverse,
        near_mask, copied=range(6),
    )
    base, matrix_high, matrix_low = call(
        coupling_kernel,
        [
            ((count, 2 * width + 2 * rank), F32),
            ((2 * sides * rank, 2 * width + 2 * rank), BF16),
            ((2 * sides * rank, 2 * width + 2 * rank), BF16),
        ],
        high, low, picker, mask, box_inverse_parts, near_coupling, cost=COST,
    )
    even, odd = beside(u, "box")
    (row,) = call(join_kernel, [((3,) + u.shape, F32)], even, odd, u)
    (static,) = call(hold_kernel, [(static.shape, F32)], static, cost=COST)
    if boxes == 8:
        four, two, one = [swapped(static, "box", k) for k in (4, 2, 1)]
        (four,) = call(copy_kernel, [(static.shape, F32)], four, two, one, base, hbm=(1, 2, 3))
        five, six, three = swapped(four, "box", 1), swapped(four, "box", 2), swapped(one, "box", 2)
        early, late, waited = [static, four, two, one, five, six], [three], [five]
        offsets = (0, 4, 2, 1, 5, 6, 3, 7)
    else:
        early, late, waited = [static[None]], [], []
        offsets = [0]
        step = boxes // 2
        while step > 0:
            early.append(swapped(jnp.concatenate(early), "box", step))
            offsets += [k ^ step for k in offsets]
            step //= 2
    even, odd = beside(row, "blk")
    length = 2 * share + -(-share // 16) * 8
    message = ((boxes // 2, length, width), F32)
    keep, send = call(
        message_kernel, [message, message],
        even, row, odd, base, matrix_high, matrix_low,
        cost=COST,
    )
    pieces = call(
        functools.partial(forward_kernel, boxes // 2), [((2, length, width), F32)] * (boxes // 2),
        keep, swapped(send, "box", 1), *waited, hbm=range(2, 2 + len(waited)),
    )
    if late:
        (six,) = call(copy_kernel, [(six.shape, F32)], six, pieces[0], hbm=(1,))
        late.append(swapped(six, "box", 1))
    pieces = [swapped(pieces[k], "box", 2 * k) for k in reversed(range(1, boxes // 2))] + [pieces[0]]
    top = ((2 * depth, 2 * depth), BF16)
    local = ((boxes, 6 * rank, 2 * width), BF16)
    prepared = call(prepare_kernel, [top, top, local], *early, *late)
    (out,) = call(
        functools.partial(top_kernel, offsets), [((2, share, boxes * width), F32)], *prepared, *pieces,
        extra=[pltpu.VMEM((boxes, share // 2, width), F32)],
    )
    return out


def solution(mesh):
    return jax.shard_map(
        on_device,
        mesh=mesh,
        in_specs=(
            P(None, ("blk", "box")),
            P("batch"),
            P(("blk", "box"), None),
            P(("blk", "box"), None),
            P(("blk", "box"), None, None, None),
            P(("blk", "box"), None, None, None, None),
            P("blk", None, "box", None),
        ),
        out_specs=P(None, ("batch", "box"), "blk"),
        check_vma=False,
    )
```

```python
import functools

import jax
import jax.numpy as jnp
import numpy as np
from jax import lax
from jax.experimental import pallas as pl
from jax.experimental.pallas import tpu as pltpu
from jax.sharding import PartitionSpec as P

SWEEP = 16384
WAVENUMBER = 24.0
F32 = jnp.float32
BF16 = jnp.bfloat16
COST = pl.CostEstimate(flops=10**10, bytes_accessed=10**7, transcendentals=0)
VMEM = pl.BlockSpec(memory_space=pltpu.VMEM)
NN = (((1,), (0,)), ((), ()))
NT = (((1,), (1,)), ((), ()))
TN = (((0,), (0,)), ((), ()))

HALF_PI_1 = float(np.float32(201.0 / 128.0))
HALF_PI_2 = float(np.float32(np.round((np.pi / 2 - HALF_PI_1) * 2.0**22) / 2.0**22))
HALF_PI_3 = float(np.float32(np.pi / 2 - HALF_PI_1 - HALF_PI_2))


def cat(parts, axis):
    return jnp.concatenate(parts, axis=axis)


def dot(a, b, form=NN):
    return lax.dot_general(a, b, form, preferred_element_type=F32)


def split(x):
    high = x.astype(BF16)
    return high, (x - high.astype(F32)).astype(BF16)


def dot3(a, b, form=NN):
    return dot(a[0], b[0], form) + (dot(a[0], b[1], form) + dot(a[1], b[0], form))


def both(pair, function):
    return function(pair[0]), function(pair[1])


def sin_cos_small(r):
    s = r * r
    sin = r + r * s * (-1.6666654611e-1 + s * (8.3321608736e-3 - s * 1.9515295891e-4))
    cos = 1.0 - 0.5 * s + s * s * (4.166664568298827e-2 + s * (-1.388731625493765e-3 + s * 2.443315711809948e-5))
    return sin, cos


def by_quadrant(quadrant, sin, cos):
    odd = (quadrant & 1) == 1
    out_sin = jnp.where(odd, cos, sin)
    out_cos = jnp.where(odd, sin, cos)
    out_sin = jnp.where((quadrant & 2) == 2, -out_sin, out_sin)
    out_cos = jnp.where(((quadrant + 1) & 2) == 2, -out_cos, out_cos)
    return out_sin, out_cos


def one_hot(skeleton, width):
    rows = lax.broadcasted_iota(jnp.int32, (width, skeleton.shape[1]), 0)
    return jnp.where(rows == skeleton, 1.0, 0.0).astype(BF16)


def rows_form(re, im):
    return cat([cat([re, -im], 1), cat([im, re], 1)], 0)


def columns_form(re, im):
    return cat([cat([re, im], 1), cat([-im, re], 1)], 0)


def field_kernel(points_in, angles_in, skeleton_in, inverse_in, top_in, mask_in, u_out, static_out, high_out, low_out,
                 picker_out, mask_out, points, angles, skeleton, inverse, top, mask, sems):
    copies = [
        pltpu.make_async_copy(source, target, sems.at[k])
        for k, (source, target) in enumerate((
            (angles_in, angles), (points_in, points), (skeleton_in, skeleton), (inverse_in, inverse), (top_in, top),
            (mask_in, mask),
        ))
    ]
    for copy in copies:
        copy.start()
    count = angles.shape[1]
    width = points.shape[1]
    rank = skeleton.shape[1]
    copies[0].wait()
    ids = angles[...]
    quadrant = (ids + SWEEP // 8) >> (SWEEP.bit_length() - 3)
    rest = ids - quadrant * (SWEEP // 4)
    sin, cos = by_quadrant(quadrant, *sin_cos_small(rest.astype(F32) * (2.0 * np.pi / SWEEP)))
    pick = lax.broadcasted_iota(jnp.int32, (8, count), 0) == 0
    columns = jnp.where(pick, cos, sin).T
    cos_column = columns[:, 0:1]
    sin_column = columns[:, 1:2]
    copies[1].wait()
    x = points[0:1, :] * WAVENUMBER
    yz = points[1:2, :] * (0.6 * WAVENUMBER) + points[2:3, :] * (0.8 * WAVENUMBER)
    phase = x * cos_column + yz * sin_column
    turns = jnp.round(phase * (2.0 / np.pi))
    r = ((phase - turns * HALF_PI_1) - turns * HALF_PI_2) - turns * HALF_PI_3
    field_sin, field_cos = by_quadrant(turns.astype(jnp.int32), *sin_cos_small(r))
    field = split(cat([field_cos, field_sin], 1))
    high_out[...] = field[0]
    low_out[...] = field[1]
    copies[2].wait()
    picker = one_hot(skeleton[...], width)
    picker_out[...] = picker
    copies[5].wait()
    mask_out[...] = mask[...].astype(F32)
    copies[3].wait()
    parts = split(cat([inverse[0, 0], inverse[0, 1]], 1))
    rows = dot(picker, cat(parts, 1), TN)
    rows_high = rows[:, : 2 * width]
    rows_low = rows[:, 2 * width :]
    whole = rows_high + rows_low
    form = both((rows_high, rows_low), lambda v: rows_form(v[:, :width], v[:, width:]).astype(BF16))
    u_out[...] = dot3(form, field, NT)
    depth = top.shape[3]
    copies[4].wait()
    for part in range(2):
        at = slice(part * rank, (part + 1) * rank)
        static_out[at, :depth] = top[0, part]
        static_out[at, depth:] = whole[:, part * width : (part + 1) * width]


def coupling_kernel(high, low, picker_in, mask, inverse, coupling, base_out, high_out, low_out):
    width = inverse.shape[2]
    sides = coupling.shape[1]
    rank = coupling.shape[3]
    depth = sides * rank
    field = (high[...], low[...])
    re = split(inverse[0, 0])
    im = split(inverse[0, 1])
    row_matrix = (rows_form(re[0], im[0]), rows_form(re[1], im[1]))
    column_matrix = (columns_form(re[0], im[0]), columns_form(re[1], im[1]))
    picker = picker_in[...]
    zero = jnp.zeros_like(picker)
    picker2 = cat([cat([picker, zero], 1), cat([zero, picker], 1)], 0)
    z = split(dot3(field, row_matrix, NT))
    u = dot(z[0], picker2) + dot(z[1], picker2)
    near = []
    for side in range(sides):
        weight = mask[:, side : side + 1]
        near.append(cat([coupling[0, side, 0] * weight, coupling[0, side, 1] * weight], 1))
    near = split(cat(near, 0))
    base_out[:, : 2 * width] = dot3(z, column_matrix)
    base_out[:, 2 * width :] = u
    applied = split(dot3(near, column_matrix))
    for k, out in enumerate((high_out, low_out)):
        chosen = dot(near[k], picker2).astype(BF16)
        for matrix, at, part in ((applied[k], 0, width), (chosen, 2 * width, rank)):
            out[:depth, at : at + 2 * part] = matrix
            out[depth:, at : at + part] = -matrix[:, part:]
            out[depth:, at + part : at + 2 * part] = matrix[:, :part]


def hold_kernel(static, out):
    out[...] = static[...]


def pack_kernel(four, two, one, base, four_out, pair_out):
    four_out[...] = four[...]
    pair_out[0] = two[...]
    pair_out[1] = four[...]


def copy_kernel(value, *refs):
    out = refs[-1]
    out[...] = value[...]


def join_kernel(even, odd, u, row_out):
    first = lax.axis_index("box") % 2 == 0
    row_out[0] = jnp.where(first, odd[...], even[...])
    row_out[1] = u[...]
    row_out[2] = jnp.where(first, even[...], odd[...])


def message_kernel(even, middle, odd, base, high, low, *refs):
    outs, natural = refs[:-1], refs[-1]
    first = lax.axis_index("blk") % 2 == 0
    up = jnp.where(first, odd[...], even[...])
    down = jnp.where(first, even[...], odd[...])
    boxes, _, width = natural.shape
    count = base.shape[0]
    rank = up.shape[1] // 2
    share = count // boxes
    half = share // 2
    order = (up[0], up[1], up[2], middle[0], middle[2], down[0], down[1], down[2])
    stacked = cat([v[:rank] for v in order] + [v[rank:] for v in order], 0)
    near = split(stacked.T)
    w = base[...] - dot3(near, (high[...], low[...]))
    for box in range(boxes):
        rows = w[box * share : (box + 1) * share]
        natural[box, :share] = rows[:, :width]
        natural[box, share : 2 * share] = rows[:, width : 2 * width]
        t = rows[:, 2 * width :]
        natural[box, 2 * share : 2 * share + half] = cat([t[:half], t[half:]], 1)
    me = lax.axis_index("box")
    for k in range(boxes):
        outs[k // 2][k % 2] = natural[me ^ k]


def forward_kernel(count, *refs):
    out = refs[-1]
    for k in range(count):
        out[k] = refs[k][1]


def blocks_of(refs):
    return [block for v in refs for block in ([v[k] for k in range(v.shape[0])] if len(v.shape) == 3 else [v[...]])]


def stacked_form(block, rank, depth):
    high, low = both(block, lambda part: columns_form(part[:rank, depth:], part[rank:, depth:]))
    return cat([high, high, low], 0)


def prepare_kernel(*refs):
    top_high, top_low, local_out = refs[-3:]
    depth = top_high.shape[1] // 2
    rank = local_out.shape[1] // 6
    for k, block in enumerate(blocks_of(refs[:-3])):
        at = slice(2 * k * rank, 2 * (k + 1) * rank)
        parts = split(block)
        for part, top_out in zip(parts, (top_high, top_low)):
            top_out[at] = rows_form(part[:rank, :depth], part[rank:, :depth])
        local_out[k] = stacked_form(parts, rank, depth)


def top_kernel(offsets, top_high, top_low, local, *refs):
    pieces = refs[:-3][::-1]
    came, out, packed = refs[-3:]
    boxes = 2 * len(pieces)
    width = came.shape[2]
    share = out.shape[1]
    half = share // 2
    rank = local.shape[1] // 6
    rows = 2 * rank
    me = lax.axis_index("box")
    for k in range(boxes):
        packed[me ^ k] = came[k // 2, 2 * share : 2 * share + half] if k % 2 else pieces[k // 2][0, 2 * share : 2 * share + half]
    t_re = []
    t_im = []
    for box in range(boxes):
        t = cat([packed[box, :, :rows], packed[box, :, rows:]], 0)
        t_re.append(t[:, :rank])
        t_im.append(t[:, rank:])
    t = split(cat(t_re + t_im, 1))
    first = dot(cat(t, 0), top_high[...], NT)
    y = split(first[:share] + (first[share:] + dot(t[0], top_low[...], NT)))
    for k in range(boxes):
        at = slice(k * rows, (k + 1) * rows)
        x = dot(cat([y[0][:, at], y[1][:, at], y[0][:, at]], 1), local[k])
        offset = offsets[k]
        piece, side = (came, offset // 2) if offset % 2 else (pieces[offset // 2], 0)
        at = pl.ds(pl.multiple_of((me ^ offset) * width, width), width)
        out[0, :, at] = piece[side, :share] + x[:, :width]
        out[1, :, at] = piece[side, share : 2 * share] + x[:, width:]


def call(kernel, outs, *arrays, hbm=(), copied=(), extra=(), cost=None):
    spaces = {i: pl.BlockSpec(memory_space=pl.ANY) for i in hbm}
    spaces.update({i: pl.BlockSpec(memory_space=pltpu.HBM) for i in copied})
    scratch = [pltpu.VMEM(arrays[i].shape, arrays[i].dtype) for i in copied]
    if scratch:
        scratch.append(pltpu.SemaphoreType.DMA((len(scratch),)))
    scratch += extra
    arrays = [pltpu.with_memory_space_constraint(v, pltpu.HBM) if i in copied else v for i, v in enumerate(arrays)]
    return pl.pallas_call(
        kernel,
        out_shape=[jax.ShapeDtypeStruct(shape, dtype) for shape, dtype in outs],
        in_specs=[spaces.get(i, VMEM) for i in range(len(arrays))],
        out_specs=[VMEM] * len(outs),
        scratch_shapes=scratch,
        cost_estimate=cost,
        compiler_params=pltpu.CompilerParams(vmem_limit_bytes=40 * 1024 * 1024),
    )(*arrays)


def swapped(value, axis, bit):
    return lax.ppermute(value, axis, [(i, i ^ bit) for i in range(lax.axis_size(axis))])


def beside(value, axis):
    count = lax.axis_size(axis)
    even = lax.ppermute(value, axis, [(i, i ^ 1) for i in range(count)])
    odd = lax.ppermute(value, axis, [(i, (i + 1) % count if i % 2 else (i - 1) % count) for i in range(count)])
    return even, odd


def on_device(surface_points, angle_ids, near_mask, skeleton, box_inverse_parts, near_coupling, top_inverse):
    boxes = lax.axis_size("box")
    width = box_inverse_parts.shape[2]
    count = angle_ids.shape[0]
    rank = skeleton.shape[1]
    sides = near_mask.shape[1]
    depth = top_inverse.shape[3]
    share = count // boxes
    u, static, high, low, picker, mask = call(
        field_kernel,
        [
            ((2 * rank, count), F32),
            ((2 * rank, depth + width), F32),
            ((count, 2 * width), BF16),
            ((count, 2 * width), BF16),
            ((width, rank), BF16),
            (near_mask.shape, F32),
        ],
        surface_points, angle_ids.reshape(1, count), skeleton, box_inverse_parts, top_inverse,
        near_mask, copied=range(6),
    )
    base, matrix_high, matrix_low = call(
        coupling_kernel,
        [
            ((count, 2 * width + 2 * rank), F32),
            ((2 * sides * rank, 2 * width + 2 * rank), BF16),
            ((2 * sides * rank, 2 * width + 2 * rank), BF16),
        ],
        high, low, picker, mask, box_inverse_parts, near_coupling, cost=COST,
    )
    even, odd = beside(u, "box")
    (row,) = call(join_kernel, [((3,) + u.shape, F32)], even, odd, u)
    (static,) = call(hold_kernel, [(static.shape, F32)], static, cost=COST)
    if boxes == 8:
        four = swapped(static, "box", 4)
        (again,) = call(hold_kernel, [(static.shape, F32)], static, cost=COST)
        two, one = swapped(again, "box", 2), swapped(again, "box", 1)
        four, pair = call(
            pack_kernel, [(static.shape, F32), ((2,) + static.shape, F32)], four, two, one, base, hbm=(2, 3)
        )
        six, others = swapped(four, "box", 2), swapped(pair, "box", 1)
        early, late, waited = [static, four, two, one, others, six], [], [others]
        offsets = (0, 4, 2, 1, 3, 5, 6, 7)
    else:
        early, late, waited = [static[None]], [], []
        offsets = [0]
        step = boxes // 2
        while step > 0:
            early.append(swapped(jnp.concatenate(early), "box", step))
            offsets += [k ^ step for k in offsets]
            step //= 2
    even, odd = beside(row, "blk")
    length = 2 * share + -(-share // 16) * 8
    pieces = call(
        message_kernel, [((2, length, width), F32)] * (boxes // 2),
        even, row, odd, base, matrix_high, matrix_low,
        cost=COST, extra=[pltpu.VMEM((boxes, length, width), F32)],
    )
    pieces = [swapped(pieces[k], "box", 2 * k) for k in reversed(range(1, boxes // 2))] + [pieces[0]]
    (send,) = call(
        functools.partial(forward_kernel, boxes // 2), [((boxes // 2, length, width), F32)],
        *pieces[::-1], *waited, hbm=range(boxes // 2, boxes // 2 + len(waited)),
    )
    came = swapped(send, "box", 1)
    if boxes == 8:
        (six,) = call(copy_kernel, [(six.shape, F32)], six, pieces[0], hbm=(1,))
        late.append(swapped(six, "box", 1))
    top = ((2 * depth, 2 * depth), BF16)
    local = ((boxes, 6 * rank, 2 * width), BF16)
    prepared = call(prepare_kernel, [top, top, local], *early, *late)
    (out,) = call(
        functools.partial(top_kernel, offsets), [((2, share, boxes * width), F32)], *prepared, *pieces, came,
        extra=[pltpu.VMEM((boxes, share // 2, width), F32)],
    )
    return out


def solution(mesh):
    return jax.shard_map(
        on_device,
        mesh=mesh,
        in_specs=(
            P(None, ("blk", "box")),
            P("batch"),
            P(("blk", "box"), None),
            P(("blk", "box"), None),
            P(("blk", "box"), None, None, None),
            P(("blk", "box"), None, None, None, None),
            P("blk", None, "box", None),
        ),
        out_specs=P(None, ("batch", "box"), "blk"),
        check_vma=False,
    )
```

```python
import functools

import jax
import jax.numpy as jnp
import numpy as np
from jax import lax
from jax.experimental import pallas as pl
from jax.experimental.pallas import tpu as pltpu
from jax.sharding import PartitionSpec as P

SWEEP = 16384
WAVENUMBER = 24.0
F32 = jnp.float32
BF16 = jnp.bfloat16
COST = pl.CostEstimate(flops=10**10, bytes_accessed=10**7, transcendentals=0)
VMEM = pl.BlockSpec(memory_space=pltpu.VMEM)
NN = (((1,), (0,)), ((), ()))
NT = (((1,), (1,)), ((), ()))
TN = (((0,), (0,)), ((), ()))

HALF_PI_1 = float(np.float32(201.0 / 128.0))
HALF_PI_2 = float(np.float32(np.round((np.pi / 2 - HALF_PI_1) * 2.0**22) / 2.0**22))
HALF_PI_3 = float(np.float32(np.pi / 2 - HALF_PI_1 - HALF_PI_2))


def cat(parts, axis):
    return jnp.concatenate(parts, axis=axis)


def dot(a, b, form=NN):
    return lax.dot_general(a, b, form, preferred_element_type=F32)


def split(x):
    high = x.astype(BF16)
    return high, (x - high.astype(F32)).astype(BF16)


def dot3(a, b, form=NN):
    return dot(a[0], b[0], form) + (dot(a[0], b[1], form) + dot(a[1], b[0], form))


def both(pair, function):
    return function(pair[0]), function(pair[1])


def sin_cos_small(r):
    s = r * r
    sin = r + r * s * (-1.6666654611e-1 + s * (8.3321608736e-3 - s * 1.9515295891e-4))
    cos = 1.0 - 0.5 * s + s * s * (4.166664568298827e-2 + s * (-1.388731625493765e-3 + s * 2.443315711809948e-5))
    return sin, cos


def by_quadrant(quadrant, sin, cos):
    odd = (quadrant & 1) == 1
    out_sin = jnp.where(odd, cos, sin)
    out_cos = jnp.where(odd, sin, cos)
    out_sin = jnp.where((quadrant & 2) == 2, -out_sin, out_sin)
    out_cos = jnp.where(((quadrant + 1) & 2) == 2, -out_cos, out_cos)
    return out_sin, out_cos


def one_hot(skeleton, width):
    rows = lax.broadcasted_iota(jnp.int32, (width, skeleton.shape[1]), 0)
    return jnp.where(rows == skeleton, 1.0, 0.0).astype(BF16)


def rows_form(re, im):
    return cat([cat([re, -im], 1), cat([im, re], 1)], 0)


def columns_form(re, im):
    return cat([cat([re, im], 1), cat([-im, re], 1)], 0)


def field_kernel(points_in, angles_in, skeleton_in, top_in, mask_in, inverse_in, coupling_in,
                 u_out, static_out, high_out, low_out, picker_out, mask_out, inverse, coupling,
                 points, angles, skeleton, top, mask, sems, more_sems):
    copies = [
        pltpu.make_async_copy(source, target, sems.at[k])
        for k, (source, target) in enumerate((
            (angles_in, angles), (points_in, points), (skeleton_in, skeleton), (top_in, top), (mask_in, mask),
        ))
    ]
    copies.append(pltpu.make_async_copy(inverse_in, inverse, more_sems.at[0]))
    copies.append(pltpu.make_async_copy(coupling_in, coupling, more_sems.at[1]))
    for copy in copies:
        copy.start()
    count = angles.shape[1]
    width = points.shape[1]
    rank = skeleton.shape[1]
    copies[0].wait()
    ids = angles[...]
    quadrant = (ids + SWEEP // 8) >> (SWEEP.bit_length() - 3)
    rest = ids - quadrant * (SWEEP // 4)
    sin, cos = by_quadrant(quadrant, *sin_cos_small(rest.astype(F32) * (2.0 * np.pi / SWEEP)))
    pick = lax.broadcasted_iota(jnp.int32, (8, count), 0) == 0
    columns = jnp.where(pick, cos, sin).T
    cos_column = columns[:, 0:1]
    sin_column = columns[:, 1:2]
    copies[1].wait()
    x = points[0:1, :] * WAVENUMBER
    yz = points[1:2, :] * (0.6 * WAVENUMBER) + points[2:3, :] * (0.8 * WAVENUMBER)
    phase = x * cos_column + yz * sin_column
    turns = jnp.round(phase * (2.0 / np.pi))
    r = ((phase - turns * HALF_PI_1) - turns * HALF_PI_2) - turns * HALF_PI_3
    field_sin, field_cos = by_quadrant(turns.astype(jnp.int32), *sin_cos_small(r))
    field = split(cat([field_cos, field_sin], 1))
    high_out[...] = field[0]
    low_out[...] = field[1]
    copies[2].wait()
    picker = one_hot(skeleton[...], width)
    picker_out[...] = picker
    copies[4].wait()
    mask_out[...] = mask[...].astype(F32)
    copies[5].wait()
    parts = split(cat([inverse[0, 0], inverse[0, 1]], 1))
    rows = dot(picker, cat(parts, 1), TN)
    rows_high = rows[:, : 2 * width]
    rows_low = rows[:, 2 * width :]
    whole = rows_high + rows_low
    form = both((rows_high, rows_low), lambda v: rows_form(v[:, :width], v[:, width:]).astype(BF16))
    u_out[...] = dot3(form, field, NT)
    depth = top.shape[3]
    copies[3].wait()
    for part in range(2):
        at = slice(part * rank, (part + 1) * rank)
        static_out[at, :depth] = top[0, part]
        static_out[at, depth:] = whole[:, part * width : (part + 1) * width]
    copies[6].wait()


def coupling_kernel(high, low, picker_in, mask, inverse, coupling, base_out, high_out, low_out):
    width = inverse.shape[2]
    sides = coupling.shape[1]
    rank = coupling.shape[3]
    depth = sides * rank
    field = (high[...], low[...])
    re = split(inverse[0, 0])
    im = split(inverse[0, 1])
    row_matrix = (rows_form(re[0], im[0]), rows_form(re[1], im[1]))
    column_matrix = (columns_form(re[0], im[0]), columns_form(re[1], im[1]))
    picker = picker_in[...]
    zero = jnp.zeros_like(picker)
    picker2 = cat([cat([picker, zero], 1), cat([zero, picker], 1)], 0)
    z = split(dot3(field, row_matrix, NT))
    u = dot(z[0], picker2) + dot(z[1], picker2)
    near = []
    for side in range(sides):
        weight = mask[:, side : side + 1]
        near.append(cat([coupling[0, side, 0] * weight, coupling[0, side, 1] * weight], 1))
    near = split(cat(near, 0))
    base_out[:, : 2 * width] = dot3(z, column_matrix)
    base_out[:, 2 * width :] = u
    applied = split(dot3(near, column_matrix))
    for k, out in enumerate((high_out, low_out)):
        chosen = dot(near[k], picker2).astype(BF16)
        for matrix, at, part in ((applied[k], 0, width), (chosen, 2 * width, rank)):
            out[:depth, at : at + 2 * part] = matrix
            out[depth:, at : at + part] = -matrix[:, part:]
            out[depth:, at + part : at + 2 * part] = matrix[:, :part]


def hold_kernel(static, before, out):
    out[...] = static[...]


def pack_kernel(four, two, one, four_out, pair_out):
    four_out[...] = four[...]
    pair_out[0] = two[...]
    pair_out[1] = four[...]


def copy_kernel(value, *refs):
    out = refs[-1]
    out[...] = value[1]


def join_kernel(odd, even, u, row_out):
    first = lax.axis_index("box") % 2 == 0
    row_out[0] = jnp.where(first, odd[...], even[...])
    row_out[1] = u[...]
    row_out[2] = jnp.where(first, even[...], odd[...])


def message_kernel(even, middle, odd, base, high, low, *refs):
    outs, natural = refs[:-1], refs[-1]
    first = lax.axis_index("blk") % 2 == 0
    up = jnp.where(first, odd[...], even[...])
    down = jnp.where(first, even[...], odd[...])
    boxes, _, width = natural.shape
    count = base.shape[0]
    rank = up.shape[1] // 2
    share = count // boxes
    half = share // 2
    order = (up[0], up[1], up[2], middle[0], middle[2], down[0], down[1], down[2])
    stacked = cat([v[:rank] for v in order] + [v[rank:] for v in order], 0)
    near = split(stacked.T)
    w = base[...] - dot3(near, (high[...], low[...]))
    for box in range(boxes):
        rows = w[box * share : (box + 1) * share]
        natural[box, :share] = rows[:, :width]
        natural[box, share : 2 * share] = rows[:, width : 2 * width]
        t = rows[:, 2 * width :]
        natural[box, 2 * share : 2 * share + half] = cat([t[:half], t[half:]], 1)
    me = lax.axis_index("box")
    for k in range(boxes):
        outs[k // 2][k % 2] = natural[me ^ k]


def forward_kernel(count, *refs):
    out = refs[-1]
    for k in range(count):
        out[k] = refs[k][1]


def blocks_of(refs):
    return [block for v in refs for block in ([v[k] for k in range(v.shape[0])] if len(v.shape) == 3 else [v[...]])]


def stacked_form(block, rank, depth):
    high, low = both(block, lambda part: columns_form(part[:rank, depth:], part[rank:, depth:]))
    return cat([high, high, low], 0)


def prepare_kernel(*refs):
    top_high, top_low, local_out = refs[-3:]
    depth = top_high.shape[1] // 2
    rank = local_out.shape[1] // 6
    for k, block in enumerate(blocks_of(refs[:-3])):
        at = slice(2 * k * rank, 2 * (k + 1) * rank)
        parts = split(block)
        for part, top_out in zip(parts, (top_high, top_low)):
            top_out[at] = rows_form(part[:rank, :depth], part[rank:, :depth])
        local_out[k] = stacked_form(parts, rank, depth)


def top_kernel(offsets, top_high, top_low, local, *refs):
    pieces = refs[:-3][::-1]
    came, out, packed = refs[-3:]
    boxes = 2 * len(pieces)
    width = came.shape[2]
    share = out.shape[1]
    half = share // 2
    rank = local.shape[1] // 6
    rows = 2 * rank
    me = lax.axis_index("box")
    for k in range(boxes):
        packed[me ^ k] = came[k // 2, 2 * share : 2 * share + half] if k % 2 else pieces[k // 2][0, 2 * share : 2 * share + half]
    t_re = []
    t_im = []
    for box in range(boxes):
        t = cat([packed[box, :, :rows], packed[box, :, rows:]], 0)
        t_re.append(t[:, :rank])
        t_im.append(t[:, rank:])
    t = split(cat(t_re + t_im, 1))
    first = dot(cat(t, 0), top_high[...], NT)
    y = split(first[:share] + (first[share:] + dot(t[0], top_low[...], NT)))
    for k in range(boxes):
        at = slice(k * rows, (k + 1) * rows)
        x = dot(cat([y[0][:, at], y[1][:, at], y[0][:, at]], 1), local[k])
        offset = offsets[k]
        piece, side = (came, offset // 2) if offset % 2 else (pieces[offset // 2], 0)
        at = pl.ds(pl.multiple_of((me ^ offset) * width, width), width)
        out[0, :, at] = piece[side, :share] + x[:, :width]
        out[1, :, at] = piece[side, share : 2 * share] + x[:, width:]


def call(kernel, outs, *arrays, hbm=(), copied=(), held=(), extra=(), cost=None):
    spaces = {i: pl.BlockSpec(memory_space=pl.ANY) for i in hbm}
    spaces.update({i: pl.BlockSpec(memory_space=pltpu.HBM) for i in (*copied, *held)})
    scratch = [pltpu.VMEM(arrays[i].shape, arrays[i].dtype) for i in copied]
    if scratch:
        scratch.append(pltpu.SemaphoreType.DMA((len(scratch),)))
    scratch += extra
    arrays = [pltpu.with_memory_space_constraint(v, pltpu.HBM) if i in (*copied, *held) else v for i, v in enumerate(arrays)]
    return pl.pallas_call(
        kernel,
        out_shape=[jax.ShapeDtypeStruct(shape, dtype) for shape, dtype in outs],
        in_specs=[spaces.get(i, VMEM) for i in range(len(arrays))],
        out_specs=[VMEM] * len(outs),
        scratch_shapes=scratch,
        cost_estimate=cost,
        compiler_params=pltpu.CompilerParams(vmem_limit_bytes=40 * 1024 * 1024),
    )(*arrays)


def swapped(value, axis, bit):
    return lax.ppermute(value, axis, [(i, i ^ bit) for i in range(lax.axis_size(axis))])


def beside(value, axis):
    count = lax.axis_size(axis)
    even = lax.ppermute(value, axis, [(i, i ^ 1) for i in range(count)])
    odd = lax.ppermute(value, axis, [(i, (i + 1) % count if i % 2 else (i - 1) % count) for i in range(count)])
    return even, odd


def on_device(surface_points, angle_ids, near_mask, skeleton, box_inverse_parts, near_coupling, top_inverse):
    boxes = lax.axis_size("box")
    width = box_inverse_parts.shape[2]
    count = angle_ids.shape[0]
    rank = skeleton.shape[1]
    sides = near_mask.shape[1]
    depth = top_inverse.shape[3]
    share = count // boxes
    u, static, high, low, picker, mask, inverse, coupling = call(
        field_kernel,
        [
            ((2 * rank, count), F32),
            ((2 * rank, depth + width), F32),
            ((count, 2 * width), BF16),
            ((count, 2 * width), BF16),
            ((width, rank), BF16),
            (near_mask.shape, F32),
            (box_inverse_parts.shape, F32),
            (near_coupling.shape, F32),
        ],
        surface_points, angle_ids.reshape(1, count), skeleton, top_inverse, near_mask,
        box_inverse_parts, near_coupling, copied=range(5), held=(5, 6), extra=[pltpu.SemaphoreType.DMA((2,))],
    )
    base, matrix_high, matrix_low = call(
        coupling_kernel,
        [
            ((count, 2 * width + 2 * rank), F32),
            ((2 * sides * rank, 2 * width + 2 * rank), BF16),
            ((2 * sides * rank, 2 * width + 2 * rank), BF16),
        ],
        high, low, picker, mask, inverse, coupling, cost=COST,
    )
    even, odd = beside(u, "box")
    (row,) = call(join_kernel, [((3,) + u.shape, F32)], odd, even, u)
    (static,) = call(hold_kernel, [(static.shape, F32)], static, base, hbm=(1,), cost=COST)
    if boxes == 8:
        four = swapped(static, "box", 4)
        (again,) = call(hold_kernel, [(static.shape, F32)], static, base, hbm=(1,), cost=COST)
        two, one = swapped(again, "box", 2), swapped(again, "box", 1)
        four, pair = call(
            pack_kernel, [(static.shape, F32), ((2,) + static.shape, F32)], four, two, one, hbm=(2,)
        )
        six, others = swapped(four, "box", 2), swapped(pair, "box", 1)
        early, late, waited = [static, four, two, one, others, six], [], [others, six]
        offsets = (0, 4, 2, 1, 3, 5, 6, 7)
    else:
        early, late, waited = [static[None]], [], []
        offsets = [0]
        step = boxes // 2
        while step > 0:
            early.append(swapped(jnp.concatenate(early), "box", step))
            offsets += [k ^ step for k in offsets]
            step //= 2
    even, odd = beside(row, "blk")
    length = 2 * share + -(-share // 16) * 8
    pieces = call(
        message_kernel, [((2, length, width), F32)] * (boxes // 2),
        even, row, odd, base, matrix_high, matrix_low,
        cost=COST, extra=[pltpu.VMEM((boxes, length, width), F32)],
    )
    pieces = [swapped(pieces[k], "box", 2 * k) for k in reversed(range(1, boxes // 2))] + [pieces[0]]
    (send,) = call(
        functools.partial(forward_kernel, boxes // 2), [((boxes // 2, length, width), F32)],
        *pieces[::-1], *waited, hbm=range(boxes // 2, boxes // 2 + len(waited)),
    )
    came = swapped(send, "box", 1)
    if boxes == 8:
        (five,) = call(copy_kernel, [(six.shape, F32)], others, pieces[0], hbm=(1,))
        late.append(swapped(five, "box", 2))
    top = ((2 * depth, 2 * depth), BF16)
    local = ((boxes, 6 * rank, 2 * width), BF16)
    prepared = call(prepare_kernel, [top, top, local], *early, *late)
    (out,) = call(
        functools.partial(top_kernel, offsets), [((2, share, boxes * width), F32)], *prepared, *pieces, came,
        extra=[pltpu.VMEM((boxes, share // 2, width), F32)],
    )
    return out


def solution(mesh):
    return jax.shard_map(
        on_device,
        mesh=mesh,
        in_specs=(
            P(None, ("blk", "box")),
            P("batch"),
            P(("blk", "box"), None),
            P(("blk", "box"), None),
            P(("blk", "box"), None, None, None),
            P(("blk", "box"), None, None, None, None),
            P("blk", None, "box", None),
        ),
        out_specs=P(None, ("batch", "box"), "blk"),
        check_vma=False,
    )
```

```python
import functools

import jax
import jax.numpy as jnp
import numpy as np
from jax import lax
from jax.experimental import pallas as pl
from jax.experimental.pallas import tpu as pltpu
from jax.sharding import PartitionSpec as P

SWEEP = 16384
WAVENUMBER = 24.0
F32 = jnp.float32
BF16 = jnp.bfloat16
COST = pl.CostEstimate(flops=10**10, bytes_accessed=10**7, transcendentals=0)
VMEM = pl.BlockSpec(memory_space=pltpu.VMEM)
NN = (((1,), (0,)), ((), ()))
NT = (((1,), (1,)), ((), ()))
TN = (((0,), (0,)), ((), ()))

HALF_PI_1 = float(np.float32(201.0 / 128.0))
HALF_PI_2 = float(np.float32(np.round((np.pi / 2 - HALF_PI_1) * 2.0**22) / 2.0**22))
HALF_PI_3 = float(np.float32(np.pi / 2 - HALF_PI_1 - HALF_PI_2))


def cat(parts, axis):
    return jnp.concatenate(parts, axis=axis)


def dot(a, b, form=NN):
    return lax.dot_general(a, b, form, preferred_element_type=F32)


def split(x):
    high = x.astype(BF16)
    return high, (x - high.astype(F32)).astype(BF16)


def dot3(a, b, form=NN):
    return dot(a[0], b[0], form) + (dot(a[0], b[1], form) + dot(a[1], b[0], form))


def both(pair, function):
    return function(pair[0]), function(pair[1])


def sin_cos_small(r):
    s = r * r
    sin = r + r * s * (-1.6666654611e-1 + s * (8.3321608736e-3 - s * 1.9515295891e-4))
    cos = 1.0 - 0.5 * s + s * s * (4.166664568298827e-2 + s * (-1.388731625493765e-3 + s * 2.443315711809948e-5))
    return sin, cos


def by_quadrant(quadrant, sin, cos):
    odd = (quadrant & 1) == 1
    out_sin = jnp.where(odd, cos, sin)
    out_cos = jnp.where(odd, sin, cos)
    out_sin = jnp.where((quadrant & 2) == 2, -out_sin, out_sin)
    out_cos = jnp.where(((quadrant + 1) & 2) == 2, -out_cos, out_cos)
    return out_sin, out_cos


def one_hot(skeleton, width):
    rows = lax.broadcasted_iota(jnp.int32, (width, skeleton.shape[1]), 0)
    return jnp.where(rows == skeleton, 1.0, 0.0).astype(BF16)


def rows_form(re, im):
    return cat([cat([re, -im], 1), cat([im, re], 1)], 0)


def columns_form(re, im):
    return cat([cat([re, im], 1), cat([-im, re], 1)], 0)


def field_kernel(points_in, angles_in, skeleton_in, top_in, mask_in, inverse_in, coupling_in,
                 u_out, static_out, high_out, low_out, picker_out, mask_out, inverse, coupling,
                 points, angles, skeleton, top, mask, sems, more_sems):
    copies = [
        pltpu.make_async_copy(source, target, sems.at[k])
        for k, (source, target) in enumerate((
            (angles_in, angles), (points_in, points), (skeleton_in, skeleton), (top_in, top), (mask_in, mask),
        ))
    ]
    copies.append(pltpu.make_async_copy(inverse_in, inverse, more_sems.at[0]))
    copies.append(pltpu.make_async_copy(coupling_in, coupling, more_sems.at[1]))
    for copy in copies:
        copy.start()
    count = angles.shape[1]
    width = points.shape[1]
    rank = skeleton.shape[1]
    copies[0].wait()
    ids = angles[...]
    quadrant = (ids + SWEEP // 8) >> (SWEEP.bit_length() - 3)
    rest = ids - quadrant * (SWEEP // 4)
    sin, cos = by_quadrant(quadrant, *sin_cos_small(rest.astype(F32) * (2.0 * np.pi / SWEEP)))
    pick = lax.broadcasted_iota(jnp.int32, (8, count), 0) == 0
    columns = jnp.where(pick, cos, sin).T
    cos_column = columns[:, 0:1]
    sin_column = columns[:, 1:2]
    copies[1].wait()
    x = points[0:1, :] * WAVENUMBER
    yz = points[1:2, :] * (0.6 * WAVENUMBER) + points[2:3, :] * (0.8 * WAVENUMBER)
    phase = x * cos_column + yz * sin_column
    turns = jnp.round(phase * (2.0 / np.pi))
    r = ((phase - turns * HALF_PI_1) - turns * HALF_PI_2) - turns * HALF_PI_3
    field_sin, field_cos = by_quadrant(turns.astype(jnp.int32), *sin_cos_small(r))
    field = split(cat([field_cos, field_sin], 1))
    high_out[...] = field[0]
    low_out[...] = field[1]
    copies[2].wait()
    picker = one_hot(skeleton[...], width)
    picker_out[...] = picker
    copies[4].wait()
    mask_out[...] = mask[...].astype(F32)
    copies[5].wait()
    parts = split(cat([inverse[0, 0], inverse[0, 1]], 1))
    rows = dot(picker, cat(parts, 1), TN)
    rows_high = rows[:, : 2 * width]
    rows_low = rows[:, 2 * width :]
    whole = rows_high + rows_low
    form = both((rows_high, rows_low), lambda v: rows_form(v[:, :width], v[:, width:]).astype(BF16))
    u_out[...] = dot3(form, field, NT)
    depth = top.shape[3]
    copies[3].wait()
    for part in range(2):
        at = slice(part * rank, (part + 1) * rank)
        static_out[at, :depth] = top[0, part]
        static_out[at, depth:] = whole[:, part * width : (part + 1) * width]
    copies[6].wait()


def coupling_kernel(high, low, picker_in, mask, inverse, coupling, base_out, high_out, low_out):
    width = inverse.shape[2]
    sides = coupling.shape[1]
    rank = coupling.shape[3]
    depth = sides * rank
    field = (high[...], low[...])
    re = split(inverse[0, 0])
    im = split(inverse[0, 1])
    row_matrix = (rows_form(re[0], im[0]), rows_form(re[1], im[1]))
    column_matrix = (columns_form(re[0], im[0]), columns_form(re[1], im[1]))
    picker = picker_in[...]
    zero = jnp.zeros_like(picker)
    picker2 = cat([cat([picker, zero], 1), cat([zero, picker], 1)], 0)
    z = split(dot3(field, row_matrix, NT))
    u = dot(z[0], picker2) + dot(z[1], picker2)
    near = []
    for side in range(sides):
        weight = mask[:, side : side + 1]
        near.append(cat([coupling[0, side, 0] * weight, coupling[0, side, 1] * weight], 1))
    near = split(cat(near, 0))
    base_out[:, : 2 * width] = dot3(z, column_matrix)
    base_out[:, 2 * width :] = u
    applied = split(dot3(near, column_matrix))
    for k, out in enumerate((high_out, low_out)):
        chosen = dot(near[k], picker2).astype(BF16)
        for matrix, at, part in ((applied[k], 0, width), (chosen, 2 * width, rank)):
            out[:depth, at : at + 2 * part] = matrix
            out[depth:, at : at + part] = -matrix[:, part:]
            out[depth:, at + part : at + 2 * part] = matrix[:, :part]


def hold_kernel(static, out):
    out[...] = static[...]


def pack_kernel(four, two, one, base, four_out, pair_out):
    four_out[...] = four[...]
    pair_out[0] = two[...]
    pair_out[1] = four[...]


def copy_kernel(value, *refs):
    out = refs[-1]
    out[...] = value[1]


def join_kernel(even, odd, u, row_out):
    first = lax.axis_index("box") % 2 == 0
    row_out[0] = jnp.where(first, odd[...], even[...])
    row_out[1] = u[...]
    row_out[2] = jnp.where(first, even[...], odd[...])


def message_kernel(even, middle, odd, base, high, low, *refs):
    outs, natural = refs[:-1], refs[-1]
    first = lax.axis_index("blk") % 2 == 0
    up = jnp.where(first, odd[...], even[...])
    down = jnp.where(first, even[...], odd[...])
    boxes, _, width = natural.shape
    count = base.shape[0]
    rank = up.shape[1] // 2
    share = count // boxes
    half = share // 2
    order = (up[0], up[1], up[2], middle[0], middle[2], down[0], down[1], down[2])
    stacked = cat([v[:rank] for v in order] + [v[rank:] for v in order], 0)
    near = split(stacked.T)
    w = base[...] - dot3(near, (high[...], low[...]))
    for box in range(boxes):
        rows = w[box * share : (box + 1) * share]
        natural[box, :share] = rows[:, :width]
        natural[box, share : 2 * share] = rows[:, width : 2 * width]
        t = rows[:, 2 * width :]
        natural[box, 2 * share : 2 * share + half] = cat([t[:half], t[half:]], 1)
    me = lax.axis_index("box")
    for k in range(boxes):
        outs[k // 2][k % 2] = natural[me ^ k]


def forward_kernel(count, *refs):
    out = refs[-1]
    for k in range(count):
        out[k] = refs[k][1]


def blocks_of(refs):
    return [block for v in refs for block in ([v[k] for k in range(v.shape[0])] if len(v.shape) == 3 else [v[...]])]


def stacked_form(block, rank, depth):
    high, low = both(block, lambda part: columns_form(part[:rank, depth:], part[rank:, depth:]))
    return cat([high, high, low], 0)


def prepare_kernel(*refs):
    top_high, top_low, local_out = refs[-3:]
    depth = top_high.shape[1] // 2
    rank = local_out.shape[1] // 6
    for k, block in enumerate(blocks_of(refs[:-3])):
        at = slice(2 * k * rank, 2 * (k + 1) * rank)
        parts = split(block)
        for part, top_out in zip(parts, (top_high, top_low)):
            top_out[at] = rows_form(part[:rank, :depth], part[rank:, :depth])
        local_out[k] = stacked_form(parts, rank, depth)


def top_kernel(offsets, top_high, top_low, local, *refs):
    pieces = refs[:-3][::-1]
    came, out, packed = refs[-3:]
    boxes = 2 * len(pieces)
    width = came.shape[2]
    share = out.shape[1]
    half = share // 2
    rank = local.shape[1] // 6
    rows = 2 * rank
    me = lax.axis_index("box")
    for k in range(boxes):
        packed[me ^ k] = came[k // 2, 2 * share : 2 * share + half] if k % 2 else pieces[k // 2][0, 2 * share : 2 * share + half]
    t_re = []
    t_im = []
    for box in range(boxes):
        t = cat([packed[box, :, :rows], packed[box, :, rows:]], 0)
        t_re.append(t[:, :rank])
        t_im.append(t[:, rank:])
    t = split(cat(t_re + t_im, 1))
    first = dot(cat(t, 0), top_high[...], NT)
    y = split(first[:share] + (first[share:] + dot(t[0], top_low[...], NT)))
    for k in range(boxes):
        at = slice(k * rows, (k + 1) * rows)
        x = dot(cat([y[0][:, at], y[1][:, at], y[0][:, at]], 1), local[k])
        offset = offsets[k]
        piece, side = (came, offset // 2) if offset % 2 else (pieces[offset // 2], 0)
        at = pl.ds(pl.multiple_of((me ^ offset) * width, width), width)
        out[0, :, at] = piece[side, :share] + x[:, :width]
        out[1, :, at] = piece[side, share : 2 * share] + x[:, width:]


def call(kernel, outs, *arrays, hbm=(), copied=(), held=(), extra=(), cost=None):
    spaces = {i: pl.BlockSpec(memory_space=pl.ANY) for i in hbm}
    spaces.update({i: pl.BlockSpec(memory_space=pltpu.HBM) for i in (*copied, *held)})
    scratch = [pltpu.VMEM(arrays[i].shape, arrays[i].dtype) for i in copied]
    if scratch:
        scratch.append(pltpu.SemaphoreType.DMA((len(scratch),)))
    scratch += extra
    arrays = [pltpu.with_memory_space_constraint(v, pltpu.HBM) if i in (*copied, *held) else v for i, v in enumerate(arrays)]
    return pl.pallas_call(
        kernel,
        out_shape=[jax.ShapeDtypeStruct(shape, dtype) for shape, dtype in outs],
        in_specs=[spaces.get(i, VMEM) for i in range(len(arrays))],
        out_specs=[VMEM] * len(outs),
        scratch_shapes=scratch,
        cost_estimate=cost,
        compiler_params=pltpu.CompilerParams(vmem_limit_bytes=40 * 1024 * 1024),
    )(*arrays)


def swapped(value, axis, bit):
    return lax.ppermute(value, axis, [(i, i ^ bit) for i in range(lax.axis_size(axis))])


def beside(value, axis):
    count = lax.axis_size(axis)
    even = lax.ppermute(value, axis, [(i, i ^ 1) for i in range(count)])
    odd = lax.ppermute(value, axis, [(i, (i + 1) % count if i % 2 else (i - 1) % count) for i in range(count)])
    return even, odd


def on_device(surface_points, angle_ids, near_mask, skeleton, box_inverse_parts, near_coupling, top_inverse):
    boxes = lax.axis_size("box")
    width = box_inverse_parts.shape[2]
    count = angle_ids.shape[0]
    rank = skeleton.shape[1]
    sides = near_mask.shape[1]
    depth = top_inverse.shape[3]
    share = count // boxes
    u, static, high, low, picker, mask, inverse, coupling = call(
        field_kernel,
        [
            ((2 * rank, count), F32),
            ((2 * rank, depth + width), F32),
            ((count, 2 * width), BF16),
            ((count, 2 * width), BF16),
            ((width, rank), BF16),
            (near_mask.shape, F32),
            (box_inverse_parts.shape, F32),
            (near_coupling.shape, F32),
        ],
        surface_points, angle_ids.reshape(1, count), skeleton, top_inverse, near_mask,
        box_inverse_parts, near_coupling, copied=range(5), held=(5, 6), extra=[pltpu.SemaphoreType.DMA((2,))],
    )
    base, matrix_high, matrix_low = call(
        coupling_kernel,
        [
            ((count, 2 * width + 2 * rank), F32),
            ((2 * sides * rank, 2 * width + 2 * rank), BF16),
            ((2 * sides * rank, 2 * width + 2 * rank), BF16),
        ],
        high, low, picker, mask, inverse, coupling, cost=COST,
    )
    even, odd = beside(u, "box")
    (row,) = call(join_kernel, [((3,) + u.shape, F32)], even, odd, u)
    (static,) = call(hold_kernel, [(static.shape, F32)], static, cost=COST)
    if boxes == 8:
        four = swapped(static, "box", 4)
        (again,) = call(hold_kernel, [(static.shape, F32)], static, cost=COST)
        two, one = swapped(again, "box", 2), swapped(again, "box", 1)
        four, pair = call(
            pack_kernel, [(static.shape, F32), ((2,) + static.shape, F32)], four, two, one, base, hbm=(2, 3)
        )
        six, others = swapped(four, "box", 2), swapped(pair, "box", 1)
        early, late, waited = [static, four, two, one, others, six], [], [others]
        offsets = (0, 4, 2, 1, 3, 5, 6, 7)
    else:
        early, late, waited = [static[None]], [], []
        offsets = [0]
        step = boxes // 2
        while step > 0:
            early.append(swapped(jnp.concatenate(early), "box", step))
            offsets += [k ^ step for k in offsets]
            step //= 2
    even, odd = beside(row, "blk")
    length = 2 * share + -(-share // 16) * 8
    pieces = call(
        message_kernel, [((2, length, width), F32)] * (boxes // 2),
        even, row, odd, base, matrix_high, matrix_low,
        cost=COST, extra=[pltpu.VMEM((boxes, length, width), F32)],
    )
    pieces = [swapped(pieces[k], "box", 2 * k) for k in reversed(range(1, boxes // 2))] + [pieces[0]]
    (send,) = call(
        functools.partial(forward_kernel, boxes // 2), [((boxes // 2, length, width), F32)],
        *pieces[::-1], *waited, hbm=range(boxes // 2, boxes // 2 + len(waited)),
    )
    came = swapped(send, "box", 1)
    if boxes == 8:
        (five,) = call(copy_kernel, [(six.shape, F32)], others, pieces[0], hbm=(1,))
        late.append(swapped(five, "box", 2))
    top = ((2 * depth, 2 * depth), BF16)
    local = ((boxes, 6 * rank, 2 * width), BF16)
    prepared = call(prepare_kernel, [top, top, local], *early, *late)
    (out,) = call(
        functools.partial(top_kernel, offsets), [((2, share, boxes * width), F32)], *prepared, *pieces, came,
        extra=[pltpu.VMEM((boxes, share // 2, width), F32)],
    )
    return out


def solution(mesh):
    return jax.shard_map(
        on_device,
        mesh=mesh,
        in_specs=(
            P(None, ("blk", "box")),
            P("batch"),
            P(("blk", "box"), None),
            P(("blk", "box"), None),
            P(("blk", "box"), None, None, None),
            P(("blk", "box"), None, None, None, None),
            P("blk", None, "box", None),
        ),
        out_specs=P(None, ("batch", "box"), "blk"),
        check_vma=False,
    )
```

```python
import functools

import jax
import jax.numpy as jnp
import numpy as np
from jax import lax
from jax.experimental import pallas as pl
from jax.experimental.pallas import tpu as pltpu
from jax.sharding import PartitionSpec as P

SWEEP = 16384
WAVENUMBER = 24.0
F32 = jnp.float32
BF16 = jnp.bfloat16
COST = pl.CostEstimate(flops=10**10, bytes_accessed=10**7, transcendentals=0)
VMEM = pl.BlockSpec(memory_space=pltpu.VMEM)
NN = (((1,), (0,)), ((), ()))
NT = (((1,), (1,)), ((), ()))
TN = (((0,), (0,)), ((), ()))

HALF_PI_1 = float(np.float32(201.0 / 128.0))
HALF_PI_2 = float(np.float32(np.round((np.pi / 2 - HALF_PI_1) * 2.0**22) / 2.0**22))
HALF_PI_3 = float(np.float32(np.pi / 2 - HALF_PI_1 - HALF_PI_2))


def cat(parts, axis):
    return jnp.concatenate(parts, axis=axis)


def dot(a, b, form=NN):
    return lax.dot_general(a, b, form, preferred_element_type=F32)


def split(x):
    high = x.astype(BF16)
    return high, (x - high.astype(F32)).astype(BF16)


def dot3(a, b, form=NN):
    return dot(a[0], b[0], form) + (dot(a[0], b[1], form) + dot(a[1], b[0], form))


def both(pair, function):
    return function(pair[0]), function(pair[1])


def sin_cos_small(r):
    s = r * r
    sin = r + r * s * (-1.6666654611e-1 + s * (8.3321608736e-3 - s * 1.9515295891e-4))
    cos = 1.0 - 0.5 * s + s * s * (4.166664568298827e-2 + s * (-1.388731625493765e-3 + s * 2.443315711809948e-5))
    return sin, cos


def by_quadrant(quadrant, sin, cos):
    odd = (quadrant & 1) == 1
    out_sin = jnp.where(odd, cos, sin)
    out_cos = jnp.where(odd, sin, cos)
    out_sin = jnp.where((quadrant & 2) == 2, -out_sin, out_sin)
    out_cos = jnp.where(((quadrant + 1) & 2) == 2, -out_cos, out_cos)
    return out_sin, out_cos


def one_hot(skeleton, width):
    rows = lax.broadcasted_iota(jnp.int32, (width, skeleton.shape[1]), 0)
    return jnp.where(rows == skeleton, 1.0, 0.0).astype(BF16)


def rows_form(re, im):
    return cat([cat([re, -im], 1), cat([im, re], 1)], 0)


def columns_form(re, im):
    return cat([cat([re, im], 1), cat([-im, re], 1)], 0)


def field_kernel(points_in, angles_in, skeleton_in, top_in, mask_in, inverse_in, coupling_in,
                 u_out, static_out, high_out, low_out, picker_out, mask_out, inverse, coupling,
                 points, angles, skeleton, top, mask, sems, more_sems):
    copies = [
        pltpu.make_async_copy(source, target, sems.at[k])
        for k, (source, target) in enumerate((
            (angles_in, angles), (points_in, points), (skeleton_in, skeleton), (top_in, top), (mask_in, mask),
        ))
    ]
    copies.append(pltpu.make_async_copy(inverse_in, inverse, more_sems.at[0]))
    copies.append(pltpu.make_async_copy(coupling_in, coupling, more_sems.at[1]))
    for copy in copies:
        copy.start()
    count = angles.shape[1]
    width = points.shape[1]
    rank = skeleton.shape[1]
    copies[0].wait()
    ids = angles[...]
    quadrant = (ids + SWEEP // 8) >> (SWEEP.bit_length() - 3)
    rest = ids - quadrant * (SWEEP // 4)
    sin, cos = by_quadrant(quadrant, *sin_cos_small(rest.astype(F32) * (2.0 * np.pi / SWEEP)))
    pick = lax.broadcasted_iota(jnp.int32, (8, count), 0) == 0
    columns = jnp.where(pick, cos, sin).T
    cos_column = columns[:, 0:1]
    sin_column = columns[:, 1:2]
    copies[1].wait()
    x = points[0:1, :] * WAVENUMBER
    yz = points[1:2, :] * (0.6 * WAVENUMBER) + points[2:3, :] * (0.8 * WAVENUMBER)
    phase = x * cos_column + yz * sin_column
    turns = jnp.round(phase * (2.0 / np.pi))
    r = ((phase - turns * HALF_PI_1) - turns * HALF_PI_2) - turns * HALF_PI_3
    field_sin, field_cos = by_quadrant(turns.astype(jnp.int32), *sin_cos_small(r))
    field = split(cat([field_cos, field_sin], 1))
    high_out[...] = field[0]
    low_out[...] = field[1]
    copies[2].wait()
    picker = one_hot(skeleton[...], width)
    picker_out[...] = picker
    copies[4].wait()
    mask_out[...] = mask[...].astype(F32)
    copies[5].wait()
    parts = split(cat([inverse[0, 0], inverse[0, 1]], 1))
    rows = dot(picker, cat(parts, 1), TN)
    rows_high = rows[:, : 2 * width]
    rows_low = rows[:, 2 * width :]
    whole = rows_high + rows_low
    form = both((rows_high, rows_low), lambda v: rows_form(v[:, :width], v[:, width:]).astype(BF16))
    u_out[...] = dot3(form, field, NT)
    depth = top.shape[3]
    copies[3].wait()
    for part in range(2):
        at = slice(part * rank, (part + 1) * rank)
        static_out[at, :depth] = top[0, part]
        static_out[at, depth:] = whole[:, part * width : (part + 1) * width]
    copies[6].wait()


def coupling_kernel(high, low, picker_in, mask, inverse, coupling, base_out, high_out, low_out):
    width = inverse.shape[2]
    sides = coupling.shape[1]
    rank = coupling.shape[3]
    depth = sides * rank
    field = (high[...], low[...])
    re = split(inverse[0, 0])
    im = split(inverse[0, 1])
    row_matrix = (rows_form(re[0], im[0]), rows_form(re[1], im[1]))
    column_matrix = (columns_form(re[0], im[0]), columns_form(re[1], im[1]))
    picker = picker_in[...]
    zero = jnp.zeros_like(picker)
    picker2 = cat([cat([picker, zero], 1), cat([zero, picker], 1)], 0)
    z = split(dot3(field, row_matrix, NT))
    u = dot(z[0], picker2) + dot(z[1], picker2)
    near = []
    for side in range(sides):
        weight = mask[:, side : side + 1]
        near.append(cat([coupling[0, side, 0] * weight, coupling[0, side, 1] * weight], 1))
    near = split(cat(near, 0))
    base_out[:, : 2 * width] = dot3(z, column_matrix)
    base_out[:, 2 * width :] = u
    applied = split(dot3(near, column_matrix))
    for k, out in enumerate((high_out, low_out)):
        chosen = dot(near[k], picker2).astype(BF16)
        for matrix, at, part in ((applied[k], 0, width), (chosen, 2 * width, rank)):
            out[:depth, at : at + 2 * part] = matrix
            out[depth:, at : at + part] = -matrix[:, part:]
            out[depth:, at + part : at + 2 * part] = matrix[:, :part]


def hold_kernel(static, out):
    out[...] = static[...]


def pack_kernel(one, base, four, two, four_out, pair_out):
    four_out[...] = four[...]
    pair_out[0] = two[...]
    pair_out[1] = four[...]


def copy_kernel(value, *refs):
    out = refs[-1]
    out[...] = value[1]


def join_kernel(even, odd, u, row_out):
    first = lax.axis_index("box") % 2 == 0
    row_out[0] = jnp.where(first, odd[...], even[...])
    row_out[1] = u[...]
    row_out[2] = jnp.where(first, even[...], odd[...])


def message_kernel(even, middle, odd, base, high, low, *refs):
    outs, natural = refs[:-1], refs[-1]
    first = lax.axis_index("blk") % 2 == 0
    up = jnp.where(first, odd[...], even[...])
    down = jnp.where(first, even[...], odd[...])
    boxes, _, width = natural.shape
    count = base.shape[0]
    rank = up.shape[1] // 2
    share = count // boxes
    half = share // 2
    order = (up[0], up[1], up[2], middle[0], middle[2], down[0], down[1], down[2])
    stacked = cat([v[:rank] for v in order] + [v[rank:] for v in order], 0)
    near = split(stacked.T)
    w = base[...] - dot3(near, (high[...], low[...]))
    for box in range(boxes):
        rows = w[box * share : (box + 1) * share]
        natural[box, :share] = rows[:, :width]
        natural[box, share : 2 * share] = rows[:, width : 2 * width]
        t = rows[:, 2 * width :]
        natural[box, 2 * share : 2 * share + half] = cat([t[:half], t[half:]], 1)
    me = lax.axis_index("box")
    for k in range(boxes):
        outs[k // 2][k % 2] = natural[me ^ k]


def forward_kernel(order, *refs):
    out = refs[-1]
    for k, piece in zip(order, refs):
        out[k] = piece[1]


def blocks_of(refs):
    return [block for v in refs for block in ([v[k] for k in range(v.shape[0])] if len(v.shape) == 3 else [v[...]])]


def stacked_form(block, rank, depth):
    high, low = both(block, lambda part: columns_form(part[:rank, depth:], part[rank:, depth:]))
    return cat([high, high, low], 0)


def prepare_kernel(*refs):
    top_high, top_low, local_out = refs[-3:]
    depth = top_high.shape[1] // 2
    rank = local_out.shape[1] // 6
    for k, block in enumerate(blocks_of(refs[:-3])):
        at = slice(2 * k * rank, 2 * (k + 1) * rank)
        parts = split(block)
        for part, top_out in zip(parts, (top_high, top_low)):
            top_out[at] = rows_form(part[:rank, :depth], part[rank:, :depth])
        local_out[k] = stacked_form(parts, rank, depth)


def top_kernel(offsets, order, top_high, top_low, local, *refs):
    pieces = dict(zip(order, refs))
    came, out, packed = refs[-3:]
    boxes = 2 * len(pieces)
    width = came.shape[2]
    share = out.shape[1]
    half = share // 2
    rank = local.shape[1] // 6
    rows = 2 * rank
    me = lax.axis_index("box")
    for k in range(boxes):
        packed[me ^ k] = came[k // 2, 2 * share : 2 * share + half] if k % 2 else pieces[k // 2][0, 2 * share : 2 * share + half]
    t_re = []
    t_im = []
    for box in range(boxes):
        t = cat([packed[box, :, :rows], packed[box, :, rows:]], 0)
        t_re.append(t[:, :rank])
        t_im.append(t[:, rank:])
    t = split(cat(t_re + t_im, 1))
    first = dot(cat(t, 0), top_high[...], NT)
    y = split(first[:share] + (first[share:] + dot(t[0], top_low[...], NT)))
    for k in range(boxes):
        at = slice(k * rows, (k + 1) * rows)
        x = dot(cat([y[0][:, at], y[1][:, at], y[0][:, at]], 1), local[k])
        offset = offsets[k]
        piece, side = (came, offset // 2) if offset % 2 else (pieces[offset // 2], 0)
        at = pl.ds(pl.multiple_of((me ^ offset) * width, width), width)
        out[0, :, at] = piece[side, :share] + x[:, :width]
        out[1, :, at] = piece[side, share : 2 * share] + x[:, width:]


def call(kernel, outs, *arrays, hbm=(), copied=(), held=(), extra=(), cost=None):
    spaces = {i: pl.BlockSpec(memory_space=pl.ANY) for i in hbm}
    spaces.update({i: pl.BlockSpec(memory_space=pltpu.HBM) for i in (*copied, *held)})
    scratch = [pltpu.VMEM(arrays[i].shape, arrays[i].dtype) for i in copied]
    if scratch:
        scratch.append(pltpu.SemaphoreType.DMA((len(scratch),)))
    scratch += extra
    arrays = [pltpu.with_memory_space_constraint(v, pltpu.HBM) if i in (*copied, *held) else v for i, v in enumerate(arrays)]
    return pl.pallas_call(
        kernel,
        out_shape=[jax.ShapeDtypeStruct(shape, dtype) for shape, dtype in outs],
        in_specs=[spaces.get(i, VMEM) for i in range(len(arrays))],
        out_specs=[VMEM] * len(outs),
        scratch_shapes=scratch,
        cost_estimate=cost,
        compiler_params=pltpu.CompilerParams(vmem_limit_bytes=40 * 1024 * 1024),
    )(*arrays)


def swapped(value, axis, bit):
    return lax.ppermute(value, axis, [(i, i ^ bit) for i in range(lax.axis_size(axis))])


def beside(value, axis):
    count = lax.axis_size(axis)
    even = lax.ppermute(value, axis, [(i, i ^ 1) for i in range(count)])
    odd = lax.ppermute(value, axis, [(i, (i + 1) % count if i % 2 else (i - 1) % count) for i in range(count)])
    return even, odd


def on_device(surface_points, angle_ids, near_mask, skeleton, box_inverse_parts, near_coupling, top_inverse):
    boxes = lax.axis_size("box")
    width = box_inverse_parts.shape[2]
    count = angle_ids.shape[0]
    rank = skeleton.shape[1]
    sides = near_mask.shape[1]
    depth = top_inverse.shape[3]
    share = count // boxes
    u, static, high, low, picker, mask, inverse, coupling = call(
        field_kernel,
        [
            ((2 * rank, count), F32),
            ((2 * rank, depth + width), F32),
            ((count, 2 * width), BF16),
            ((count, 2 * width), BF16),
            ((width, rank), BF16),
            (near_mask.shape, F32),
            (box_inverse_parts.shape, F32),
            (near_coupling.shape, F32),
        ],
        surface_points, angle_ids.reshape(1, count), skeleton, top_inverse, near_mask,
        box_inverse_parts, near_coupling, copied=range(5), held=(5, 6), extra=[pltpu.SemaphoreType.DMA((2,))],
    )
    base, matrix_high, matrix_low = call(
        coupling_kernel,
        [
            ((count, 2 * width + 2 * rank), F32),
            ((2 * sides * rank, 2 * width + 2 * rank), BF16),
            ((2 * sides * rank, 2 * width + 2 * rank), BF16),
        ],
        high, low, picker, mask, inverse, coupling, cost=COST,
    )
    even, odd = beside(u, "box")
    (row,) = call(join_kernel, [((3,) + u.shape, F32)], even, odd, u)
    (static,) = call(hold_kernel, [(static.shape, F32)], static, cost=COST)
    if boxes == 8:
        one = swapped(static, "box", 1)
        (again,) = call(hold_kernel, [(static.shape, F32)], static, cost=COST)
        four, two = swapped(again, "box", 4), swapped(again, "box", 2)
        four, pair = call(
            pack_kernel, [(static.shape, F32), ((2,) + static.shape, F32)], one, base, four, two, hbm=(0, 1)
        )
        six, others = swapped(four, "box", 2), swapped(pair, "box", 1)
        early, late, waited = [static, one, four, two, others, six], [], [others]
        offsets = (0, 1, 4, 2, 3, 5, 6, 7)
    else:
        early, late, waited = [static[None]], [], []
        offsets = [0]
        step = boxes // 2
        while step > 0:
            early.append(swapped(jnp.concatenate(early), "box", step))
            offsets += [k ^ step for k in offsets]
            step //= 2
    even, odd = beside(row, "blk")
    length = 2 * share + -(-share // 16) * 8
    pieces = call(
        message_kernel, [((2, length, width), F32)] * (boxes // 2),
        even, row, odd, base, matrix_high, matrix_low,
        cost=COST, extra=[pltpu.VMEM((boxes, length, width), F32)],
    )
    order = (2, 3, 1) if boxes == 8 else tuple(range(1, boxes // 2))
    pieces = {0: pieces[0], **{k: swapped(pieces[k], "box", 2 * k) for k in order}}
    order += (0,)
    (send,) = call(
        functools.partial(forward_kernel, order), [((boxes // 2, length, width), F32)],
        *[pieces[k] for k in order], *waited, hbm=range(boxes // 2, boxes // 2 + len(waited)),
    )
    came = swapped(send, "box", 1)
    if boxes == 8:
        (five,) = call(copy_kernel, [(six.shape, F32)], others, pieces[order[0]], hbm=(1,))
        late.append(swapped(five, "box", 2))
    top = ((2 * depth, 2 * depth), BF16)
    local = ((boxes, 6 * rank, 2 * width), BF16)
    prepared = call(prepare_kernel, [top, top, local], *early, *late)
    (out,) = call(
        functools.partial(top_kernel, offsets, order), [((2, share, boxes * width), F32)], *prepared, *[pieces[k] for k in order], came,
        extra=[pltpu.VMEM((boxes, share // 2, width), F32)],
    )
    return out


def solution(mesh):
    return jax.shard_map(
        on_device,
        mesh=mesh,
        in_specs=(
            P(None, ("blk", "box")),
            P("batch"),
            P(("blk", "box"), None),
            P(("blk", "box"), None),
            P(("blk", "box"), None, None, None),
            P(("blk", "box"), None, None, None, None),
            P("blk", None, "box", None),
        ),
        out_specs=P(None, ("batch", "box"), "blk"),
        check_vma=False,
    )
```

```python
import functools

import jax
import jax.numpy as jnp
import numpy as np
from jax import lax
from jax.experimental import pallas as pl
from jax.experimental.pallas import tpu as pltpu
from jax.sharding import PartitionSpec as P

SWEEP = 16384
WAVENUMBER = 24.0
F32 = jnp.float32
BF16 = jnp.bfloat16
COST = pl.CostEstimate(flops=10**10, bytes_accessed=10**7, transcendentals=0)
VMEM = pl.BlockSpec(memory_space=pltpu.VMEM)
NN = (((1,), (0,)), ((), ()))
NT = (((1,), (1,)), ((), ()))
TN = (((0,), (0,)), ((), ()))

HALF_PI_1 = float(np.float32(201.0 / 128.0))
HALF_PI_2 = float(np.float32(np.round((np.pi / 2 - HALF_PI_1) * 2.0**22) / 2.0**22))
HALF_PI_3 = float(np.float32(np.pi / 2 - HALF_PI_1 - HALF_PI_2))


def cat(parts, axis):
    return jnp.concatenate(parts, axis=axis)


def dot(a, b, form=NN):
    return lax.dot_general(a, b, form, preferred_element_type=F32)


def split(x):
    high = x.astype(BF16)
    return high, (x - high.astype(F32)).astype(BF16)


def dot3(a, b, form=NN):
    return dot(a[0], b[0], form) + (dot(a[0], b[1], form) + dot(a[1], b[0], form))


def both(pair, function):
    return function(pair[0]), function(pair[1])


def sin_cos_small(r):
    s = r * r
    sin = r + r * s * (-1.6666654611e-1 + s * (8.3321608736e-3 - s * 1.9515295891e-4))
    cos = 1.0 - 0.5 * s + s * s * (4.166664568298827e-2 + s * (-1.388731625493765e-3 + s * 2.443315711809948e-5))
    return sin, cos


def by_quadrant(quadrant, sin, cos):
    odd = (quadrant & 1) == 1
    out_sin = jnp.where(odd, cos, sin)
    out_cos = jnp.where(odd, sin, cos)
    out_sin = jnp.where((quadrant & 2) == 2, -out_sin, out_sin)
    out_cos = jnp.where(((quadrant + 1) & 2) == 2, -out_cos, out_cos)
    return out_sin, out_cos


def one_hot(skeleton, width):
    rows = lax.broadcasted_iota(jnp.int32, (width, skeleton.shape[1]), 0)
    return jnp.where(rows == skeleton, 1.0, 0.0).astype(BF16)


def rows_form(re, im):
    return cat([cat([re, -im], 1), cat([im, re], 1)], 0)


def columns_form(re, im):
    return cat([cat([re, im], 1), cat([-im, re], 1)], 0)


def field_kernel(points_in, angles_in, skeleton_in, top_in, mask_in, inverse_in, coupling_in,
                 u_out, static_out, high_out, low_out, picker_out, mask_out, inverse, coupling,
                 points, angles, skeleton, top, mask, sems, more_sems):
    copies = [
        pltpu.make_async_copy(source, target, sems.at[k])
        for k, (source, target) in enumerate((
            (angles_in, angles), (points_in, points), (skeleton_in, skeleton), (top_in, top), (mask_in, mask),
        ))
    ]
    copies.append(pltpu.make_async_copy(inverse_in, inverse, more_sems.at[0]))
    copies.append(pltpu.make_async_copy(coupling_in, coupling, more_sems.at[1]))
    for copy in copies:
        copy.start()
    count = angles.shape[1]
    width = points.shape[1]
    rank = skeleton.shape[1]
    copies[0].wait()
    ids = angles[...]
    quadrant = (ids + SWEEP // 8) >> (SWEEP.bit_length() - 3)
    rest = ids - quadrant * (SWEEP // 4)
    sin, cos = by_quadrant(quadrant, *sin_cos_small(rest.astype(F32) * (2.0 * np.pi / SWEEP)))
    pick = lax.broadcasted_iota(jnp.int32, (8, count), 0) == 0
    columns = jnp.where(pick, cos, sin).T
    cos_column = columns[:, 0:1]
    sin_column = columns[:, 1:2]
    copies[1].wait()
    x = points[0:1, :] * WAVENUMBER
    yz = points[1:2, :] * (0.6 * WAVENUMBER) + points[2:3, :] * (0.8 * WAVENUMBER)
    phase = x * cos_column + yz * sin_column
    turns = jnp.round(phase * (2.0 / np.pi))
    r = ((phase - turns * HALF_PI_1) - turns * HALF_PI_2) - turns * HALF_PI_3
    field_sin, field_cos = by_quadrant(turns.astype(jnp.int32), *sin_cos_small(r))
    field = split(cat([field_cos, field_sin], 1))
    high_out[...] = field[0]
    low_out[...] = field[1]
    copies[2].wait()
    picker = one_hot(skeleton[...], width)
    picker_out[...] = picker
    copies[4].wait()
    mask_out[...] = mask[...].astype(F32)
    copies[5].wait()
    parts = split(cat([inverse[0, 0], inverse[0, 1]], 1))
    rows = dot(picker, cat(parts, 1), TN)
    rows_high = rows[:, : 2 * width]
    rows_low = rows[:, 2 * width :]
    whole = rows_high + rows_low
    form = both((rows_high, rows_low), lambda v: rows_form(v[:, :width], v[:, width:]).astype(BF16))
    u_out[...] = dot3(form, field, NT)
    depth = top.shape[3]
    copies[3].wait()
    for part in range(2):
        at = slice(part * rank, (part + 1) * rank)
        static_out[at, :depth] = top[0, part]
        static_out[at, depth:] = whole[:, part * width : (part + 1) * width]
    copies[6].wait()


def coupling_kernel(high, low, picker_in, mask, inverse, coupling, base_out, high_out, low_out):
    width = inverse.shape[2]
    sides = coupling.shape[1]
    rank = coupling.shape[3]
    depth = sides * rank
    field = (high[...], low[...])
    re = split(inverse[0, 0])
    im = split(inverse[0, 1])
    row_matrix = (rows_form(re[0], im[0]), rows_form(re[1], im[1]))
    column_matrix = (columns_form(re[0], im[0]), columns_form(re[1], im[1]))
    picker = picker_in[...]
    zero = jnp.zeros_like(picker)
    picker2 = cat([cat([picker, zero], 1), cat([zero, picker], 1)], 0)
    z = split(dot3(field, row_matrix, NT))
    u = dot(z[0], picker2) + dot(z[1], picker2)
    near = []
    for side in range(sides):
        weight = mask[:, side : side + 1]
        near.append(cat([coupling[0, side, 0] * weight, coupling[0, side, 1] * weight], 1))
    near = split(cat(near, 0))
    base_out[:, : 2 * width] = dot3(z, column_matrix)
    base_out[:, 2 * width :] = u
    applied = split(dot3(near, column_matrix))
    for k, out in enumerate((high_out, low_out)):
        chosen = dot(near[k], picker2).astype(BF16)
        for matrix, at, part in ((applied[k], 0, width), (chosen, 2 * width, rank)):
            out[:depth, at : at + 2 * part] = matrix
            out[depth:, at : at + part] = -matrix[:, part:]
            out[depth:, at + part : at + 2 * part] = matrix[:, :part]


def hold_kernel(static, out):
    out[...] = static[...]


def pack_kernel(four, two, one, base, four_out, pair_out):
    four_out[...] = four[...]
    pair_out[0] = two[...]
    pair_out[1] = four[...]


def copy_kernel(value, *refs):
    out = refs[-1]
    out[...] = value[1]


def join_kernel(odd, even, u, row_out):
    first = lax.axis_index("box") % 2 == 0
    row_out[0] = jnp.where(first, odd[...], even[...])
    row_out[1] = u[...]
    row_out[2] = jnp.where(first, even[...], odd[...])


def message_kernel(even, middle, odd, base, high, low, *refs):
    outs, natural = refs[:-1], refs[-1]
    first = lax.axis_index("blk") % 2 == 0
    up = jnp.where(first, odd[...], even[...])
    down = jnp.where(first, even[...], odd[...])
    boxes, _, width = natural.shape
    count = base.shape[0]
    rank = up.shape[1] // 2
    share = count // boxes
    half = share // 2
    order = (up[0], up[1], up[2], middle[0], middle[2], down[0], down[1], down[2])
    stacked = cat([v[:rank] for v in order] + [v[rank:] for v in order], 0)
    near = split(stacked.T)
    w = base[...] - dot3(near, (high[...], low[...]))
    for box in range(boxes):
        rows = w[box * share : (box + 1) * share]
        natural[box, :share] = rows[:, :width]
        natural[box, share : 2 * share] = rows[:, width : 2 * width]
        t = rows[:, 2 * width :]
        natural[box, 2 * share : 2 * share + half] = cat([t[:half], t[half:]], 1)
    me = lax.axis_index("box")
    for k in range(boxes):
        outs[k // 2][k % 2] = natural[me ^ k]


def forward_kernel(count, *refs):
    out = refs[-1]
    for k in range(count):
        out[k] = refs[k][1]


def blocks_of(refs):
    return [block for v in refs for block in ([v[k] for k in range(v.shape[0])] if len(v.shape) == 3 else [v[...]])]


def stacked_form(block, rank, depth):
    high, low = both(block, lambda part: columns_form(part[:rank, depth:], part[rank:, depth:]))
    return cat([high, high, low], 0)


def prepare_kernel(*refs):
    top_high, top_low, local_out = refs[-3:]
    depth = top_high.shape[1] // 2
    rank = local_out.shape[1] // 6
    for k, block in enumerate(blocks_of(refs[:-3])):
        at = slice(2 * k * rank, 2 * (k + 1) * rank)
        parts = split(block)
        for part, top_out in zip(parts, (top_high, top_low)):
            top_out[at] = rows_form(part[:rank, :depth], part[rank:, :depth])
        local_out[k] = stacked_form(parts, rank, depth)


def top_kernel(offsets, top_high, top_low, local, *refs):
    pieces = refs[:-3][::-1]
    came, out, packed = refs[-3:]
    boxes = 2 * len(pieces)
    width = came.shape[2]
    share = out.shape[1]
    half = share // 2
    rank = local.shape[1] // 6
    rows = 2 * rank
    me = lax.axis_index("box")
    for k in range(boxes):
        packed[me ^ k] = came[k // 2, 2 * share : 2 * share + half] if k % 2 else pieces[k // 2][0, 2 * share : 2 * share + half]
    t_re = []
    t_im = []
    for box in range(boxes):
        t = cat([packed[box, :, :rows], packed[box, :, rows:]], 0)
        t_re.append(t[:, :rank])
        t_im.append(t[:, rank:])
    t = split(cat(t_re + t_im, 1))
    first = dot(cat(t, 0), top_high[...], NT)
    y = split(first[:share] + (first[share:] + dot(t[0], top_low[...], NT)))
    for k in range(boxes):
        at = slice(k * rows, (k + 1) * rows)
        x = dot(cat([y[0][:, at], y[1][:, at], y[0][:, at]], 1), local[k])
        offset = offsets[k]
        piece, side = (came, offset // 2) if offset % 2 else (pieces[offset // 2], 0)
        at = pl.ds(pl.multiple_of((me ^ offset) * width, width), width)
        out[0, :, at] = piece[side, :share] + x[:, :width]
        out[1, :, at] = piece[side, share : 2 * share] + x[:, width:]


def call(kernel, outs, *arrays, hbm=(), copied=(), held=(), extra=(), cost=None):
    spaces = {i: pl.BlockSpec(memory_space=pl.ANY) for i in hbm}
    spaces.update({i: pl.BlockSpec(memory_space=pltpu.HBM) for i in (*copied, *held)})
    scratch = [pltpu.VMEM(arrays[i].shape, arrays[i].dtype) for i in copied]
    if scratch:
        scratch.append(pltpu.SemaphoreType.DMA((len(scratch),)))
    scratch += extra
    arrays = [pltpu.with_memory_space_constraint(v, pltpu.HBM) if i in (*copied, *held) else v for i, v in enumerate(arrays)]
    return pl.pallas_call(
        kernel,
        out_shape=[jax.ShapeDtypeStruct(shape, dtype) for shape, dtype in outs],
        in_specs=[spaces.get(i, VMEM) for i in range(len(arrays))],
        out_specs=[VMEM] * len(outs),
        scratch_shapes=scratch,
        cost_estimate=cost,
        compiler_params=pltpu.CompilerParams(vmem_limit_bytes=40 * 1024 * 1024),
    )(*arrays)


def swapped(value, axis, bit):
    return lax.ppermute(value, axis, [(i, i ^ bit) for i in range(lax.axis_size(axis))])


def beside(value, axis):
    count = lax.axis_size(axis)
    even = lax.ppermute(value, axis, [(i, i ^ 1) for i in range(count)])
    odd = lax.ppermute(value, axis, [(i, (i + 1) % count if i % 2 else (i - 1) % count) for i in range(count)])
    return even, odd


def on_device(surface_points, angle_ids, near_mask, skeleton, box_inverse_parts, near_coupling, top_inverse):
    boxes = lax.axis_size("box")
    width = box_inverse_parts.shape[2]
    count = angle_ids.shape[0]
    rank = skeleton.shape[1]
    sides = near_mask.shape[1]
    depth = top_inverse.shape[3]
    share = count // boxes
    u, static, high, low, picker, mask, inverse, coupling = call(
        field_kernel,
        [
            ((2 * rank, count), F32),
            ((2 * rank, depth + width), F32),
            ((count, 2 * width), BF16),
            ((count, 2 * width), BF16),
            ((width, rank), BF16),
            (near_mask.shape, F32),
            (box_inverse_parts.shape, F32),
            (near_coupling.shape, F32),
        ],
        surface_points, angle_ids.reshape(1, count), skeleton, top_inverse, near_mask,
        box_inverse_parts, near_coupling, copied=range(5), held=(5, 6), extra=[pltpu.SemaphoreType.DMA((2,))],
    )
    base, matrix_high, matrix_low = call(
        coupling_kernel,
        [
            ((count, 2 * width + 2 * rank), F32),
            ((2 * sides * rank, 2 * width + 2 * rank), BF16),
            ((2 * sides * rank, 2 * width + 2 * rank), BF16),
        ],
        high, low, picker, mask, inverse, coupling, cost=COST,
    )
    even, odd = beside(u, "box")
    (row,) = call(join_kernel, [((3,) + u.shape, F32)], odd, even, u)
    (static,) = call(hold_kernel, [(static.shape, F32)], static, cost=COST)
    if boxes == 8:
        four = swapped(static, "box", 4)
        (again,) = call(hold_kernel, [(static.shape, F32)], static, cost=COST)
        two, one = swapped(again, "box", 2), swapped(again, "box", 1)
        four, pair = call(
            pack_kernel, [(static.shape, F32), ((2,) + static.shape, F32)], four, two, one, base, hbm=(2, 3)
        )
        six, others = swapped(four, "box", 2), swapped(pair, "box", 1)
        early, late, waited = [static, four, two, one, others, six], [], [others]
        offsets = (0, 4, 2, 1, 3, 5, 6, 7)
    else:
        early, late, waited = [static[None]], [], []
        offsets = [0]
        step = boxes // 2
        while step > 0:
            early.append(swapped(jnp.concatenate(early), "box", step))
            offsets += [k ^ step for k in offsets]
            step //= 2
    even, odd = beside(row, "blk")
    length = 2 * share + -(-share // 16) * 8
    pieces = call(
        message_kernel, [((2, length, width), F32)] * (boxes // 2),
        even, row, odd, base, matrix_high, matrix_low,
        cost=COST, extra=[pltpu.VMEM((boxes, length, width), F32)],
    )
    pieces = [swapped(pieces[k], "box", 2 * k) for k in reversed(range(1, boxes // 2))] + [pieces[0]]
    (send,) = call(
        functools.partial(forward_kernel, boxes // 2), [((boxes // 2, length, width), F32)],
        *pieces[::-1], *waited, hbm=range(boxes // 2, boxes // 2 + len(waited)),
    )
    came = swapped(send, "box", 1)
    if boxes == 8:
        (five,) = call(copy_kernel, [(six.shape, F32)], others, pieces[0], hbm=(1,))
        late.append(swapped(five, "box", 2))
    top = ((2 * depth, 2 * depth), BF16)
    local = ((boxes, 6 * rank, 2 * width), BF16)
    prepared = call(prepare_kernel, [top, top, local], *early, *late)
    (out,) = call(
        functools.partial(top_kernel, offsets), [((2, share, boxes * width), F32)], *prepared, *pieces, came,
        extra=[pltpu.VMEM((boxes, share // 2, width), F32)],
    )
    return out


def solution(mesh):
    return jax.shard_map(
        on_device,
        mesh=mesh,
        in_specs=(
            P(None, ("blk", "box")),
            P("batch"),
            P(("blk", "box"), None),
            P(("blk", "box"), None),
            P(("blk", "box"), None, None, None),
            P(("blk", "box"), None, None, None, None),
            P("blk", None, "box", None),
        ),
        out_specs=P(None, ("batch", "box"), "blk"),
        check_vma=False,
    )
```

```python
import functools

import jax
import jax.numpy as jnp
import numpy as np
from jax import lax
from jax.experimental import pallas as pl
from jax.experimental.pallas import tpu as pltpu
from jax.sharding import PartitionSpec as P

SWEEP = 16384
WAVENUMBER = 24.0
F32 = jnp.float32
BF16 = jnp.bfloat16
COST = pl.CostEstimate(flops=10**10, bytes_accessed=10**7, transcendentals=0)
VMEM = pl.BlockSpec(memory_space=pltpu.VMEM)
NN = (((1,), (0,)), ((), ()))
NT = (((1,), (1,)), ((), ()))
TN = (((0,), (0,)), ((), ()))

HALF_PI_1 = float(np.float32(201.0 / 128.0))
HALF_PI_2 = float(np.float32(np.round((np.pi / 2 - HALF_PI_1) * 2.0**22) / 2.0**22))
HALF_PI_3 = float(np.float32(np.pi / 2 - HALF_PI_1 - HALF_PI_2))


def cat(parts, axis):
    return jnp.concatenate(parts, axis=axis)


def dot(a, b, form=NN):
    return lax.dot_general(a, b, form, preferred_element_type=F32)


def split(x):
    high = x.astype(BF16)
    return high, (x - high.astype(F32)).astype(BF16)


def dot3(a, b, form=NN):
    return dot(a[0], b[0], form) + (dot(a[0], b[1], form) + dot(a[1], b[0], form))


def both(pair, function):
    return function(pair[0]), function(pair[1])


def sin_cos_small(r):
    s = r * r
    sin = r + r * s * (-1.6666654611e-1 + s * (8.3321608736e-3 - s * 1.9515295891e-4))
    cos = 1.0 - 0.5 * s + s * s * (4.166664568298827e-2 + s * (-1.388731625493765e-3 + s * 2.443315711809948e-5))
    return sin, cos


def by_quadrant(quadrant, sin, cos):
    odd = (quadrant & 1) == 1
    out_sin = jnp.where(odd, cos, sin)
    out_cos = jnp.where(odd, sin, cos)
    out_sin = jnp.where((quadrant & 2) == 2, -out_sin, out_sin)
    out_cos = jnp.where(((quadrant + 1) & 2) == 2, -out_cos, out_cos)
    return out_sin, out_cos


def one_hot(skeleton, width):
    rows = lax.broadcasted_iota(jnp.int32, (width, skeleton.shape[1]), 0)
    return jnp.where(rows == skeleton, 1.0, 0.0).astype(BF16)


def rows_form(re, im):
    return cat([cat([re, -im], 1), cat([im, re], 1)], 0)


def columns_form(re, im):
    return cat([cat([re, im], 1), cat([-im, re], 1)], 0)


def field_kernel(points_in, angles_in, skeleton_in, top_in, mask_in, inverse_in, coupling_in,
                 u_out, static_out, high_out, low_out, picker_out, mask_out, inverse, coupling,
                 points, angles, skeleton, top, mask, sems, more_sems):
    copies = [
        pltpu.make_async_copy(source, target, sems.at[k])
        for k, (source, target) in enumerate((
            (angles_in, angles), (points_in, points), (skeleton_in, skeleton), (top_in, top), (mask_in, mask),
        ))
    ]
    copies.append(pltpu.make_async_copy(inverse_in, inverse, more_sems.at[0]))
    copies.append(pltpu.make_async_copy(coupling_in, coupling, more_sems.at[1]))
    for copy in copies:
        copy.start()
    count = angles.shape[1]
    width = points.shape[1]
    rank = skeleton.shape[1]
    copies[0].wait()
    ids = angles[...]
    quadrant = (ids + SWEEP // 8) >> (SWEEP.bit_length() - 3)
    rest = ids - quadrant * (SWEEP // 4)
    sin, cos = by_quadrant(quadrant, *sin_cos_small(rest.astype(F32) * (2.0 * np.pi / SWEEP)))
    pick = lax.broadcasted_iota(jnp.int32, (8, count), 0) == 0
    columns = jnp.where(pick, cos, sin).T
    cos_column = columns[:, 0:1]
    sin_column = columns[:, 1:2]
    copies[1].wait()
    x = points[0:1, :] * WAVENUMBER
    yz = points[1:2, :] * (0.6 * WAVENUMBER) + points[2:3, :] * (0.8 * WAVENUMBER)
    phase = x * cos_column + yz * sin_column
    turns = jnp.round(phase * (2.0 / np.pi))
    r = ((phase - turns * HALF_PI_1) - turns * HALF_PI_2) - turns * HALF_PI_3
    field_sin, field_cos = by_quadrant(turns.astype(jnp.int32), *sin_cos_small(r))
    field = split(cat([field_cos, field_sin], 1))
    high_out[...] = field[0]
    low_out[...] = field[1]
    copies[2].wait()
    picker = one_hot(skeleton[...], width)
    picker_out[...] = picker
    copies[4].wait()
    mask_out[...] = mask[...].astype(F32)
    copies[5].wait()
    parts = split(cat([inverse[0, 0], inverse[0, 1]], 1))
    rows = dot(picker, cat(parts, 1), TN)
    rows_high = rows[:, : 2 * width]
    rows_low = rows[:, 2 * width :]
    whole = rows_high + rows_low
    form = both((rows_high, rows_low), lambda v: rows_form(v[:, :width], v[:, width:]).astype(BF16))
    u_out[...] = dot3(form, field, NT)
    depth = top.shape[3]
    copies[3].wait()
    for part in range(2):
        at = slice(part * rank, (part + 1) * rank)
        static_out[at, :depth] = top[0, part]
        static_out[at, depth:] = whole[:, part * width : (part + 1) * width]
    copies[6].wait()


def coupling_kernel(high, low, picker_in, mask, inverse, coupling, base_out, high_out, low_out):
    width = inverse.shape[2]
    sides = coupling.shape[1]
    rank = coupling.shape[3]
    depth = sides * rank
    field = (high[...], low[...])
    re = split(inverse[0, 0])
    im = split(inverse[0, 1])
    row_matrix = (rows_form(re[0], im[0]), rows_form(re[1], im[1]))
    column_matrix = (columns_form(re[0], im[0]), columns_form(re[1], im[1]))
    picker = picker_in[...]
    zero = jnp.zeros_like(picker)
    picker2 = cat([cat([picker, zero], 1), cat([zero, picker], 1)], 0)
    z = split(dot3(field, row_matrix, NT))
    u = dot(z[0], picker2) + dot(z[1], picker2)
    near = []
    for side in range(sides):
        weight = mask[:, side : side + 1]
        near.append(cat([coupling[0, side, 0] * weight, coupling[0, side, 1] * weight], 1))
    near = split(cat(near, 0))
    base_out[:, : 2 * width] = dot3(z, column_matrix)
    base_out[:, 2 * width :] = u
    applied = split(dot3(near, column_matrix))
    for k, out in enumerate((high_out, low_out)):
        chosen = dot(near[k], picker2).astype(BF16)
        for matrix, at, part in ((applied[k], 0, width), (chosen, 2 * width, rank)):
            out[:depth, at : at + 2 * part] = matrix
            out[depth:, at : at + part] = -matrix[:, part:]
            out[depth:, at + part : at + 2 * part] = matrix[:, :part]


def hold_kernel(static, out):
    out[...] = static[...]


def pack_kernel(four, two, one, base, four_out, pair_out):
    four_out[...] = four[...]
    pair_out[0] = two[...]
    pair_out[1] = four[...]


def copy_kernel(value, *refs):
    out = refs[-1]
    out[...] = value[1]


def join_kernel(even, odd, u, row_out):
    first = lax.axis_index("box") % 2 == 0
    row_out[0] = jnp.where(first, odd[...], even[...])
    row_out[1] = u[...]
    row_out[2] = jnp.where(first, even[...], odd[...])


def message_kernel(odd, middle, even, base, high, low, *refs):
    outs, natural = refs[:-1], refs[-1]
    first = lax.axis_index("blk") % 2 == 0
    up = jnp.where(first, odd[...], even[...])
    down = jnp.where(first, even[...], odd[...])
    boxes, _, width = natural.shape
    count = base.shape[0]
    rank = up.shape[1] // 2
    share = count // boxes
    half = share // 2
    order = (up[0], up[1], up[2], middle[0], middle[2], down[0], down[1], down[2])
    stacked = cat([v[:rank] for v in order] + [v[rank:] for v in order], 0)
    near = split(stacked.T)
    w = base[...] - dot3(near, (high[...], low[...]))
    for box in range(boxes):
        rows = w[box * share : (box + 1) * share]
        natural[box, :share] = rows[:, :width]
        natural[box, share : 2 * share] = rows[:, width : 2 * width]
        t = rows[:, 2 * width :]
        natural[box, 2 * share : 2 * share + half] = cat([t[:half], t[half:]], 1)
    me = lax.axis_index("box")
    for k in range(boxes):
        outs[k // 2][k % 2] = natural[me ^ k]


def forward_kernel(count, *refs):
    out = refs[-1]
    for k in range(count):
        out[k] = refs[k][1]


def blocks_of(refs):
    return [block for v in refs for block in ([v[k] for k in range(v.shape[0])] if len(v.shape) == 3 else [v[...]])]


def stacked_form(block, rank, depth):
    high, low = both(block, lambda part: columns_form(part[:rank, depth:], part[rank:, depth:]))
    return cat([high, high, low], 0)


def prepare_kernel(*refs):
    top_high, top_low, local_out = refs[-3:]
    depth = top_high.shape[1] // 2
    rank = local_out.shape[1] // 6
    for k, block in enumerate(blocks_of(refs[:-3])):
        at = slice(2 * k * rank, 2 * (k + 1) * rank)
        parts = split(block)
        for part, top_out in zip(parts, (top_high, top_low)):
            top_out[at] = rows_form(part[:rank, :depth], part[rank:, :depth])
        local_out[k] = stacked_form(parts, rank, depth)


def top_kernel(offsets, top_high, top_low, local, *refs):
    pieces = refs[:-3][::-1]
    came, out, packed = refs[-3:]
    boxes = 2 * len(pieces)
    width = came.shape[2]
    share = out.shape[1]
    half = share // 2
    rank = local.shape[1] // 6
    rows = 2 * rank
    me = lax.axis_index("box")
    for k in range(boxes):
        packed[me ^ k] = came[k // 2, 2 * share : 2 * share + half] if k % 2 else pieces[k // 2][0, 2 * share : 2 * share + half]
    t_re = []
    t_im = []
    for box in range(boxes):
        t = cat([packed[box, :, :rows], packed[box, :, rows:]], 0)
        t_re.append(t[:, :rank])
        t_im.append(t[:, rank:])
    t = split(cat(t_re + t_im, 1))
    first = dot(cat(t, 0), top_high[...], NT)
    y = split(first[:share] + (first[share:] + dot(t[0], top_low[...], NT)))
    for k in range(boxes):
        at = slice(k * rows, (k + 1) * rows)
        x = dot(cat([y[0][:, at], y[1][:, at], y[0][:, at]], 1), local[k])
        offset = offsets[k]
        piece, side = (came, offset // 2) if offset % 2 else (pieces[offset // 2], 0)
        at = pl.ds(pl.multiple_of((me ^ offset) * width, width), width)
        out[0, :, at] = piece[side, :share] + x[:, :width]
        out[1, :, at] = piece[side, share : 2 * share] + x[:, width:]


def call(kernel, outs, *arrays, hbm=(), copied=(), held=(), extra=(), cost=None):
    spaces = {i: pl.BlockSpec(memory_space=pl.ANY) for i in hbm}
    spaces.update({i: pl.BlockSpec(memory_space=pltpu.HBM) for i in (*copied, *held)})
    scratch = [pltpu.VMEM(arrays[i].shape, arrays[i].dtype) for i in copied]
    if scratch:
        scratch.append(pltpu.SemaphoreType.DMA((len(scratch),)))
    scratch += extra
    arrays = [pltpu.with_memory_space_constraint(v, pltpu.HBM) if i in (*copied, *held) else v for i, v in enumerate(arrays)]
    return pl.pallas_call(
        kernel,
        out_shape=[jax.ShapeDtypeStruct(shape, dtype) for shape, dtype in outs],
        in_specs=[spaces.get(i, VMEM) for i in range(len(arrays))],
        out_specs=[VMEM] * len(outs),
        scratch_shapes=scratch,
        cost_estimate=cost,
        compiler_params=pltpu.CompilerParams(vmem_limit_bytes=40 * 1024 * 1024),
    )(*arrays)


def swapped(value, axis, bit):
    return lax.ppermute(value, axis, [(i, i ^ bit) for i in range(lax.axis_size(axis))])


def beside(value, axis):
    count = lax.axis_size(axis)
    even = lax.ppermute(value, axis, [(i, i ^ 1) for i in range(count)])
    odd = lax.ppermute(value, axis, [(i, (i + 1) % count if i % 2 else (i - 1) % count) for i in range(count)])
    return even, odd


def on_device(surface_points, angle_ids, near_mask, skeleton, box_inverse_parts, near_coupling, top_inverse):
    boxes = lax.axis_size("box")
    width = box_inverse_parts.shape[2]
    count = angle_ids.shape[0]
    rank = skeleton.shape[1]
    sides = near_mask.shape[1]
    depth = top_inverse.shape[3]
    share = count // boxes
    u, static, high, low, picker, mask, inverse, coupling = call(
        field_kernel,
        [
            ((2 * rank, count), F32),
            ((2 * rank, depth + width), F32),
            ((count, 2 * width), BF16),
            ((count, 2 * width), BF16),
            ((width, rank), BF16),
            (near_mask.shape, F32),
            (box_inverse_parts.shape, F32),
            (near_coupling.shape, F32),
        ],
        surface_points, angle_ids.reshape(1, count), skeleton, top_inverse, near_mask,
        box_inverse_parts, near_coupling, copied=range(5), held=(5, 6), extra=[pltpu.SemaphoreType.DMA((2,))],
    )
    base, matrix_high, matrix_low = call(
        coupling_kernel,
        [
            ((count, 2 * width + 2 * rank), F32),
            ((2 * sides * rank, 2 * width + 2 * rank), BF16),
            ((2 * sides * rank, 2 * width + 2 * rank), BF16),
        ],
        high, low, picker, mask, inverse, coupling, cost=COST,
    )
    even, odd = beside(u, "box")
    (row,) = call(join_kernel, [((3,) + u.shape, F32)], even, odd, u)
    (static,) = call(hold_kernel, [(static.shape, F32)], static, cost=COST)
    if boxes == 8:
        four = swapped(static, "box", 4)
        (again,) = call(hold_kernel, [(static.shape, F32)], static, cost=COST)
        two, one = swapped(again, "box", 2), swapped(again, "box", 1)
        four, pair = call(
            pack_kernel, [(static.shape, F32), ((2,) + static.shape, F32)], four, two, one, base, hbm=(2, 3)
        )
        six, others = swapped(four, "box", 2), swapped(pair, "box", 1)
        early, late, waited = [static, four, two, one, others, six], [], [others]
        offsets = (0, 4, 2, 1, 3, 5, 6, 7)
    else:
        early, late, waited = [static[None]], [], []
        offsets = [0]
        step = boxes // 2
        while step > 0:
            early.append(swapped(jnp.concatenate(early), "box", step))
            offsets += [k ^ step for k in offsets]
            step //= 2
    even, odd = beside(row, "blk")
    length = 2 * share + -(-share // 16) * 8
    pieces = call(
        message_kernel, [((2, length, width), F32)] * (boxes // 2),
        odd, row, even, base, matrix_high, matrix_low,
        cost=COST, extra=[pltpu.VMEM((boxes, length, width), F32)],
    )
    pieces = [swapped(pieces[k], "box", 2 * k) for k in reversed(range(1, boxes // 2))] + [pieces[0]]
    (send,) = call(
        functools.partial(forward_kernel, boxes // 2), [((boxes // 2, length, width), F32)],
        *pieces[::-1], *waited, hbm=range(boxes // 2, boxes // 2 + len(waited)),
    )
    came = swapped(send, "box", 1)
    if boxes == 8:
        (five,) = call(copy_kernel, [(six.shape, F32)], others, pieces[0], hbm=(1,))
        late.append(swapped(five, "box", 2))
    top = ((2 * depth, 2 * depth), BF16)
    local = ((boxes, 6 * rank, 2 * width), BF16)
    prepared = call(prepare_kernel, [top, top, local], *early, *late)
    (out,) = call(
        functools.partial(top_kernel, offsets), [((2, share, boxes * width), F32)], *prepared, *pieces, came,
        extra=[pltpu.VMEM((boxes, share // 2, width), F32)],
    )
    return out


def solution(mesh):
    return jax.shard_map(
        on_device,
        mesh=mesh,
        in_specs=(
            P(None, ("blk", "box")),
            P("batch"),
            P(("blk", "box"), None),
            P(("blk", "box"), None),
            P(("blk", "box"), None, None, None),
            P(("blk", "box"), None, None, None, None),
            P("blk", None, "box", None),
        ),
        out_specs=P(None, ("batch", "box"), "blk"),
        check_vma=False,
    )
```

```python
import functools

import jax
import jax.numpy as jnp
import numpy as np
from jax import lax
from jax.experimental import pallas as pl
from jax.experimental.pallas import tpu as pltpu
from jax.sharding import PartitionSpec as P

SWEEP = 16384
WAVENUMBER = 24.0
F32 = jnp.float32
BF16 = jnp.bfloat16
COST = pl.CostEstimate(flops=10**10, bytes_accessed=10**7, transcendentals=0)
VMEM = pl.BlockSpec(memory_space=pltpu.VMEM)
NN = (((1,), (0,)), ((), ()))
NT = (((1,), (1,)), ((), ()))
TN = (((0,), (0,)), ((), ()))

HALF_PI_1 = float(np.float32(201.0 / 128.0))
HALF_PI_2 = float(np.float32(np.round((np.pi / 2 - HALF_PI_1) * 2.0**22) / 2.0**22))
HALF_PI_3 = float(np.float32(np.pi / 2 - HALF_PI_1 - HALF_PI_2))


def cat(parts, axis):
    return jnp.concatenate(parts, axis=axis)


def dot(a, b, form=NN):
    return lax.dot_general(a, b, form, preferred_element_type=F32)


def split(x):
    high = x.astype(BF16)
    return high, (x - high.astype(F32)).astype(BF16)


def dot3(a, b, form=NN):
    return dot(a[0], b[0], form) + (dot(a[0], b[1], form) + dot(a[1], b[0], form))


def both(pair, function):
    return function(pair[0]), function(pair[1])


def sin_cos_small(r):
    s = r * r
    sin = r + r * s * (-1.6666654611e-1 + s * (8.3321608736e-3 - s * 1.9515295891e-4))
    cos = 1.0 - 0.5 * s + s * s * (4.166664568298827e-2 + s * (-1.388731625493765e-3 + s * 2.443315711809948e-5))
    return sin, cos


def by_quadrant(quadrant, sin, cos):
    odd = (quadrant & 1) == 1
    out_sin = jnp.where(odd, cos, sin)
    out_cos = jnp.where(odd, sin, cos)
    out_sin = jnp.where((quadrant & 2) == 2, -out_sin, out_sin)
    out_cos = jnp.where(((quadrant + 1) & 2) == 2, -out_cos, out_cos)
    return out_sin, out_cos


def one_hot(skeleton, width):
    rows = lax.broadcasted_iota(jnp.int32, (width, skeleton.shape[1]), 0)
    return jnp.where(rows == skeleton, 1.0, 0.0).astype(BF16)


def rows_form(re, im):
    return cat([cat([re, -im], 1), cat([im, re], 1)], 0)


def columns_form(re, im):
    return cat([cat([re, im], 1), cat([-im, re], 1)], 0)


def field_kernel(points_in, angles_in, skeleton_in, top_in, mask_in, inverse_in, coupling_in,
                 u_out, static_out, high_out, low_out, picker_out, mask_out, inverse, coupling,
                 points, angles, skeleton, top, mask, sems, more_sems):
    copies = [
        pltpu.make_async_copy(source, target, sems.at[k])
        for k, (source, target) in enumerate((
            (angles_in, angles), (points_in, points), (skeleton_in, skeleton), (top_in, top), (mask_in, mask),
        ))
    ]
    copies.append(pltpu.make_async_copy(inverse_in, inverse, more_sems.at[0]))
    copies.append(pltpu.make_async_copy(coupling_in, coupling, more_sems.at[1]))
    for copy in copies:
        copy.start()
    count = angles.shape[1]
    width = points.shape[1]
    rank = skeleton.shape[1]
    copies[0].wait()
    ids = angles[...]
    quadrant = (ids + SWEEP // 8) >> (SWEEP.bit_length() - 3)
    rest = ids - quadrant * (SWEEP // 4)
    sin, cos = by_quadrant(quadrant, *sin_cos_small(rest.astype(F32) * (2.0 * np.pi / SWEEP)))
    pick = lax.broadcasted_iota(jnp.int32, (8, count), 0) == 0
    columns = jnp.where(pick, cos, sin).T
    cos_column = columns[:, 0:1]
    sin_column = columns[:, 1:2]
    copies[1].wait()
    x = points[0:1, :] * WAVENUMBER
    yz = points[1:2, :] * (0.6 * WAVENUMBER) + points[2:3, :] * (0.8 * WAVENUMBER)
    phase = x * cos_column + yz * sin_column
    turns = jnp.round(phase * (2.0 / np.pi))
    r = ((phase - turns * HALF_PI_1) - turns * HALF_PI_2) - turns * HALF_PI_3
    field_sin, field_cos = by_quadrant(turns.astype(jnp.int32), *sin_cos_small(r))
    field = split(cat([field_cos, field_sin], 1))
    high_out[...] = field[0]
    low_out[...] = field[1]
    copies[2].wait()
    picker = one_hot(skeleton[...], width)
    picker_out[...] = picker
    copies[4].wait()
    mask_out[...] = mask[...].astype(F32)
    copies[5].wait()
    parts = split(cat([inverse[0, 0], inverse[0, 1]], 1))
    rows = dot(picker, cat(parts, 1), TN)
    rows_high = rows[:, : 2 * width]
    rows_low = rows[:, 2 * width :]
    whole = rows_high + rows_low
    form = both((rows_high, rows_low), lambda v: rows_form(v[:, :width], v[:, width:]).astype(BF16))
    u_out[...] = dot3(form, field, NT)
    depth = top.shape[3]
    copies[3].wait()
    for part in range(2):
        at = slice(part * rank, (part + 1) * rank)
        static_out[at, :depth] = top[0, part]
        static_out[at, depth:] = whole[:, part * width : (part + 1) * width]
    copies[6].wait()


def coupling_kernel(high, low, picker_in, mask, inverse, coupling, base_out, high_out, low_out):
    width = inverse.shape[2]
    sides = coupling.shape[1]
    rank = coupling.shape[3]
    depth = sides * rank
    field = (high[...], low[...])
    re = split(inverse[0, 0])
    im = split(inverse[0, 1])
    row_matrix = (rows_form(re[0], im[0]), rows_form(re[1], im[1]))
    column_matrix = (columns_form(re[0], im[0]), columns_form(re[1], im[1]))
    picker = picker_in[...]
    zero = jnp.zeros_like(picker)
    picker2 = cat([cat([picker, zero], 1), cat([zero, picker], 1)], 0)
    z = split(dot3(field, row_matrix, NT))
    u = dot(z[0], picker2) + dot(z[1], picker2)
    near = []
    for side in range(sides):
        weight = mask[:, side : side + 1]
        near.append(cat([coupling[0, side, 0] * weight, coupling[0, side, 1] * weight], 1))
    near = split(cat(near, 0))
    base_out[:, : 2 * width] = dot3(z, column_matrix)
    base_out[:, 2 * width :] = u
    applied = split(dot3(near, column_matrix))
    for k, out in enumerate((high_out, low_out)):
        chosen = dot(near[k], picker2).astype(BF16)
        for matrix, at, part in ((applied[k], 0, width), (chosen, 2 * width, rank)):
            out[:depth, at : at + 2 * part] = matrix
            out[depth:, at : at + part] = -matrix[:, part:]
            out[depth:, at + part : at + 2 * part] = matrix[:, :part]


def hold_kernel(static, out):
    out[...] = static[...]


def pack_kernel(four, two, one, base, four_out, pair_out):
    four_out[...] = four[...]
    pair_out[0] = two[...]
    pair_out[1] = four[...]


def copy_kernel(value, *refs):
    out = refs[-1]
    out[...] = value[1]


def join_kernel(even, odd, u, row_out):
    first = lax.axis_index("box") % 2 == 0
    row_out[0] = jnp.where(first, odd[...], even[...])
    row_out[1] = u[...]
    row_out[2] = jnp.where(first, even[...], odd[...])


def message_kernel(even, middle, odd, base, high, low, *refs):
    outs, natural = refs[:-1], refs[-1]
    first = lax.axis_index("blk") % 2 == 0
    up = jnp.where(first, odd[...], even[...])
    down = jnp.where(first, even[...], odd[...])
    boxes, _, width = natural.shape
    count = base.shape[0]
    rank = up.shape[1] // 2
    share = count // boxes
    half = share // 2
    order = (up[0], up[1], up[2], middle[0], middle[2], down[0], down[1], down[2])
    stacked = cat([v[:rank] for v in order] + [v[rank:] for v in order], 0)
    near = split(stacked.T)
    w = base[...] - dot3(near, (high[...], low[...]))
    for box in range(boxes):
        rows = w[box * share : (box + 1) * share]
        natural[box, :share] = rows[:, :width]
        natural[box, share : 2 * share] = rows[:, width : 2 * width]
        t = rows[:, 2 * width :]
        natural[box, 2 * share : 2 * share + half] = cat([t[:half], t[half:]], 1)
    me = lax.axis_index("box")
    for k in range(boxes):
        outs[k // 2][k % 2] = natural[me ^ k]


def forward_kernel(count, *refs):
    out = refs[-1]
    for k in range(count):
        out[k] = refs[k][1]


def blocks_of(refs):
    return [block for v in refs for block in ([v[k] for k in range(v.shape[0])] if len(v.shape) == 3 else [v[...]])]


def stacked_form(block, rank, depth):
    high, low = both(block, lambda part: columns_form(part[:rank, depth:], part[rank:, depth:]))
    return cat([high, high, low], 0)


def prepare_kernel(*refs):
    top_high, top_low, local_out = refs[-3:]
    depth = top_high.shape[1] // 2
    rank = local_out.shape[1] // 6
    for k, block in enumerate(blocks_of(refs[:-3])):
        at = slice(2 * k * rank, 2 * (k + 1) * rank)
        parts = split(block)
        for part, top_out in zip(parts, (top_high, top_low)):
            top_out[at] = rows_form(part[:rank, :depth], part[rank:, :depth])
        local_out[k] = stacked_form(parts, rank, depth)


def top_kernel(offsets, top_high, top_low, local, *refs):
    pieces = refs[:-3][::-1]
    came, out, packed = refs[-3:]
    boxes = 2 * len(pieces)
    width = came.shape[2]
    share = out.shape[1]
    half = share // 2
    rank = local.shape[1] // 6
    rows = 2 * rank
    me = lax.axis_index("box")
    for k in range(boxes):
        packed[me ^ k] = came[k // 2, 2 * share : 2 * share + half] if k % 2 else pieces[k // 2][0, 2 * share : 2 * share + half]
    t_re = []
    t_im = []
    for box in range(boxes):
        t = cat([packed[box, :, :rows], packed[box, :, rows:]], 0)
        t_re.append(t[:, :rank])
        t_im.append(t[:, rank:])
    t = split(cat(t_re + t_im, 1))
    first = dot(cat(t, 0), top_high[...], NT)
    y = split(first[:share] + (first[share:] + dot(t[0], top_low[...], NT)))
    for k in range(boxes):
        at = slice(k * rows, (k + 1) * rows)
        x = dot(cat([y[0][:, at], y[1][:, at], y[0][:, at]], 1), local[k])
        offset = offsets[k]
        piece, side = (came, offset // 2) if offset % 2 else (pieces[offset // 2], 0)
        at = pl.ds(pl.multiple_of((me ^ offset) * width, width), width)
        out[0, :, at] = piece[side, :share] + x[:, :width]
        out[1, :, at] = piece[side, share : 2 * share] + x[:, width:]


def call(kernel, outs, *arrays, hbm=(), copied=(), held=(), extra=(), cost=None):
    spaces = {i: pl.BlockSpec(memory_space=pl.ANY) for i in hbm}
    spaces.update({i: pl.BlockSpec(memory_space=pltpu.HBM) for i in (*copied, *held)})
    scratch = [pltpu.VMEM(arrays[i].shape, arrays[i].dtype) for i in copied]
    if scratch:
        scratch.append(pltpu.SemaphoreType.DMA((len(scratch),)))
    scratch += extra
    arrays = [pltpu.with_memory_space_constraint(v, pltpu.HBM) if i in (*copied, *held) else v for i, v in enumerate(arrays)]
    return pl.pallas_call(
        kernel,
        out_shape=[jax.ShapeDtypeStruct(shape, dtype) for shape, dtype in outs],
        in_specs=[spaces.get(i, VMEM) for i in range(len(arrays))],
        out_specs=[VMEM] * len(outs),
        scratch_shapes=scratch,
        cost_estimate=cost,
        compiler_params=pltpu.CompilerParams(vmem_limit_bytes=40 * 1024 * 1024),
    )(*arrays)


def swapped(value, axis, bit):
    return lax.ppermute(value, axis, [(i, i ^ bit) for i in range(lax.axis_size(axis))])


def beside(value, axis):
    count = lax.axis_size(axis)
    even = lax.ppermute(value, axis, [(i, i ^ 1) for i in range(count)])
    odd = lax.ppermute(value, axis, [(i, (i + 1) % count if i % 2 else (i - 1) % count) for i in range(count)])
    return even, odd


def on_device(surface_points, angle_ids, near_mask, skeleton, box_inverse_parts, near_coupling, top_inverse):
    boxes = lax.axis_size("box")
    width = box_inverse_parts.shape[2]
    count = angle_ids.shape[0]
    rank = skeleton.shape[1]
    sides = near_mask.shape[1]
    depth = top_inverse.shape[3]
    share = count // boxes
    u, static, high, low, picker, mask, inverse, coupling = call(
        field_kernel,
        [
            ((2 * rank, count), F32),
            ((2 * rank, depth + width), F32),
            ((count, 2 * width), BF16),
            ((count, 2 * width), BF16),
            ((width, rank), BF16),
            (near_mask.shape, F32),
            (box_inverse_parts.shape, F32),
            (near_coupling.shape, F32),
        ],
        surface_points, angle_ids.reshape(1, count), skeleton, top_inverse, near_mask,
        box_inverse_parts, near_coupling, copied=range(5), held=(5, 6), extra=[pltpu.SemaphoreType.DMA((2,))],
    )
    base, matrix_high, matrix_low = call(
        coupling_kernel,
        [
            ((count, 2 * width + 2 * rank), F32),
            ((2 * sides * rank, 2 * width + 2 * rank), BF16),
            ((2 * sides * rank, 2 * width + 2 * rank), BF16),
        ],
        high, low, picker, mask, inverse, coupling, cost=COST,
    )
    even, odd = beside(u, "box")
    (row,) = call(join_kernel, [((3,) + u.shape, F32)], even, odd, u)
    (static,) = call(hold_kernel, [(static.shape, F32)], static, cost=COST)
    if boxes == 8:
        four = swapped(static, "box", 4)
        (again,) = call(hold_kernel, [(static.shape, F32)], static, cost=COST)
        two, one = swapped(again, "box", 2), swapped(again, "box", 1)
        four, pair = call(
            pack_kernel, [(static.shape, F32), ((2,) + static.shape, F32)], four, two, one, base, hbm=(2, 3)
        )
        six, others = swapped(four, "box", 2), swapped(pair, "box", 1)
        early, late, waited = [static, four, two, one, others, six], [], [others, six]
        offsets = (0, 4, 2, 1, 3, 5, 6, 7)
    else:
        early, late, waited = [static[None]], [], []
        offsets = [0]
        step = boxes // 2
        while step > 0:
            early.append(swapped(jnp.concatenate(early), "box", step))
            offsets += [k ^ step for k in offsets]
            step //= 2
    even, odd = beside(row, "blk")
    length = 2 * share + -(-share // 16) * 8
    pieces = call(
        message_kernel, [((2, length, width), F32)] * (boxes // 2),
        even, row, odd, base, matrix_high, matrix_low,
        cost=COST, extra=[pltpu.VMEM((boxes, length, width), F32)],
    )
    pieces = [swapped(pieces[k], "box", 2 * k) for k in reversed(range(1, boxes // 2))] + [pieces[0]]
    (send,) = call(
        functools.partial(forward_kernel, boxes // 2), [((boxes // 2, length, width), F32)],
        *pieces[::-1], *waited, hbm=range(boxes // 2, boxes // 2 + len(waited)),
    )
    came = swapped(send, "box", 1)
    if boxes == 8:
        (five,) = call(copy_kernel, [(six.shape, F32)], others, pieces[0], hbm=(1,))
        late.append(swapped(five, "box", 2))
    top = ((2 * depth, 2 * depth), BF16)
    local = ((boxes, 6 * rank, 2 * width), BF16)
    prepared = call(prepare_kernel, [top, top, local], *early, *late)
    (out,) = call(
        functools.partial(top_kernel, offsets), [((2, share, boxes * width), F32)], *prepared, *pieces, came,
        extra=[pltpu.VMEM((boxes, share // 2, width), F32)],
    )
    return out


def solution(mesh):
    return jax.shard_map(
        on_device,
        mesh=mesh,
        in_specs=(
            P(None, ("blk", "box")),
            P("batch"),
            P(("blk", "box"), None),
            P(("blk", "box"), None),
            P(("blk", "box"), None, None, None),
            P(("blk", "box"), None, None, None, None),
            P("blk", None, "box", None),
        ),
        out_specs=P(None, ("batch", "box"), "blk"),
        check_vma=False,
    )
```

```python
import functools

import jax
import jax.numpy as jnp
import numpy as np
from jax import lax
from jax.experimental import pallas as pl
from jax.experimental.pallas import tpu as pltpu
from jax.sharding import PartitionSpec as P

SWEEP = 16384
WAVENUMBER = 24.0
F32 = jnp.float32
BF16 = jnp.bfloat16
COST = pl.CostEstimate(flops=10**10, bytes_accessed=10**7, transcendentals=0)
VMEM = pl.BlockSpec(memory_space=pltpu.VMEM)
NN = (((1,), (0,)), ((), ()))
NT = (((1,), (1,)), ((), ()))
TN = (((0,), (0,)), ((), ()))

HALF_PI_1 = float(np.float32(201.0 / 128.0))
HALF_PI_2 = float(np.float32(np.round((np.pi / 2 - HALF_PI_1) * 2.0**22) / 2.0**22))
HALF_PI_3 = float(np.float32(np.pi / 2 - HALF_PI_1 - HALF_PI_2))


def cat(parts, axis):
    return jnp.concatenate(parts, axis=axis)


def dot(a, b, form=NN):
    return lax.dot_general(a, b, form, preferred_element_type=F32)


def split(x):
    high = x.astype(BF16)
    return high, (x - high.astype(F32)).astype(BF16)


def dot3(a, b, form=NN):
    return dot(a[0], b[0], form) + (dot(a[0], b[1], form) + dot(a[1], b[0], form))


def both(pair, function):
    return function(pair[0]), function(pair[1])


def sin_cos_small(r):
    s = r * r
    sin = r + r * s * (-1.6666654611e-1 + s * (8.3321608736e-3 - s * 1.9515295891e-4))
    cos = 1.0 - 0.5 * s + s * s * (4.166664568298827e-2 + s * (-1.388731625493765e-3 + s * 2.443315711809948e-5))
    return sin, cos


def by_quadrant(quadrant, sin, cos):
    odd = (quadrant & 1) == 1
    out_sin = jnp.where(odd, cos, sin)
    out_cos = jnp.where(odd, sin, cos)
    out_sin = jnp.where((quadrant & 2) == 2, -out_sin, out_sin)
    out_cos = jnp.where(((quadrant + 1) & 2) == 2, -out_cos, out_cos)
    return out_sin, out_cos


def one_hot(skeleton, width):
    rows = lax.broadcasted_iota(jnp.int32, (width, skeleton.shape[1]), 0)
    return jnp.where(rows == skeleton, 1.0, 0.0).astype(BF16)


def rows_form(re, im):
    return cat([cat([re, -im], 1), cat([im, re], 1)], 0)


def columns_form(re, im):
    return cat([cat([re, im], 1), cat([-im, re], 1)], 0)


def field_kernel(points_in, angles_in, skeleton_in, top_in, mask_in, inverse_in, coupling_in,
                 u_out, static_out, high_out, low_out, picker_out, mask_out, inverse, coupling,
                 points, angles, skeleton, top, mask, sems, more_sems):
    copies = [
        pltpu.make_async_copy(source, target, sems.at[k])
        for k, (source, target) in enumerate((
            (angles_in, angles), (points_in, points), (skeleton_in, skeleton), (top_in, top), (mask_in, mask),
        ))
    ]
    copies.append(pltpu.make_async_copy(inverse_in, inverse, more_sems.at[0]))
    copies.append(pltpu.make_async_copy(coupling_in, coupling, more_sems.at[1]))
    for copy in copies:
        copy.start()
    count = angles.shape[1]
    width = points.shape[1]
    rank = skeleton.shape[1]
    copies[0].wait()
    ids = angles[...]
    quadrant = (ids + SWEEP // 8) >> (SWEEP.bit_length() - 3)
    rest = ids - quadrant * (SWEEP // 4)
    sin, cos = by_quadrant(quadrant, *sin_cos_small(rest.astype(F32) * (2.0 * np.pi / SWEEP)))
    pick = lax.broadcasted_iota(jnp.int32, (8, count), 0) == 0
    columns = jnp.where(pick, cos, sin).T
    cos_column = columns[:, 0:1]
    sin_column = columns[:, 1:2]
    copies[1].wait()
    x = points[0:1, :] * WAVENUMBER
    yz = points[1:2, :] * (0.6 * WAVENUMBER) + points[2:3, :] * (0.8 * WAVENUMBER)
    phase = x * cos_column + yz * sin_column
    turns = jnp.round(phase * (2.0 / np.pi))
    r = ((phase - turns * HALF_PI_1) - turns * HALF_PI_2) - turns * HALF_PI_3
    field_sin, field_cos = by_quadrant(turns.astype(jnp.int32), *sin_cos_small(r))
    field = split(cat([field_cos, field_sin], 1))
    high_out[...] = field[0]
    low_out[...] = field[1]
    copies[2].wait()
    picker = one_hot(skeleton[...], width)
    picker_out[...] = picker
    copies[4].wait()
    mask_out[...] = mask[...].astype(F32)
    copies[5].wait()
    parts = split(cat([inverse[0, 0], inverse[0, 1]], 1))
    rows = dot(picker, cat(parts, 1), TN)
    rows_high = rows[:, : 2 * width]
    rows_low = rows[:, 2 * width :]
    whole = rows_high + rows_low
    form = both((rows_high, rows_low), lambda v: rows_form(v[:, :width], v[:, width:]).astype(BF16))
    u_out[...] = dot3(form, field, NT)
    depth = top.shape[3]
    copies[3].wait()
    for part in range(2):
        at = slice(part * rank, (part + 1) * rank)
        static_out[at, :depth] = top[0, part]
        static_out[at, depth:] = whole[:, part * width : (part + 1) * width]
    copies[6].wait()


def coupling_kernel(high, low, picker_in, mask, inverse, coupling, base_out, high_out, low_out):
    width = inverse.shape[2]
    sides = coupling.shape[1]
    rank = coupling.shape[3]
    depth = sides * rank
    field = (high[...], low[...])
    re = split(inverse[0, 0])
    im = split(inverse[0, 1])
    row_matrix = (rows_form(re[0], im[0]), rows_form(re[1], im[1]))
    column_matrix = (columns_form(re[0], im[0]), columns_form(re[1], im[1]))
    picker = picker_in[...]
    zero = jnp.zeros_like(picker)
    picker2 = cat([cat([picker, zero], 1), cat([zero, picker], 1)], 0)
    z = split(dot3(field, row_matrix, NT))
    u = dot(z[0], picker2) + dot(z[1], picker2)
    near = []
    for side in range(sides):
        weight = mask[:, side : side + 1]
        near.append(cat([coupling[0, side, 0] * weight, coupling[0, side, 1] * weight], 1))
    near = split(cat(near, 0))
    base_out[:, : 2 * width] = dot3(z, column_matrix)
    base_out[:, 2 * width :] = u
    applied = split(dot3(near, column_matrix))
    for k, out in enumerate((high_out, low_out)):
        chosen = dot(near[k], picker2).astype(BF16)
        for matrix, at, part in ((applied[k], 0, width), (chosen, 2 * width, rank)):
            out[:depth, at : at + 2 * part] = matrix
            out[depth:, at : at + part] = -matrix[:, part:]
            out[depth:, at + part : at + 2 * part] = matrix[:, :part]


def hold_kernel(static, out):
    out[...] = static[...]


def pack_kernel(four, two, one, base, four_out, pair_out):
    four_out[...] = four[...]
    pair_out[0] = two[...]
    pair_out[1] = four[...]


def copy_kernel(value, *refs):
    out = refs[-1]
    out[...] = value[1]


def join_kernel(even, odd, u, row_out):
    first = lax.axis_index("box") % 2 == 0
    row_out[0] = jnp.where(first, odd[...], even[...])
    row_out[1] = u[...]
    row_out[2] = jnp.where(first, even[...], odd[...])


def message_kernel(even, middle, odd, base, high, low, *refs):
    outs, natural = refs[:-1], refs[-1]
    first = lax.axis_index("blk") % 2 == 0
    up = jnp.where(first, odd[...], even[...])
    down = jnp.where(first, even[...], odd[...])
    boxes, _, width = natural.shape
    count = base.shape[0]
    rank = up.shape[1] // 2
    share = count // boxes
    half = share // 2
    order = (up[0], up[1], up[2], middle[0], middle[2], down[0], down[1], down[2])
    stacked = cat([v[:rank] for v in order] + [v[rank:] for v in order], 0)
    near = split(stacked.T)
    w = base[...] - dot3(near, (high[...], low[...]))
    for box in range(boxes):
        rows = w[box * share : (box + 1) * share]
        natural[box, :share] = rows[:, :width]
        natural[box, share : 2 * share] = rows[:, width : 2 * width]
        t = rows[:, 2 * width :]
        natural[box, 2 * share : 2 * share + half] = cat([t[:half], t[half:]], 1)
    me = lax.axis_index("box")
    for k in range(boxes):
        outs[k // 2][k % 2] = natural[me ^ k]


def forward_kernel(count, *refs):
    out = refs[-1]
    for k in range(count):
        out[k] = refs[k][1]


def blocks_of(refs):
    return [block for v in refs for block in ([v[k] for k in range(v.shape[0])] if len(v.shape) == 3 else [v[...]])]


def stacked_form(block, rank, depth):
    high, low = both(block, lambda part: columns_form(part[:rank, depth:], part[rank:, depth:]))
    return cat([high, high, low], 0)


def prepare_kernel(*refs):
    top_high, top_low, local_out = refs[-3:]
    depth = top_high.shape[1] // 2
    rank = local_out.shape[1] // 6
    for k, block in enumerate(blocks_of(refs[:-3])):
        at = slice(2 * k * rank, 2 * (k + 1) * rank)
        parts = split(block)
        for part, top_out in zip(parts, (top_high, top_low)):
            top_out[at] = rows_form(part[:rank, :depth], part[rank:, :depth])
        local_out[k] = stacked_form(parts, rank, depth)


def top_kernel(offsets, top_high, top_low, local, *refs):
    pieces = refs[:-4][::-1]
    first_half, second_half, out, packed = refs[-4:]
    boxes = 2 * len(pieces)
    width = first_half.shape[2]
    ways = [0, *reversed(range(1, boxes // 2))]
    came = {k: (first_half, i) for i, k in enumerate(ways[:1])}
    came.update({k: (second_half, i) for i, k in enumerate(ways[1:])})
    share = out.shape[1]
    half = share // 2
    rank = local.shape[1] // 6
    rows = 2 * rank
    me = lax.axis_index("box")
    blocks = [came[k // 2] if k % 2 else (pieces[k // 2], 0) for k in range(boxes)]
    for k, (piece, side) in enumerate(blocks):
        packed[me ^ k] = piece[side, 2 * share : 2 * share + half]
    t_re = []
    t_im = []
    for box in range(boxes):
        t = cat([packed[box, :, :rows], packed[box, :, rows:]], 0)
        t_re.append(t[:, :rank])
        t_im.append(t[:, rank:])
    t = split(cat(t_re + t_im, 1))
    first = dot(cat(t, 0), top_high[...], NT)
    y = split(first[:share] + (first[share:] + dot(t[0], top_low[...], NT)))
    for k in range(boxes):
        at = slice(k * rows, (k + 1) * rows)
        x = dot(cat([y[0][:, at], y[1][:, at], y[0][:, at]], 1), local[k])
        offset = offsets[k]
        piece, side = blocks[offset]
        at = pl.ds(pl.multiple_of((me ^ offset) * width, width), width)
        out[0, :, at] = piece[side, :share] + x[:, :width]
        out[1, :, at] = piece[side, share : 2 * share] + x[:, width:]


def call(kernel, outs, *arrays, hbm=(), copied=(), held=(), extra=(), cost=None):
    spaces = {i: pl.BlockSpec(memory_space=pl.ANY) for i in hbm}
    spaces.update({i: pl.BlockSpec(memory_space=pltpu.HBM) for i in (*copied, *held)})
    scratch = [pltpu.VMEM(arrays[i].shape, arrays[i].dtype) for i in copied]
    if scratch:
        scratch.append(pltpu.SemaphoreType.DMA((len(scratch),)))
    scratch += extra
    arrays = [pltpu.with_memory_space_constraint(v, pltpu.HBM) if i in (*copied, *held) else v for i, v in enumerate(arrays)]
    return pl.pallas_call(
        kernel,
        out_shape=[jax.ShapeDtypeStruct(shape, dtype) for shape, dtype in outs],
        in_specs=[spaces.get(i, VMEM) for i in range(len(arrays))],
        out_specs=[VMEM] * len(outs),
        scratch_shapes=scratch,
        cost_estimate=cost,
        compiler_params=pltpu.CompilerParams(vmem_limit_bytes=40 * 1024 * 1024),
    )(*arrays)


def swapped(value, axis, bit):
    return lax.ppermute(value, axis, [(i, i ^ bit) for i in range(lax.axis_size(axis))])


def beside(value, axis):
    count = lax.axis_size(axis)
    even = lax.ppermute(value, axis, [(i, i ^ 1) for i in range(count)])
    odd = lax.ppermute(value, axis, [(i, (i + 1) % count if i % 2 else (i - 1) % count) for i in range(count)])
    return even, odd


def on_device(surface_points, angle_ids, near_mask, skeleton, box_inverse_parts, near_coupling, top_inverse):
    boxes = lax.axis_size("box")
    width = box_inverse_parts.shape[2]
    count = angle_ids.shape[0]
    rank = skeleton.shape[1]
    sides = near_mask.shape[1]
    depth = top_inverse.shape[3]
    share = count // boxes
    u, static, high, low, picker, mask, inverse, coupling = call(
        field_kernel,
        [
            ((2 * rank, count), F32),
            ((2 * rank, depth + width), F32),
            ((count, 2 * width), BF16),
            ((count, 2 * width), BF16),
            ((width, rank), BF16),
            (near_mask.shape, F32),
            (box_inverse_parts.shape, F32),
            (near_coupling.shape, F32),
        ],
        surface_points, angle_ids.reshape(1, count), skeleton, top_inverse, near_mask,
        box_inverse_parts, near_coupling, copied=range(5), held=(5, 6), extra=[pltpu.SemaphoreType.DMA((2,))],
    )
    base, matrix_high, matrix_low = call(
        coupling_kernel,
        [
            ((count, 2 * width + 2 * rank), F32),
            ((2 * sides * rank, 2 * width + 2 * rank), BF16),
            ((2 * sides * rank, 2 * width + 2 * rank), BF16),
        ],
        high, low, picker, mask, inverse, coupling, cost=COST,
    )
    even, odd = beside(u, "box")
    (row,) = call(join_kernel, [((3,) + u.shape, F32)], even, odd, u)
    (static,) = call(hold_kernel, [(static.shape, F32)], static, cost=COST)
    if boxes == 8:
        four = swapped(static, "box", 4)
        (again,) = call(hold_kernel, [(static.shape, F32)], static, cost=COST)
        two, one = swapped(again, "box", 2), swapped(again, "box", 1)
        four, pair = call(
            pack_kernel, [(static.shape, F32), ((2,) + static.shape, F32)], four, two, one, base, hbm=(2, 3)
        )
        six, others = swapped(four, "box", 2), swapped(pair, "box", 1)
        early, late, waited = [static, four, two, one, others, six], [], [others]
        offsets = (0, 4, 2, 1, 3, 5, 6, 7)
    else:
        early, late, waited = [static[None]], [], []
        offsets = [0]
        step = boxes // 2
        while step > 0:
            early.append(swapped(jnp.concatenate(early), "box", step))
            offsets += [k ^ step for k in offsets]
            step //= 2
    even, odd = beside(row, "blk")
    length = 2 * share + -(-share // 16) * 8
    pieces = call(
        message_kernel, [((2, length, width), F32)] * (boxes // 2),
        even, row, odd, base, matrix_high, matrix_low,
        cost=COST, extra=[pltpu.VMEM((boxes, length, width), F32)],
    )
    pieces = [swapped(pieces[k], "box", 2 * k) for k in reversed(range(1, boxes // 2))] + [pieces[0]]
    ways = [0, *reversed(range(1, boxes // 2))]
    came = []
    for half in (ways[:1], ways[1:]):
        held = [*waited, *came] if came else []
        (send,) = call(
            functools.partial(forward_kernel, len(half)), [((len(half), length, width), F32)],
            *[pieces[-1 - k] for k in half], *held, hbm=range(len(half), len(half) + len(held)),
        )
        came.append(swapped(send, "box", 1))
    if boxes == 8:
        (five,) = call(copy_kernel, [(six.shape, F32)], others, pieces[0], hbm=(1,))
        late.append(swapped(five, "box", 2))
    top = ((2 * depth, 2 * depth), BF16)
    local = ((boxes, 6 * rank, 2 * width), BF16)
    prepared = call(prepare_kernel, [top, top, local], *early, *late)
    (out,) = call(
        functools.partial(top_kernel, offsets), [((2, share, boxes * width), F32)], *prepared, *pieces, *came,
        extra=[pltpu.VMEM((boxes, share // 2, width), F32)],
    )
    return out


def solution(mesh):
    return jax.shard_map(
        on_device,
        mesh=mesh,
        in_specs=(
            P(None, ("blk", "box")),
            P("batch"),
            P(("blk", "box"), None),
            P(("blk", "box"), None),
            P(("blk", "box"), None, None, None),
            P(("blk", "box"), None, None, None, None),
            P("blk", None, "box", None),
        ),
        out_specs=P(None, ("batch", "box"), "blk"),
        check_vma=False,
    )
```
